32 devices in a mesh: dp: 32 (over z, y, x, core).
Axes of the slice: x: 2, y: 2, z: 4, core: 2. Of those that a mesh axis runs over, the one named last changes fastest.
Arguments:
- clip_tokens: bfloat16 [32, 8, 256, 512], P('dp'), may hold values from -6 to 6
- cotangent: bfloat16 [32, 8, 256, 512], P('dp'), may hold values from -6 to 6
- lengths: int32 [32], P('dp'), may hold values from 1 to 8
- params: float32 [2, 3145728], P(None, 'dp'), may hold values from -0.35355339 to 0.35355339, as said below
- param_moment: float32 [2, 3145728], P(None, 'dp'), may hold values from -80 to 80
- param_second: float32 [2, 3145728], P(None, 'dp'), may hold values from 13.1072 to 52.4288
- norm_par: float32 [4096], P('dp'), may hold values from -1.2 to 1.3, as said below
- norm_moment: float32 [4096], P('dp'), may hold values from -192 to 192
- norm_second: float32 [4096], P('dp'), may hold values from 98.304 to 393.216
Outputs:
- output: float32 [32, 8, 256, 512], P('dp')
- grad_input: float32 [32, 8, 256, 512], P('dp')
- new_params: float32 [2, 3145728], P(None, 'dp')
- new_moment: float32 [2, 3145728], P(None, 'dp')
- new_second: float32 [2, 3145728], P(None, 'dp')
- params_copy: bfloat16 [2, 3145728], P(None, 'dp')
- new_norm: float32 [4096], P('dp')
- new_norm_moment: float32 [4096], P('dp')
- new_norm_second: float32 [4096], P('dp')
The draws below stay inside these ranges and needn't reach their ends.
Inputs may be any that keep to these rules, and one draw needn't show every extreme that they name: Slots 0 to lengths - 1 of a clip are its real steps. `params`: master matrices of both blocks, packed as the steps say. `norm_par`: gains and biases of the four norms, packed as the steps say.
All inputs are finite; a program needn't handle non-finite values.
Results may differ from the reference program's by a relative error of at most 0.02.
The reference program's roundings to bfloat16 on the way count: a program that leaves them out, or rounds other values in their place, can miss the bound.
Values may be sent and summed in bfloat16 or wider, within the bound.
A program may use at most 320 MiB of HBM per device.

```python
import math
from functools import partial
import jax
import jax.numpy as jnp
from jax import lax

D = 512
HEADS = 8
HEAD_DIM = 64
FF = 2048
PATCHES = 256
T_MAX = 8
STEP = 7
CLIPS = 32
BLOCK_PARAMS = 3145728
NORMS = 4096


def draw_params(key, part):
    block_size = 4 * D * D + 2 * D * FF
    normal_draw = jnp.clip(jax.random.normal(key, (2, block_size), jnp.float32), -4.0, 4.0)
    position = jnp.arange(block_size)
    scaling = jnp.where(position < 3 * D * D, 1.4 * D ** (-0.5), jnp.where(position < 4 * D * D, 2.0 * D ** (-0.5), jnp.where(position < 4 * D * D + D * FF, D ** (-0.5), FF ** (-0.5))))
    return normal_draw * scaling[None, :].astype(jnp.float32)


def draw_norm_par(key, part):
    key_gain = jax.random.fold_in(key, 11)
    key_shift = jax.random.fold_in(key, 23)
    position = jnp.arange(8 * D)
    gains = 1.0 + jax.random.uniform(key_gain, (8 * D,), jnp.float32, -0.3, 0.3)
    shifts = 0.3 * jnp.clip(jax.random.normal(key_shift, (8 * D,), jnp.float32), -4.0, 4.0)
    return jnp.where(position // D % 2 == 0, gains, shifts)


def with_ends(array, key, smallest, largest):
    spot = [jax.random.randint(jax.random.fold_in(key, axis), (), 0, length) for axis, length in enumerate(array.shape)]
    widest = array.shape.index(max(array.shape))
    next_to = spot[:widest] + [(spot[widest] + 1) % array.shape[widest]] + spot[widest + 1:]
    return array.at[tuple(spot)].set(smallest).at[tuple(next_to)].set(largest)


def block_scale(stream_key, shape, pieces, smallest, high):
    def one(axis_at, parts):
        draws = jax.random.uniform(jax.random.fold_in(jax.random.fold_in(stream_key, 6), axis_at), (parts,), jnp.float32, smallest / len(pieces), high / len(pieces))
        return jnp.repeat(jnp.exp(draws), shape[axis_at] // parts).reshape((-1,) + (1,) * (len(shape) - axis_at - 1))

    loudness = one(*pieces[0])
    for cut in pieces[1:]:
        loudness = loudness * one(*cut)
    return loudness


def centred(own_key, shape, width, bound, cuts=(), held_as=jnp.bfloat16):
    values = jax.random.normal(own_key, shape, jnp.float32) * width
    if len(cuts) > 0:
        values = block_scale(own_key, shape, cuts, -0.22, 0.18) * values
    return jnp.clip(values, min=-bound, max=bound).astype(held_as)


def setup_inputs(seed: int = 0) -> dict:
    splits = jax.random.split(jax.random.key(seed), 10)
    return {
        "clip_tokens": centred(splits[0], (CLIPS, T_MAX, PATCHES, D), 1.0, 6.0, ((0, 32),)),
        "cotangent": centred(splits[1], (CLIPS, T_MAX, PATCHES, D), 1.0, 6.0, ((0, 32),)),
        "lengths": with_ends(jax.random.randint(splits[2], (CLIPS,), 1, T_MAX + 1), jax.random.fold_in(splits[2], 1), 1, T_MAX).astype(jnp.int32),
        "params": draw_params(jax.random.fold_in(splits[9], 71), 0),
        "param_moment": centred(splits[4], (2, BLOCK_PARAMS), (0.05 * (CLIPS * T_MAX * PATCHES) ** 0.5), 80.0, ((1, 32),), jnp.float32),
        "param_second": jnp.clip(jnp.exp(math.log(52.4288) - 1.3862944 * jax.random.uniform(splits[5], (2, BLOCK_PARAMS), jnp.float32) ** block_scale(splits[5], (2, BLOCK_PARAMS), ((1, 32),), -0.2, 0.2)), 13.1072, 52.4288),
        "norm_par": draw_norm_par(jax.random.fold_in(splits[9], 71), 0),
        "norm_moment": centred(splits[7], (NORMS,), (0.13 * (CLIPS * T_MAX * PATCHES) ** 0.5), 192.0, ((0, 32),), jnp.float32),
        "norm_second": jnp.clip(jnp.exp(math.log(393.216) - 1.3862944 * jax.random.uniform(splits[8], (NORMS,), jnp.float32) ** block_scale(splits[8], (NORMS,), ((0, 32),), -0.2, 0.2)), 98.304, 393.216),
    }


@jax.custom_vjp
def low(v):
    return lax.optimization_barrier(v.astype(jnp.bfloat16)).astype(jnp.float32)

@jax.custom_vjp
def low_back(v):
    return v

def low_keep(v):
    return (low(v), None)

def low_pass(kept, grad):
    return (grad,)

def back_keep(v):
    return (v, None)

def back_low(kept, grad):
    return (low(grad),)
low.defvjp(low_keep, low_pass)
low_back.defvjp(back_keep, back_low)
highest = lax.Precision.HIGHEST
norm_epsilon = 1e-05
beta_first = 0.9
beta_second = 0.999
learn_rate = 0.05
norm_rate = 0.5
weight_decay = 0.1
adam_floor = 1e-08
masked_score = -1e+30

def norm_apply(token_rows, norm_gain, norm_shift):
    center = token_rows - lax.optimization_barrier(jnp.mean(token_rows, axis=-1, keepdims=True))
    spread = lax.optimization_barrier(jnp.mean(center * center, axis=-1, keepdims=True))
    return center * lax.rsqrt(spread + norm_epsilon) * norm_gain + norm_shift

def dense(left_side, right_side):
    return jnp.dot(left_side, right_side, precision=highest, preferred_element_type=jnp.float32)

def unpack(flat_weights, model_width, hidden_width):
    cut_qkv = 3 * model_width * model_width
    cut_out = 4 * model_width * model_width
    cut_up = cut_out + model_width * hidden_width
    return (flat_weights[:cut_qkv].reshape(model_width, 3 * model_width), flat_weights[cut_qkv:cut_out].reshape(model_width, model_width), flat_weights[cut_out:cut_up].reshape(model_width, hidden_width), flat_weights[cut_up:].reshape(hidden_width, model_width))

def spatial_mix(queries, keys, values):
    scores = low_back(jnp.einsum('tphe,tqhe->thpq', queries, keys, precision=highest) * HEAD_DIM ** (-0.5))
    attention = jax.nn.softmax(scores, axis=-1)
    return jnp.einsum('thpq,tqhe->tphe', low(attention), values, precision=highest)

def temporal_mix(queries, keys, values, length):
    scores = low_back(jnp.einsum('tphe,uphe->phtu', queries, keys, precision=highest) * HEAD_DIM ** (-0.5))
    slot_index = jnp.arange(T_MAX)
    allowed = (slot_index[None, :] <= slot_index[:, None]) & (slot_index[None, :] < length)
    scores = jnp.where(allowed, scores, masked_score)
    attention = jax.nn.softmax(scores, axis=-1)
    return jnp.einsum('phtu,uphe->tphe', low(attention), values, precision=highest)

def block_apply(token_rows, flat_weights, norm_pair, mixer):
    w_qkv, w_out, w_up, w_down = unpack(flat_weights, D, FF)
    normed = low(norm_apply(token_rows, norm_pair[0, 0], norm_pair[0, 1]))
    packed = low(low_back(dense(normed, w_qkv)))
    token_grid = packed.reshape(T_MAX, PATCHES, 3, HEADS, HEAD_DIM)
    mixture = low_back(low(mixer(token_grid[:, :, 0], token_grid[:, :, 1], token_grid[:, :, 2])))
    token_rows = token_rows + low_back(dense(mixture.reshape(-1, D), w_out))
    second = low(norm_apply(token_rows, norm_pair[1, 0], norm_pair[1, 1]))
    hidden_pre = low_back(dense(second, w_up))
    active = low(jax.nn.gelu(hidden_pre, approximate=False))
    return token_rows + low_back(dense(active, w_down))

def adamw(param_value, moment, second, grad_total, step_value, rate, decay_rate):
    moment_next = beta_first * moment + (1.0 - beta_first) * grad_total
    second_next = beta_second * second + (1.0 - beta_second) * grad_total * grad_total
    moment_hat = moment_next / (1.0 - beta_first ** step_value)
    second_hat = second_next / (1.0 - beta_second ** step_value)
    param_next = param_value - rate * (moment_hat / (jnp.sqrt(second_hat) + adam_floor) + decay_rate * param_value)
    return (param_next, moment_next, second_next)

def reference(clip_tokens, cotangent, lengths, params, param_moment, param_second, norm_par, norm_moment, norm_second):
    weight_copy = low(params)
    norm_copy = low(norm_par).reshape(2, 2, 2, D)

    def per_clip(totals, clip_item):
        clip_rows, clip_grad, length = clip_item

        def forward(token_rows, weights, norm_table):
            middle = block_apply(token_rows, weights[0], norm_table[0], spatial_mix)
            return block_apply(middle, weights[1], norm_table[1], partial(temporal_mix, length=length))
        result, pullback = jax.vjp(forward, clip_rows.astype(jnp.float32).reshape(-1, D), weight_copy, norm_copy)
        live_mask = (jnp.arange(T_MAX) < length).astype(jnp.float32)
        seed_grad = (clip_grad.astype(jnp.float32) * live_mask[:, None, None]).reshape(-1, D)
        grad_rows, grad_weights, grad_norms = pullback(seed_grad)
        return ((totals[0] + grad_weights, totals[1] + grad_norms), (result.reshape(T_MAX, PATCHES, D), grad_rows.reshape(T_MAX, PATCHES, D)))
    initial = (jnp.zeros(params.shape, jnp.float32), jnp.zeros((2, 2, 2, D), jnp.float32))
    (grad_weights, grad_norms), (output, grad_input) = lax.scan(per_clip, initial, (clip_tokens, cotangent, lengths))
    step_value = float(STEP)
    new_params, new_moment, new_second = adamw(params, param_moment, param_second, grad_weights, step_value, learn_rate, weight_decay)
    new_norm, new_norm_moment, new_norm_second = adamw(norm_par, norm_moment, norm_second, grad_norms.reshape(-1), step_value, norm_rate, 0.0)
    return (output, grad_input, new_params, new_moment, new_second, new_params.astype(jnp.bfloat16), new_norm, new_norm_moment, new_norm_second)
```

```python
from functools import partial

import jax
import jax.numpy as jnp
from jax import lax
from jax.experimental import pallas as pl
from jax.experimental.pallas import tpu as pltpu
from jax.sharding import PartitionSpec as P

HEADS = 8
HEAD_DIM = 64
FF = 2048
STEP = 7

norm_epsilon = 1e-05
beta_first = 0.9
beta_second = 0.999
learn_rate = 0.05
norm_rate = 0.5
weight_decay = 0.1
adam_floor = 1e-08
masked_score = -1e30

bf16 = jnp.bfloat16
f32 = jnp.float32
MIB = 2**20

SPATIAL_TILE = 256
TEMPORAL_TILE = 256
PATCH_GROUP = 16


def dot_nn(left, right):
    return lax.dot_general(left, right, (((1,), (0,)), ((), ())), preferred_element_type=f32)


def dot_nt(left, right):
    return lax.dot_general(left, right, (((1,), (1,)), ((), ())), preferred_element_type=f32)


def dot_tn(left, right):
    return lax.dot_general(left, right, (((0,), (0,)), ((), ())), preferred_element_type=f32)


def normalise(rows):
    center = rows - jnp.mean(rows, axis=-1, keepdims=True)
    spread = jnp.mean(center * center, axis=-1, keepdims=True)
    scale = lax.rsqrt(spread + norm_epsilon)
    return center * scale, scale


def fold_rows(rows):
    return jnp.sum(rows.reshape(-1, 8, rows.shape[-1]), axis=0)


def norm_backward(hat, scale, gain, grad):
    weighted = grad * gain
    mean_first = jnp.mean(weighted, axis=-1, keepdims=True)
    mean_second = jnp.mean(weighted * hat, axis=-1, keepdims=True)
    grad_rows = scale * (weighted - mean_first - hat * mean_second)
    return grad_rows, fold_rows(grad * hat), fold_rows(grad)


def gelu_pair(value):
    cumulative = 0.5 + 0.5 * lax.erf(value * 0.7071067811865476)
    density = jnp.exp(-0.5 * value * value) * 0.3989422804014327
    return value * cumulative, cumulative + value * density


def lane_halves(count):
    lane = lax.broadcasted_iota(jnp.int32, (count, 2 * HEAD_DIM), 1)
    return lane < HEAD_DIM


def only_head(pair, low_half, which):
    keep = low_half if which == 0 else jnp.logical_not(low_half)
    return jnp.where(keep, pair, jnp.zeros_like(pair))


def softmax(scores):
    top = jnp.max(scores, axis=-1, keepdims=True)
    powers = jnp.exp(scores - top)
    return powers * (1.0 / jnp.sum(powers, axis=-1, keepdims=True))


def attend(query, key, value, low_half, bias):
    query = query * jnp.asarray(HEAD_DIM**-0.5, bf16)
    weights = []
    mixture = None
    for which in range(2):
        scores = dot_nt(query, only_head(key, low_half, which))
        if bias is not None:
            scores = scores + bias
        soft = softmax(scores).astype(bf16)
        weights.append(soft)
        part = dot_nn(soft, only_head(value, low_half, which))
        mixture = part if mixture is None else mixture + part
    return weights, mixture.astype(bf16)


def attend_backward(query, key, value, grad, weights, low_half):
    scale = jnp.asarray(HEAD_DIM**-0.5, bf16)
    query = query * scale
    scaled_key = key * scale
    totals = [None, None, None]
    for which in range(2):
        soft = weights[which]
        grad_soft = dot_nt(grad, only_head(value, low_half, which))
        wide = soft.astype(f32)
        product = grad_soft * wide
        inner = jnp.sum(product, axis=-1, keepdims=True)
        grad_scores = (product - wide * inner).astype(bf16)
        parts = (
            dot_nn(grad_scores, only_head(scaled_key, low_half, which)),
            dot_tn(grad_scores, only_head(query, low_half, which)),
            dot_tn(soft, only_head(grad, low_half, which)),
        )
        totals = [p if t is None else t + p for t, p in zip(totals, parts)]
    return [t.astype(bf16) for t in totals]


def feed_forward(second, w_up, w_down, active_ref, slope_ref, chunk=512):
    hidden = w_up.shape[1]
    for start in range(0, hidden, chunk):
        active, slope = gelu_pair(dot_nn(second, w_up[:, start : start + chunk]))
        active_ref[:, start : start + chunk] = active.astype(bf16)
        slope_ref[:, start : start + chunk] = slope.astype(bf16)
    return dot_nn(active_ref[...], w_down[...])


def hidden_backward(branch, w_down, slope_ref, hidden_ref, chunk=512):
    hidden = w_down.shape[0]
    for start in range(0, hidden, chunk):
        grad = dot_nt(branch, w_down[start : start + chunk, :])
        slope = slope_ref[:, start : start + chunk].astype(f32)
        hidden_ref[:, start : start + chunk] = (grad * slope).astype(bf16)


def spatial_forward_kernel(
    x_ref, w_qkv, w_out, w_up, w_down, norm_ref,
    packed_ref, weights_ref, mixture_ref, middle_ref, active_ref, slope_ref, after_ref,
):
    width = x_ref.shape[1]
    rows = x_ref[...].astype(f32)
    hat, _ = normalise(rows)
    first = (hat * norm_ref[0:1] + norm_ref[1:2]).astype(bf16)
    packed_ref[...] = dot_nn(first, w_qkv[...]).astype(bf16)
    frame = weights_ref.shape[2]
    low_half = lane_halves(frame)
    for item in range(weights_ref.shape[0]):
        span = slice(item * frame, (item + 1) * frame)
        for pair in range(HEADS // 2):
            cut = [
                packed_ref[span, part * width + 128 * pair : part * width + 128 * (pair + 1)]
                for part in range(3)
            ]
            weights, mixture = attend(*cut, low_half, None)
            weights_ref[item, 2 * pair] = weights[0]
            weights_ref[item, 2 * pair + 1] = weights[1]
            mixture_ref[span, 128 * pair : 128 * (pair + 1)] = mixture
    middle = rows + dot_nn(mixture_ref[...], w_out[...])
    middle_ref[...] = middle
    hat, _ = normalise(middle)
    second = (hat * norm_ref[2:3] + norm_ref[3:4]).astype(bf16)
    after_ref[...] = middle + feed_forward(second, w_up, w_down, active_ref, slope_ref)


def whole(shape):
    return pl.BlockSpec(shape, lambda *_: (0,) * len(shape), pipeline_mode=pl.Buffered(1))


def tiles(tile, *rest):
    return pl.BlockSpec((tile, *rest), lambda i: (i,) + (0,) * len(rest))


def spatial_forward(x, weights, norms, frame):
    tokens, width = x.shape
    hidden = weights[2].shape[1]
    tile = SPATIAL_TILE
    frames = tile // frame
    return pl.pallas_call(
        spatial_forward_kernel,
        grid=(tokens // tile,),
        in_specs=[tiles(tile, width)] + [whole(w.shape) for w in weights] + [whole(norms.shape)],
        out_specs=[
            tiles(tile, 3 * width),
            tiles(frames, HEADS, frame, frame),
            tiles(tile, width),
            tiles(tile, width),
            tiles(tile, hidden),
            tiles(tile, hidden),
            tiles(tile, width),
        ],
        out_shape=[
            jax.ShapeDtypeStruct((tokens, 3 * width), bf16),
            jax.ShapeDtypeStruct((tokens // frame, HEADS, frame, frame), bf16),
            jax.ShapeDtypeStruct((tokens, width), bf16),
            jax.ShapeDtypeStruct((tokens, width), f32),
            jax.ShapeDtypeStruct((tokens, hidden), bf16),
            jax.ShapeDtypeStruct((tokens, hidden), bf16),
            jax.ShapeDtypeStruct((tokens, width), f32),
        ],
        compiler_params=pltpu.CompilerParams(vmem_limit_bytes=56 * MIB),
    )(x, *weights, norms)


def weight_grads(first, grad_packed, mixture, attn, second, grad_hidden, active, branch, outs, chunk=512):
    sides = ((first, grad_packed), (mixture, attn), (second, grad_hidden), (active, branch))
    for (left, right), out in zip(sides, outs):
        for start in range(0, out.shape[1], chunk):
            out[:, start : start + chunk] = dot_tn(
                left[...], right[:, start : start + chunk]
            ).astype(out.dtype)


def temporal_kernel(
    length_ref, rows_ref, cotangent_ref, w_qkv, w_out, w_up, w_down, norm_ref,
    result_ref, before_ref, g_qkv, g_out, g_up, g_down, g_norm,
    packed, slope, weights_buf, grad_mix,
    first_all, packed_all, mixture_all, attn_all, second_all, hidden_all, active_all, branch_all,
):
    step = pl.program_id(0)
    steps, patches, width = rows_ref.shape
    tile = steps * patches
    here = pl.ds(pl.multiple_of(step * tile, tile), tile)
    length = length_ref[0]
    group = PATCH_GROUP
    count = steps * group

    @pl.when(step == 0)
    def _():
        g_norm[...] = jnp.zeros_like(g_norm)

    row = lax.broadcasted_iota(jnp.int32, (count, count), 0)
    column = lax.broadcasted_iota(jnp.int32, (count, count), 1)
    seen = (row % group == column % group) & (column // group <= row // group)
    seen = seen & (column // group < length)
    bias = jnp.where(seen, 0.0, masked_score)
    low_half = lane_halves(count)

    rows = rows_ref[...].reshape(tile, width)
    hat, _ = normalise(rows)
    first = (hat * norm_ref[0:1] + norm_ref[1:2]).astype(bf16)
    first_all[here, :] = first
    packed[...] = dot_nn(first, w_qkv[...]).astype(bf16).reshape(packed.shape)

    mixture_view = mixture_all.at[here, :]

    def cut(source, part, place, pair):
        start = part * width + 128 * pair
        return source[:, place : place + group, start : start + 128].reshape(count, 128)

    for place in range(0, patches, group):
        for pair in range(HEADS // 2):
            weights, mixture = attend(
                *[cut(packed, part, place, pair) for part in range(3)], low_half, bias
            )
            for which in range(2):
                weights_buf[place // group, 2 * pair + which] = weights[which]
            grad_mix[:, place : place + group, 128 * pair : 128 * (pair + 1)] = mixture.reshape(
                steps, group, 128
            )
    mixture = grad_mix[...].reshape(tile, width)
    mixture_all[here, :] = mixture
    middle = rows + dot_nn(mixture, w_out[...])
    hat, scale = normalise(middle)
    second = (hat * norm_ref[2:3] + norm_ref[3:4]).astype(bf16)
    second_all[here, :] = second
    after = middle + feed_forward(second, w_up, w_down, active_all.at[here, :], slope)
    result_ref[...] = after.reshape(result_ref.shape)

    slot = lax.broadcasted_iota(jnp.int32, rows_ref.shape, 0)
    live = (slot < length).astype(f32)
    grad_after = (cotangent_ref[...].astype(f32) * live).reshape(tile, width)
    branch = grad_after.astype(bf16)
    branch_all[here, :] = branch
    hidden_backward(branch, w_down, slope, hidden_all.at[here, :])
    grad_second = dot_nt(hidden_all[here, :], w_up[...])
    hat, scale = normalise(middle)
    grad_rows, gain, shift = norm_backward(hat, scale, norm_ref[2:3], grad_second)
    g_norm[2] += gain
    g_norm[3] += shift
    grad_middle = grad_after + grad_rows
    attn = grad_middle.astype(bf16)
    attn_all[here, :] = attn
    grad_mix[...] = dot_nt(attn, w_out[...]).astype(bf16).reshape(grad_mix.shape)
    for place in range(0, patches, group):
        for pair in range(HEADS // 2):
            grads = attend_backward(
                *[cut(packed, part, place, pair) for part in range(3)],
                cut(grad_mix, 0, place, pair),
                [weights_buf[place // group, 2 * pair + which] for which in range(2)],
                low_half,
            )
            for part in range(3):
                start = part * width + 128 * pair
                packed[:, place : place + group, start : start + 128] = grads[part].reshape(
                    steps, group, 128
                )
    grad_packed = packed[...].reshape(tile, 3 * width)
    packed_all[here, :] = grad_packed
    grad_first = dot_nt(grad_packed, w_qkv[...])
    hat, scale = normalise(rows)
    grad_rows, gain, shift = norm_backward(hat, scale, norm_ref[0:1], grad_first)
    g_norm[0] += gain
    g_norm[1] += shift
    before_ref[...] = (grad_middle + grad_rows).reshape(before_ref.shape)

    @pl.when(step == pl.num_programs(0) - 1)
    def _():
        weight_grads(
            first_all, packed_all, mixture_all, attn_all, second_all, hidden_all, active_all,
            branch_all, (g_qkv, g_out, g_up, g_down),
        )


def temporal_block(length, rows, cotangent, weights, norms):
    steps, patches, width = rows.shape
    tokens = steps * patches
    hidden = weights[2].shape[1]
    part = TEMPORAL_TILE // steps
    slab = pl.BlockSpec((steps, part, width), lambda i: (0, i, 0))
    return pl.pallas_call(
        temporal_kernel,
        grid=(patches // part,),
        in_specs=[pl.BlockSpec(memory_space=pltpu.SMEM), slab, slab]
        + [whole(w.shape) for w in weights]
        + [whole(norms.shape)],
        out_specs=[slab, slab] + [whole(w.shape) for w in weights] + [whole((4, 8, width))],
        out_shape=[
            jax.ShapeDtypeStruct(rows.shape, f32),
            jax.ShapeDtypeStruct(rows.shape, f32),
        ]
        + [jax.ShapeDtypeStruct(w.shape, bf16) for w in weights]
        + [jax.ShapeDtypeStruct((4, 8, width), f32)],
        scratch_shapes=[
            pltpu.VMEM((steps, part, 3 * width), bf16),
            pltpu.VMEM((TEMPORAL_TILE, hidden), bf16),
            pltpu.VMEM((part // PATCH_GROUP, HEADS, steps * PATCH_GROUP, steps * PATCH_GROUP), bf16),
            pltpu.VMEM((steps, part, width), bf16),
            pltpu.VMEM((tokens, width), bf16),
            pltpu.VMEM((tokens, 3 * width), bf16),
            pltpu.VMEM((tokens, width), bf16),
            pltpu.VMEM((tokens, width), bf16),
            pltpu.VMEM((tokens, width), bf16),
            pltpu.VMEM((tokens, hidden), bf16),
            pltpu.VMEM((tokens, hidden), bf16),
            pltpu.VMEM((tokens, width), bf16),
        ],
        compiler_params=pltpu.CompilerParams(vmem_limit_bytes=62 * MIB),
    )(length, rows, cotangent, *weights, norms)


def spatial_backward_kernel(
    x_ref, grad_ref, packed_ref, weights_ref, middle_ref, slope_ref, mixture_all, active_all,
    w_qkv, w_out, w_up, w_down, norm_ref,
    before_ref, g_qkv, g_out, g_up, g_down, g_norm,
    grad_mix, first_all, packed_all, attn_all, second_all, hidden_all, branch_all,
):
    step = pl.program_id(0)
    tile, width = x_ref.shape
    here = pl.ds(pl.multiple_of(step * tile, tile), tile)

    @pl.when(step == 0)
    def _():
        g_norm[...] = jnp.zeros_like(g_norm)

    grad_after = grad_ref[...]
    branch = grad_after.astype(bf16)
    branch_all[here, :] = branch
    hidden_backward(branch, w_down, slope_ref, hidden_all.at[here, :])
    grad_second = dot_nt(hidden_all[here, :], w_up[...])
    hat, scale = normalise(middle_ref[...])
    second_all[here, :] = (hat * norm_ref[2:3] + norm_ref[3:4]).astype(bf16)
    grad_rows, gain, shift = norm_backward(hat, scale, norm_ref[2:3], grad_second)
    g_norm[2] += gain
    g_norm[3] += shift
    grad_middle = grad_after + grad_rows
    attn = grad_middle.astype(bf16)
    attn_all[here, :] = attn
    grad_mix[...] = dot_nt(attn, w_out[...]).astype(bf16)
    frame = weights_ref.shape[2]
    low_half = lane_halves(frame)
    for item in range(weights_ref.shape[0]):
        span = slice(item * frame, (item + 1) * frame)
        there = pl.ds(pl.multiple_of(step * tile + item * frame, frame), frame)
        for pair in range(HEADS // 2):
            grads = attend_backward(
                *[
                    packed_ref[span, part * width + 128 * pair : part * width + 128 * (pair + 1)]
                    for part in range(3)
                ],
                grad_mix[span, 128 * pair : 128 * (pair + 1)],
                [weights_ref[item, 2 * pair + which] for which in range(2)],
                low_half,
            )
            for part in range(3):
                start = part * width + 128 * pair
                packed_all[there, start : start + 128] = grads[part]
    grad_first = dot_nt(packed_all[here, :], w_qkv[...])
    hat, scale = normalise(x_ref[...].astype(f32))
    first_all[here, :] = (hat * norm_ref[0:1] + norm_ref[1:2]).astype(bf16)
    grad_rows, gain, shift = norm_backward(hat, scale, norm_ref[0:1], grad_first)
    g_norm[0] += gain
    g_norm[1] += shift
    before_ref[...] = grad_middle + grad_rows

    @pl.when(step == pl.num_programs(0) - 1)
    def _():
        weight_grads(
            first_all, packed_all, mixture_all, attn_all, second_all, hidden_all, active_all,
            branch_all, (g_qkv, g_out, g_up, g_down),
        )


def spatial_backward(x, grad, kept, weights, norms):
    packed, soft, mixture, middle, active, slope = kept
    tokens, width = x.shape
    hidden = weights[2].shape[1]
    frame = soft.shape[2]
    tile = SPATIAL_TILE
    return pl.pallas_call(
        spatial_backward_kernel,
        grid=(tokens // tile,),
        in_specs=[
            tiles(tile, width),
            tiles(tile, width),
            tiles(tile, 3 * width),
            tiles(tile // frame, HEADS, frame, frame),
            tiles(tile, width),
            tiles(tile, hidden),
            whole(mixture.shape),
            whole(active.shape),
        ]
        + [whole(w.shape) for w in weights]
        + [whole(norms.shape)],
        out_specs=[tiles(tile, width)]
        + [whole(w.shape) for w in weights]
        + [whole((4, 8, width))],
        out_shape=[jax.ShapeDtypeStruct((tokens, width), f32)]
        + [jax.ShapeDtypeStruct(w.shape, bf16) for w in weights]
        + [jax.ShapeDtypeStruct((4, 8, width), f32)],
        scratch_shapes=[
            pltpu.VMEM((tile, width), bf16),
            pltpu.VMEM((tokens, width), bf16),
            pltpu.VMEM((tokens, 3 * width), bf16),
            pltpu.VMEM((tokens, width), bf16),
            pltpu.VMEM((tokens, width), bf16),
            pltpu.VMEM((tokens, hidden), bf16),
            pltpu.VMEM((tokens, width), bf16),
        ],
        compiler_params=pltpu.CompilerParams(vmem_limit_bytes=62 * MIB),
    )(x, grad, packed, soft, middle, slope, mixture, active, *weights, norms)


def unpack(flat_weights, model_width, hidden_width):
    cut_qkv = 3 * model_width * model_width
    cut_out = 4 * model_width * model_width
    cut_up = cut_out + model_width * hidden_width
    return (
        flat_weights[:cut_qkv].reshape(model_width, 3 * model_width),
        flat_weights[cut_qkv:cut_out].reshape(model_width, model_width),
        flat_weights[cut_out:cut_up].reshape(model_width, hidden_width),
        flat_weights[cut_up:].reshape(hidden_width, model_width),
    )


def adamw(param_value, moment, second, grad_total, step_value, rate, decay_rate):
    moment_next = beta_first * moment + (1.0 - beta_first) * grad_total
    second_next = beta_second * second + (1.0 - beta_second) * grad_total * grad_total
    moment_hat = moment_next / (1.0 - beta_first**step_value)
    second_hat = second_next / (1.0 - beta_second**step_value)
    param_next = param_value - rate * (
        moment_hat / (jnp.sqrt(second_hat) + adam_floor) + decay_rate * param_value
    )
    return (param_next, moment_next, second_next)


def on_device(
    clip_tokens,
    cotangent,
    lengths,
    params,
    param_moment,
    param_second,
    norm_par,
    norm_moment,
    norm_second,
):
    clip_count, step_slots, patch_count, model_width = clip_tokens.shape
    shards = lax.axis_size("dp")
    gathered = lax.all_gather(params.astype(bf16), "dp", axis=1, tiled=True)
    norm_whole = lax.all_gather(norm_par.astype(bf16), "dp", axis=0, tiled=True)
    norm_table = norm_whole.astype(f32).reshape(2, 4, model_width)
    spatial_weights = unpack(gathered[0], model_width, FF)
    temporal_weights = unpack(gathered[1], model_width, FF)
    x = clip_tokens.reshape(-1, model_width)
    *kept, after = spatial_forward(x, spatial_weights, norm_table[0], patch_count)
    result, grad_after, *temporal_grads, temporal_norm = temporal_block(
        lengths,
        after.reshape(step_slots, patch_count, model_width),
        cotangent.reshape(step_slots, patch_count, model_width),
        temporal_weights,
        norm_table[1],
    )
    grad_before, *spatial_grads, spatial_norm = spatial_backward(
        x, grad_after.reshape(-1, model_width), kept, spatial_weights, norm_table[0]
    )

    def scatter(grads):
        flat = jnp.concatenate([g.reshape(-1) for g in grads])
        return lax.psum_scatter(flat, "dp", scatter_dimension=0, tiled=True).astype(f32)

    weight_sum = jnp.stack([scatter(spatial_grads), scatter(temporal_grads)])
    norm_grad = jnp.stack([spatial_norm, temporal_norm]).sum(axis=2).reshape(-1)
    norm_sum = lax.psum_scatter(norm_grad, "dp", scatter_dimension=0, tiled=True)
    step_value = float(STEP)
    new_params, new_moment, new_second = adamw(
        params, param_moment, param_second, weight_sum, step_value, learn_rate, weight_decay
    )
    new_norm, new_norm_moment, new_norm_second = adamw(
        norm_par, norm_moment, norm_second, norm_sum, step_value, norm_rate, 0.0
    )
    return (
        result.reshape(clip_tokens.shape),
        grad_before.reshape(clip_tokens.shape),
        new_params,
        new_moment,
        new_second,
        new_params.astype(bf16),
        new_norm,
        new_norm_moment,
        new_norm_second,
    )


def solution(mesh):
    placed = (
        P("dp", None, None, None),
        P("dp", None, None, None),
        P("dp"),
        P(None, "dp"),
        P(None, "dp"),
        P(None, "dp"),
        P("dp"),
        P("dp"),
        P("dp"),
    )
    return jax.shard_map(
        on_device,
        mesh=mesh,
        in_specs=placed,
        out_specs=(
            P("dp", None, None, None),
            P("dp", None, None, None),
            P(None, "dp"),
            P(None, "dp"),
            P(None, "dp"),
            P(None, "dp"),
            P("dp"),
            P("dp"),
            P("dp"),
        ),
        check_vma=False,
    )
```

```python
from functools import partial

import jax
import jax.numpy as jnp
from jax import lax
from jax.experimental import pallas as pl
from jax.experimental.pallas import tpu as pltpu
from jax.sharding import PartitionSpec as P

HEADS = 8
HEAD_DIM = 64
FF = 2048
STEP = 7

norm_epsilon = 1e-05
beta_first = 0.9
beta_second = 0.999
learn_rate = 0.05
norm_rate = 0.5
weight_decay = 0.1
adam_floor = 1e-08
masked_score = -1e30

bf16 = jnp.bfloat16
f32 = jnp.float32
MIB = 2**20

SPATIAL_TILE = 256
TEMPORAL_TILE = 256
PATCH_GROUP = 16


def dot_nn(left, right):
    return lax.dot_general(left, right, (((1,), (0,)), ((), ())), preferred_element_type=f32)


def dot_nt(left, right):
    return lax.dot_general(left, right, (((1,), (1,)), ((), ())), preferred_element_type=f32)


def dot_tn(left, right):
    return lax.dot_general(left, right, (((0,), (0,)), ((), ())), preferred_element_type=f32)


def normalise(rows):
    center = rows - jnp.mean(rows, axis=-1, keepdims=True)
    spread = jnp.mean(center * center, axis=-1, keepdims=True)
    scale = lax.rsqrt(spread + norm_epsilon)
    return center * scale, scale


def fold_rows(rows):
    return jnp.sum(rows.reshape(-1, 8, rows.shape[-1]), axis=0)


def norm_backward(hat, scale, gain, grad):
    weighted = grad * gain
    mean_first = jnp.mean(weighted, axis=-1, keepdims=True)
    mean_second = jnp.mean(weighted * hat, axis=-1, keepdims=True)
    grad_rows = scale * (weighted - mean_first - hat * mean_second)
    return grad_rows, fold_rows(grad * hat), fold_rows(grad)


def gelu_pair(value):
    cumulative = 0.5 + 0.5 * lax.erf(value * 0.7071067811865476)
    density = jnp.exp(-0.5 * value * value) * 0.3989422804014327
    return value * cumulative, cumulative + value * density


def lane_halves(count):
    lane = lax.broadcasted_iota(jnp.int32, (count, 2 * HEAD_DIM), 1)
    return lane < HEAD_DIM


def only_head(pair, low_half, which):
    keep = low_half if which == 0 else jnp.logical_not(low_half)
    return jnp.where(keep, pair, jnp.zeros_like(pair))


def softmax(scores):
    top = jnp.max(scores, axis=-1, keepdims=True)
    powers = jnp.exp(scores - top)
    return powers * (1.0 / jnp.sum(powers, axis=-1, keepdims=True))


def attend(query, key, value, low_half, bias):
    query = query * jnp.asarray(HEAD_DIM**-0.5, bf16)
    weights = []
    mixture = None
    for which in range(2):
        scores = dot_nt(query, only_head(key, low_half, which))
        if bias is not None:
            scores = scores + bias
        soft = softmax(scores).astype(bf16)
        weights.append(soft)
        part = dot_nn(soft, only_head(value, low_half, which))
        mixture = part if mixture is None else mixture + part
    return weights, mixture.astype(bf16)


def attend_backward(query, key, value, grad, weights, low_half):
    scale = jnp.asarray(HEAD_DIM**-0.5, bf16)
    query = query * scale
    scaled_key = key * scale
    totals = [None, None, None]
    for which in range(2):
        soft = weights[which]
        grad_soft = dot_nt(grad, only_head(value, low_half, which))
        wide = soft.astype(f32)
        product = grad_soft * wide
        inner = jnp.sum(product, axis=-1, keepdims=True)
        grad_scores = (product - wide * inner).astype(bf16)
        parts = (
            dot_nn(grad_scores, only_head(scaled_key, low_half, which)),
            dot_tn(grad_scores, only_head(query, low_half, which)),
            dot_tn(soft, only_head(grad, low_half, which)),
        )
        totals = [p if t is None else t + p for t, p in zip(totals, parts)]
    return [t.astype(bf16) for t in totals]


def feed_forward(second, w_up, w_down, active_ref, slope_ref, chunk=512):
    hidden = w_up.shape[1]
    for start in range(0, hidden, chunk):
        active, slope = gelu_pair(dot_nn(second, w_up[:, start : start + chunk]))
        active_ref[:, start : start + chunk] = active.astype(bf16)
        slope_ref[:, start : start + chunk] = slope.astype(bf16)
    return dot_nn(active_ref[...], w_down[...])


def hidden_backward(branch, w_down, slope_ref, hidden_ref, chunk=512):
    hidden = w_down.shape[0]
    for start in range(0, hidden, chunk):
        grad = dot_nt(branch, w_down[start : start + chunk, :])
        slope = slope_ref[:, start : start + chunk].astype(f32)
        hidden_ref[:, start : start + chunk] = (grad * slope).astype(bf16)


def spatial_forward_kernel(
    x_ref, w_qkv, w_out, w_up, w_down, norm_ref,
    packed_ref, weights_ref, mixture_ref, middle_ref, active_ref, slope_ref, after_ref,
):
    width = x_ref.shape[1]
    rows = x_ref[...].astype(f32)
    hat, _ = normalise(rows)
    first = (hat * norm_ref[0:1] + norm_ref[1:2]).astype(bf16)
    packed_ref[...] = dot_nn(first, w_qkv[...]).astype(bf16)
    frame = weights_ref.shape[2]
    low_half = lane_halves(frame)
    for item in range(weights_ref.shape[0]):
        span = slice(item * frame, (item + 1) * frame)
        for pair in range(HEADS // 2):
            cut = [
                packed_ref[span, part * width + 128 * pair : part * width + 128 * (pair + 1)]
                for part in range(3)
            ]
            weights, mixture = attend(*cut, low_half, None)
            weights_ref[item, 2 * pair] = weights[0]
            weights_ref[item, 2 * pair + 1] = weights[1]
            mixture_ref[span, 128 * pair : 128 * (pair + 1)] = mixture
    middle = rows + dot_nn(mixture_ref[...], w_out[...])
    middle_ref[...] = middle
    hat, _ = normalise(middle)
    second = (hat * norm_ref[2:3] + norm_ref[3:4]).astype(bf16)
    after_ref[...] = middle + feed_forward(second, w_up, w_down, active_ref, slope_ref)


def whole(shape):
    return pl.BlockSpec(shape, lambda *_: (0,) * len(shape), pipeline_mode=pl.Buffered(1))


def tiles(tile, *rest):
    return pl.BlockSpec((tile, *rest), lambda i: (i,) + (0,) * len(rest))


def spatial_forward(x, weights, norms, frame):
    tokens, width = x.shape
    hidden = weights[2].shape[1]
    tile = SPATIAL_TILE
    frames = tile // frame
    return pl.pallas_call(
        spatial_forward_kernel,
        grid=(tokens // tile,),
        in_specs=[tiles(tile, width)] + [whole(w.shape) for w in weights] + [whole(norms.shape)],
        out_specs=[
            tiles(tile, 3 * width),
            tiles(frames, HEADS, frame, frame),
            tiles(tile, width),
            tiles(tile, width),
            tiles(tile, hidden),
            tiles(tile, hidden),
            tiles(tile, width),
        ],
        out_shape=[
            jax.ShapeDtypeStruct((tokens, 3 * width), bf16),
            jax.ShapeDtypeStruct((tokens // frame, HEADS, frame, frame), bf16),
            jax.ShapeDtypeStruct((tokens, width), bf16),
            jax.ShapeDtypeStruct((tokens, width), f32),
            jax.ShapeDtypeStruct((tokens, hidden), bf16),
            jax.ShapeDtypeStruct((tokens, hidden), bf16),
            jax.ShapeDtypeStruct((tokens, width), f32),
        ],
        compiler_params=pltpu.CompilerParams(vmem_limit_bytes=56 * MIB),
    )(x, *weights, norms)


MESH_IDS = pl.DeviceIdType.MESH
LANES = 128
ROW_TILE = 16


def matrix_shapes(width, hidden):
    return ((width, 3 * width), (width, width), (width, hidden), (hidden, width))


def shard_plan(shards, width, hidden):
    plan = []
    base = 0
    regions = []
    for index, (rows, columns) in enumerate(matrix_shapes(width, hidden)):
        regions.append((index, base, rows, columns))
        base += rows * columns
    if base % shards:
        return None
    size = base // shards
    for device in range(shards):
        low, high = device * size, (device + 1) * size
        halves = ([], [])
        for index, start, rows, columns in regions:
            first, last = max(low, start), min(high, start + rows * columns)
            if first >= last:
                continue
            if (first - start) % columns or (last - start) % columns:
                return None
            row, count = (first - start) // columns, (last - first) // columns
            if row % ROW_TILE or count % ROW_TILE:
                return None
            stride = columns // LANES
            for block in range(stride):
                halves[2 * block // stride].append(
                    (index, row, count, block, (first - low) // LANES + block, stride)
                )
        place = 0
        entries = []
        for item in halves[0] + halves[1]:
            entries.append(item + (place,))
            place += item[2]
        plan.append(entries)
    return plan


def by_pattern(plan):
    groups = {}
    for device, entries in enumerate(plan):
        layout = tuple((e[2], e[4], e[5], e[6]) for e in entries)
        ranges = groups.setdefault(layout, [])
        if ranges and ranges[-1][1] == device:
            ranges[-1][1] = device + 1
        else:
            ranges.append([device, device + 1])
    return list(groups.items())


def on_pattern(plan, me, body):
    for layout, ranges in by_pattern(plan):
        inside = None
        for low, high in ranges:
            test = (me >= low) & (me < high)
            inside = test if inside is None else inside | test

        @pl.when(inside)
        def _(layout=layout):
            body(layout)


class Place:
    def __init__(self, me):
        self.me = me
        self.c = lax.rem(me, 2)
        self.x = lax.rem(me // 2, 2)
        self.y = lax.rem(me // 4, 2)
        self.z = me // 8

    def device(self, z, y, x, c):
        return ((z * 2 + y) * 2 + x) * 2 + c

    @property
    def sibling(self):
        return self.device(self.z, self.y, self.x, 1 - self.c)

    @property
    def across_x(self):
        return self.device(self.z, self.y, 1 - self.x, self.c)

    @property
    def across_y(self):
        return self.device(self.z, 1 - self.y, self.x, self.c)

    def plane(self, z):
        return self.device(z, self.y, self.x, self.c)


def remote(src, dst, send, recv, device):
    return pltpu.make_async_remote_copy(
        src_ref=src, dst_ref=dst, send_sem=send, recv_sem=recv, device_id=(device,), device_id_type=MESH_IDS
    )


def enter(place):
    barrier = pltpu.get_barrier_semaphore()
    partners = [place.sibling, place.across_x, place.across_y]
    partners += [place.plane(lax.rem(place.z + k, 4)) for k in range(1, 4)]
    for device in partners:
        pl.semaphore_signal(barrier, inc=1, device_id=(device,), device_id_type=MESH_IDS)
    pl.semaphore_wait(barrier, len(partners))


HALF = 384
SHARD = 784


class Gather:
    SEMS = 9

    def __init__(self, place, held, send, recv):
        self.p, self.held, self.send, self.recv = place, held, send, recv

    def along_z(self, k):
        p = self.p
        here = self.held.at[p.z, p.y, p.x, p.c]
        return remote(here, here, self.send.at[0, k - 1], self.recv.at[0, p.z], p.plane(lax.rem(p.z + k, 4)))

    def start_z(self):
        for k in range(1, 4):
            self.along_z(k).start()

    def wait_z(self, q):
        p = self.p

        @pl.when(q != p.z)
        def _():
            there = self.held.at[q, p.y, p.x, p.c]
            remote(there, there, self.send.at[0, 0], self.recv.at[0, q], p.me).wait_recv()

    def first(self, q):
        p, h = self.p, self.held
        a = h.at[q, p.y, p.x, p.c, pl.ds(0, HALF)]
        b = h.at[q, p.y, p.x, p.c, pl.ds(HALF, SHARD - HALF)]
        return (
            remote(a, a, self.send.at[1, q], self.recv.at[1, q], p.across_x),
            remote(b, b, self.send.at[2, q], self.recv.at[2, q], p.across_y),
        )

    def second(self, q):
        p, h = self.p, self.held
        a = h.at[q, p.y, :, p.c, pl.ds(0, HALF)]
        b = h.at[q, :, p.x, p.c, pl.ds(HALF, SHARD - HALF)]
        return (
            remote(a, a, self.send.at[3, q], self.recv.at[3, q], p.across_y),
            remote(b, b, self.send.at[4, q], self.recv.at[4, q], p.across_x),
        )

    def third(self, q):
        p, h = self.p, self.held
        a = h.at[q, :, :, p.c]
        return (remote(a, a, self.send.at[5, q], self.recv.at[5, q], p.sibling),)

    def begin_first(self, q):
        self.wait_z(q)
        for copy in self.first(q):
            copy.start()

    def begin_second(self, q):
        for copy in self.first(q):
            copy.wait_recv()
        for copy in self.second(q):
            copy.start()

    def begin_third(self, q):
        for copy in self.second(q):
            copy.wait_recv()
        for copy in self.third(q):
            copy.start()

    def finish(self, q):
        for copy in self.third(q):
            copy.wait_recv()

    def drain(self):
        for k in range(1, 4):
            self.along_z(k).wait_send()
        for q in range(4):
            for copy in self.first(q) + self.second(q) + self.third(q):
                copy.wait_send()


def load_shard(plan, me, shard_ref, norm_ref, held_here):
    def body(layout):
        for count, flat, stride, place in layout:
            held_here[pl.ds(place, count), :] = shard_ref[pl.ds(flat, count, stride), :].astype(bf16)

    on_pattern(plan, me, body)
    held_here[SHARD - ROW_TILE :, :] = jnp.broadcast_to(norm_ref[...], (ROW_TILE, LANES)).astype(bf16)


def coordinates(device):
    return device // 8, device // 4 % 2, device // 2 % 2, device % 2


def assemble(plan, held, outs, planes):
    for device, entries in enumerate(plan):
        z, y, x, c = coordinates(device)
        if z not in planes:
            continue
        for index, row, count, block, _, _, place in entries:
            outs[index][row : row + count, LANES * block : LANES * (block + 1)] = held[
                z, y, x, c, place : place + count, :
            ]


def assemble_norms(shards, held, norm_out):
    per_row = norm_out.shape[1] // LANES
    for device in range(shards):
        z, y, x, c = coordinates(device)
        row, column = device // per_row, device % per_row
        norm_out[row : row + 1, LANES * column : LANES * (column + 1)] = held[
            z, y, x, c, SHARD - ROW_TILE : SHARD, :
        ].astype(f32)[0:1]


def gather_kernel(plan, shard_ref, norm_ref, *refs):
    outs, norm_out, (held, send, recv) = refs[:8], refs[8], refs[9:]
    place = Place(lax.axis_index("dp"))
    enter(place)
    gathers = [Gather(place, held.at[b], send.at[b], recv.at[b]) for b in range(2)]
    for b in range(2):
        load_shard(
            plan, place.me, shard_ref.at[b], norm_ref, held.at[b, place.z, place.y, place.x, place.c]
        )
        gathers[b].start_z()
    for b in range(2):
        g = gathers[b]
        for stage in (g.begin_first, g.begin_second, g.begin_third):
            for q in range(4):
                stage(q)
        for q in range(4):
            g.finish(q)
        assemble(plan, held.at[b], outs[4 * b : 4 * b + 4], range(4))
        if b == 0:
            assemble_norms(len(plan), held.at[b], norm_out)
    for g in gathers:
        g.drain()


def gather_weights(plan, params, norm_par, width, hidden):
    size = params.shape[1]
    vmem = pl.BlockSpec(memory_space=pltpu.VMEM)
    shapes = matrix_shapes(width, hidden)
    outs = pl.pallas_call(
        partial(gather_kernel, plan),
        in_specs=[vmem, vmem],
        out_specs=[vmem] * 9,
        out_shape=[jax.ShapeDtypeStruct(s, bf16) for s in shapes * 2]
        + [jax.ShapeDtypeStruct((8, width), f32)],
        scratch_shapes=[
            pltpu.VMEM((2, 4, 2, 2, 2, SHARD, LANES), bf16),
            pltpu.SemaphoreType.DMA((2, 6, 4)),
            pltpu.SemaphoreType.DMA((2, 6, 4)),
        ],
        compiler_params=pltpu.CompilerParams(
            collective_id=0, has_side_effects=True, vmem_limit_bytes=48 * MIB
        ),
    )(params.reshape(2, size // LANES, LANES), norm_par.reshape(1, LANES))
    return outs[:4], outs[4:8], outs[8].reshape(2, 4, width)


class Scatter:
    def __init__(self, place, own, r1, r2a, r2b, r3, r4, send, recv):
        self.p, self.own = place, own
        self.r1, self.r2a, self.r2b, self.r3, self.r4 = r1, r2a, r2b, r3, r4
        self.send, self.recv = send, recv

    def first(self, q):
        p = self.p
        return (
            remote(
                self.own.at[q, :, :, 1 - p.c], self.r1.at[q], self.send.at[0, q], self.recv.at[0, q], p.sibling
            ),
        )

    def second(self, q):
        p = self.p
        low, high = pl.ds(0, HALF), pl.ds(HALF, SHARD - HALF)
        return (
            remote(
                self.r1.at[q, :, 1 - p.x, low], self.r2a.at[q], self.send.at[1, q], self.recv.at[1, q], p.across_x
            ),
            remote(
                self.r1.at[q, 1 - p.y, :, high], self.r2b.at[q], self.send.at[2, q], self.recv.at[2, q], p.across_y
            ),
        )

    def third(self, q):
        p = self.p
        low, high = pl.ds(0, HALF), pl.ds(HALF, SHARD - HALF)
        return (
            remote(
                self.r2a.at[q, 1 - p.y], self.r3.at[q, low], self.send.at[3, q], self.recv.at[3, q], p.across_y
            ),
            remote(
                self.r2b.at[q, 1 - p.x], self.r3.at[q, high], self.send.at[4, q], self.recv.at[4, q], p.across_x
            ),
        )

    def along_z(self, q):
        p = self.p
        return remote(self.r3.at[q], self.r4.at[p.z], self.send.at[5, q], self.recv.at[5, p.z], p.plane(q))

    def begin_first(self, q):
        for copy in self.first(q):
            copy.start()

    def begin_second(self, q, mine):
        for copy in self.first(q):
            copy.wait_recv()
        for y in range(2):
            for x in range(2):
                self.r1[q, y, x] = (self.r1[q, y, x].astype(f32) + mine[y, x].astype(f32)).astype(bf16)
        for copy in self.second(q):
            copy.start()

    def begin_third(self, q):
        p = self.p
        for copy in self.second(q):
            copy.wait_recv()
        low, high = pl.ds(0, HALF), pl.ds(HALF, SHARD - HALF)
        for k in range(2):
            self.r2a[q, k] = (self.r2a[q, k].astype(f32) + self.r1[q, k, p.x, low].astype(f32)).astype(bf16)
            self.r2b[q, k] = (self.r2b[q, k].astype(f32) + self.r1[q, p.y, k, high].astype(f32)).astype(bf16)
        for copy in self.third(q):
            copy.start()

    def begin_z(self, q):
        p = self.p
        for copy in self.third(q):
            copy.wait_recv()
        low, high = pl.ds(0, HALF), pl.ds(HALF, SHARD - HALF)
        self.r3[q, low] = (self.r3[q, low].astype(f32) + self.r2a[q, p.y].astype(f32)).astype(bf16)
        self.r3[q, high] = (self.r3[q, high].astype(f32) + self.r2b[q, p.x].astype(f32)).astype(bf16)

        @pl.when(q != p.z)
        def _():
            self.along_z(q).start()

    def finish(self, total):
        p = self.p
        for k in range(1, 4):
            z = lax.rem(p.z + k, 4)
            remote(self.r3.at[0], self.r4.at[z], self.send.at[5, 0], self.recv.at[5, z], p.me).wait_recv()
        total[...] = self.r3[p.z].astype(f32)
        for k in range(1, 4):
            total[...] += self.r4[lax.rem(p.z + k, 4)].astype(f32)

    def drain(self):
        for q in range(4):
            for copy in self.first(q) + self.second(q) + self.third(q):
                copy.wait_send()

            @pl.when(q != self.p.z)
            def _(q=q):
                self.along_z(q).wait_send()


SCATTER_SCRATCH = [
    pltpu.VMEM((4, 2, 2, SHARD, LANES), bf16),
    pltpu.VMEM((4, 2, HALF, LANES), bf16),
    pltpu.VMEM((4, 2, SHARD - HALF, LANES), bf16),
    pltpu.VMEM((4, SHARD, LANES), bf16),
    pltpu.VMEM((4, SHARD, LANES), bf16),
    pltpu.SemaphoreType.DMA((6, 4)),
    pltpu.SemaphoreType.DMA((6, 4)),
]


def unload_shard(plan, me, total, flat_ref):
    def body(layout):
        for count, flat, stride, place in layout:
            flat_ref[pl.ds(flat, count, stride), :] = total[pl.ds(place, count), :]

    on_pattern(plan, me, body)


def scatter_kernel(plan, g0, g1, flat0, flat1, norm_out, total, mine, load, *rest):
    place = Place(lax.axis_index("dp"))
    enter(place)
    count = len(SCATTER_SCRATCH)
    scatters = []
    for b, own in ((1, g1), (0, g0)):
        s = Scatter(place, own, *rest[b * count : (b + 1) * count])
        scatters.append((b, s, own))
    for b, s, own in scatters:
        for q in range(4):
            s.begin_first(q)
    for b, s, own in scatters:
        for q in range(4):
            copy = pltpu.make_async_copy(own.at[q, :, :, place.c], mine.at[b, q], load.at[b, q])
            copy.start()
        for q in range(4):
            pltpu.make_async_copy(own.at[q, :, :, place.c], mine.at[b, q], load.at[b, q]).wait()
            s.begin_second(q, mine.at[b, q])
        for q in range(4):
            s.begin_third(q)
        for q in range(4):
            s.begin_z(q)
    for b, s, own in scatters:
        s.finish(total)
        unload_shard(plan, place.me, total, (flat0, flat1)[b])
        if b == 1:
            norm_out[...] = total[SHARD - ROW_TILE : SHARD - ROW_TILE + 8]
        else:
            norm_out[...] += total[SHARD - ROW_TILE : SHARD - ROW_TILE + 8]
    for b, s, own in scatters:
        s.drain()


def scatter_grads(plan, grads):
    vmem = pl.BlockSpec(memory_space=pltpu.VMEM)
    rows = SHARD - ROW_TILE
    flat0, flat1, norm = pl.pallas_call(
        partial(scatter_kernel, plan),
        in_specs=[pl.BlockSpec(memory_space=pl.ANY)] * 2,
        out_specs=[vmem] * 3,
        out_shape=[
            jax.ShapeDtypeStruct((rows, LANES), f32),
            jax.ShapeDtypeStruct((rows, LANES), f32),
            jax.ShapeDtypeStruct((8, LANES), f32),
        ],
        scratch_shapes=[
            pltpu.VMEM((SHARD, LANES), f32),
            pltpu.VMEM((2, 4, 2, 2, SHARD, LANES), bf16),
            pltpu.SemaphoreType.DMA((2, 4)),
        ]
        + SCATTER_SCRATCH * 2,
        compiler_params=pltpu.CompilerParams(
            collective_id=1, has_side_effects=True, vmem_limit_bytes=48 * MIB
        ),
    )(*grads)
    return jnp.stack([flat0.reshape(-1), flat1.reshape(-1)]), norm[0] + norm[1]


def store_travel(plan, own, index, start, value):
    for device, entries in enumerate(plan):
        z, y, x, c = coordinates(device)
        for entry, row, count, block, _, _, place in entries:
            column = LANES * block - start
            if entry == index and 0 <= column < value.shape[1]:
                own[z, y, x, c, place : place + count, :] = value[row : row + count, column : column + LANES]


def store_norms(plan, own, block, sums):
    width = sums.shape[2]
    per_row = width // LANES
    line = lax.broadcasted_iota(jnp.int32, (ROW_TILE, LANES), 0)
    for device in range(len(plan)):
        z, y, x, c = coordinates(device)
        row = device // per_row - 4 * block
        if 0 <= row < 4:
            column = LANES * (device % per_row)
            value = jnp.sum(sums[row, :, column : column + LANES], axis=0, keepdims=True)
            coarse = value.astype(bf16).astype(f32)
            rows = jnp.where(line == 0, coarse, jnp.where(line == 1, value - coarse, 0.0))
        else:
            rows = jnp.zeros((ROW_TILE, LANES), f32)
        own[z, y, x, c, SHARD - ROW_TILE : SHARD, :] = rows.astype(bf16)


def weight_grads(first, grad_packed, mixture, attn, second, grad_hidden, active, branch, store, chunk=512):
    sides = ((first, grad_packed), (mixture, attn), (second, grad_hidden), (active, branch))
    for index, (left, right) in enumerate(sides):
        for start in range(0, right.shape[1], chunk):
            store(index, start, dot_tn(left[...], right[:, start : start + chunk]).astype(bf16))


def grad_outputs(plan, weights):
    shapes = [w.shape for w in weights] if plan is None else [(4, 2, 2, 2, SHARD, LANES)]
    return [whole(s) for s in shapes], [jax.ShapeDtypeStruct(s, bf16) for s in shapes]


def storing(plan, block, outs, sums):
    if plan is None:
        def store(index, start, value):
            outs[index][:, start : start + value.shape[1]] = value
        return store
    store_norms(plan, outs[0], block, sums)
    return partial(store_travel, plan, outs[0])


def temporal_kernel(
    plan, length_ref, rows_ref, cotangent_ref, w_qkv, w_out, w_up, w_down, norm_ref, result_ref, before_ref, *refs
):
    outs, g_norm = refs[:-13], refs[-13]
    packed, slope, weights_buf, grad_mix = refs[-12:-8]
    first_all, packed_all, mixture_all, attn_all, second_all, hidden_all, active_all, branch_all = refs[-8:]
    step = pl.program_id(0)
    steps, patches, width = rows_ref.shape
    tile = steps * patches
    here = pl.ds(pl.multiple_of(step * tile, tile), tile)
    length = length_ref[0]
    group = PATCH_GROUP
    count = steps * group

    @pl.when(step == 0)
    def _():
        g_norm[...] = jnp.zeros_like(g_norm)

    row = lax.broadcasted_iota(jnp.int32, (count, count), 0)
    column = lax.broadcasted_iota(jnp.int32, (count, count), 1)
    seen = (row % group == column % group) & (column // group <= row // group)
    seen = seen & (column // group < length)
    bias = jnp.where(seen, 0.0, masked_score)
    low_half = lane_halves(count)

    rows = rows_ref[...].reshape(tile, width)
    hat, _ = normalise(rows)
    first = (hat * norm_ref[0:1] + norm_ref[1:2]).astype(bf16)
    first_all[here, :] = first
    packed[...] = dot_nn(first, w_qkv[...]).astype(bf16).reshape(packed.shape)

    mixture_view = mixture_all.at[here, :]

    def cut(source, part, place, pair):
        start = part * width + 128 * pair
        return source[:, place : place + group, start : start + 128].reshape(count, 128)

    for place in range(0, patches, group):
        for pair in range(HEADS // 2):
            weights, mixture = attend(
                *[cut(packed, part, place, pair) for part in range(3)], low_half, bias
            )
            for which in range(2):
                weights_buf[place // group, 2 * pair + which] = weights[which]
            grad_mix[:, place : place + group, 128 * pair : 128 * (pair + 1)] = mixture.reshape(
                steps, group, 128
            )
    mixture = grad_mix[...].reshape(tile, width)
    mixture_all[here, :] = mixture
    middle = rows + dot_nn(mixture, w_out[...])
    hat, scale = normalise(middle)
    second = (hat * norm_ref[2:3] + norm_ref[3:4]).astype(bf16)
    second_all[here, :] = second
    after = middle + feed_forward(second, w_up, w_down, active_all.at[here, :], slope)
    result_ref[...] = after.reshape(result_ref.shape)

    slot = lax.broadcasted_iota(jnp.int32, rows_ref.shape, 0)
    live = (slot < length).astype(f32)
    grad_after = (cotangent_ref[...].astype(f32) * live).reshape(tile, width)
    branch = grad_after.astype(bf16)
    branch_all[here, :] = branch
    hidden_backward(branch, w_down, slope, hidden_all.at[here, :])
    grad_second = dot_nt(hidden_all[here, :], w_up[...])
    hat, scale = normalise(middle)
    grad_rows, gain, shift = norm_backward(hat, scale, norm_ref[2:3], grad_second)
    g_norm[2] += gain
    g_norm[3] += shift
    grad_middle = grad_after + grad_rows
    attn = grad_middle.astype(bf16)
    attn_all[here, :] = attn
    grad_mix[...] = dot_nt(attn, w_out[...]).astype(bf16).reshape(grad_mix.shape)
    for place in range(0, patches, group):
        for pair in range(HEADS // 2):
            grads = attend_backward(
                *[cut(packed, part, place, pair) for part in range(3)],
                cut(grad_mix, 0, place, pair),
                [weights_buf[place // group, 2 * pair + which] for which in range(2)],
                low_half,
            )
            for part in range(3):
                start = part * width + 128 * pair
                packed[:, place : place + group, start : start + 128] = grads[part].reshape(
                    steps, group, 128
                )
    grad_packed = packed[...].reshape(tile, 3 * width)
    packed_all[here, :] = grad_packed
    grad_first = dot_nt(grad_packed, w_qkv[...])
    hat, scale = normalise(rows)
    grad_rows, gain, shift = norm_backward(hat, scale, norm_ref[0:1], grad_first)
    g_norm[0] += gain
    g_norm[1] += shift
    before_ref[...] = (grad_middle + grad_rows).reshape(before_ref.shape)

    @pl.when(step == pl.num_programs(0) - 1)
    def _():
        weight_grads(
            first_all, packed_all, mixture_all, attn_all, second_all, hidden_all, active_all,
            branch_all, storing(plan, 1, outs, g_norm),
        )


def temporal_block(plan, length, rows, cotangent, weights, norms):
    grad_specs, grad_shapes = grad_outputs(plan, weights)
    steps, patches, width = rows.shape
    tokens = steps * patches
    hidden = weights[2].shape[1]
    part = TEMPORAL_TILE // steps
    slab = pl.BlockSpec((steps, part, width), lambda i: (0, i, 0))
    return pl.pallas_call(
        partial(temporal_kernel, plan),
        grid=(patches // part,),
        in_specs=[pl.BlockSpec(memory_space=pltpu.SMEM), slab, slab]
        + [whole(w.shape) for w in weights]
        + [whole(norms.shape)],
        out_specs=[slab, slab] + grad_specs + [whole((4, 8, width))],
        out_shape=[
            jax.ShapeDtypeStruct(rows.shape, f32),
            jax.ShapeDtypeStruct(rows.shape, f32),
        ]
        + grad_shapes
        + [jax.ShapeDtypeStruct((4, 8, width), f32)],
        scratch_shapes=[
            pltpu.VMEM((steps, part, 3 * width), bf16),
            pltpu.VMEM((TEMPORAL_TILE, hidden), bf16),
            pltpu.VMEM((part // PATCH_GROUP, HEADS, steps * PATCH_GROUP, steps * PATCH_GROUP), bf16),
            pltpu.VMEM((steps, part, width), bf16),
            pltpu.VMEM((tokens, width), bf16),
            pltpu.VMEM((tokens, 3 * width), bf16),
            pltpu.VMEM((tokens, width), bf16),
            pltpu.VMEM((tokens, width), bf16),
            pltpu.VMEM((tokens, width), bf16),
            pltpu.VMEM((tokens, hidden), bf16),
            pltpu.VMEM((tokens, hidden), bf16),
            pltpu.VMEM((tokens, width), bf16),
        ],
        compiler_params=pltpu.CompilerParams(vmem_limit_bytes=62 * MIB),
    )(length, rows, cotangent, *weights, norms)


def spatial_backward_kernel(
    plan, x_ref, grad_ref, packed_ref, weights_ref, middle_ref, slope_ref, mixture_all, active_all,
    w_qkv, w_out, w_up, w_down, norm_ref,
    before_ref, *refs,
):
    outs, g_norm = refs[:-8], refs[-8]
    grad_mix, first_all, packed_all, attn_all, second_all, hidden_all, branch_all = refs[-7:]
    step = pl.program_id(0)
    tile, width = x_ref.shape
    here = pl.ds(pl.multiple_of(step * tile, tile), tile)

    @pl.when(step == 0)
    def _():
        g_norm[...] = jnp.zeros_like(g_norm)

    grad_after = grad_ref[...]
    branch = grad_after.astype(bf16)
    branch_all[here, :] = branch
    hidden_backward(branch, w_down, slope_ref, hidden_all.at[here, :])
    grad_second = dot_nt(hidden_all[here, :], w_up[...])
    hat, scale = normalise(middle_ref[...])
    second_all[here, :] = (hat * norm_ref[2:3] + norm_ref[3:4]).astype(bf16)
    grad_rows, gain, shift = norm_backward(hat, scale, norm_ref[2:3], grad_second)
    g_norm[2] += gain
    g_norm[3] += shift
    grad_middle = grad_after + grad_rows
    attn = grad_middle.astype(bf16)
    attn_all[here, :] = attn
    grad_mix[...] = dot_nt(attn, w_out[...]).astype(bf16)
    frame = weights_ref.shape[2]
    low_half = lane_halves(frame)
    for item in range(weights_ref.shape[0]):
        span = slice(item * frame, (item + 1) * frame)
        there = pl.ds(pl.multiple_of(step * tile + item * frame, frame), frame)
        for pair in range(HEADS // 2):
            grads = attend_backward(
                *[
                    packed_ref[span, part * width + 128 * pair : part * width + 128 * (pair + 1)]
                    for part in range(3)
                ],
                grad_mix[span, 128 * pair : 128 * (pair + 1)],
                [weights_ref[item, 2 * pair + which] for which in range(2)],
                low_half,
            )
            for part in range(3):
                start = part * width + 128 * pair
                packed_all[there, start : start + 128] = grads[part]
    grad_first = dot_nt(packed_all[here, :], w_qkv[...])
    hat, scale = normalise(x_ref[...].astype(f32))
    first_all[here, :] = (hat * norm_ref[0:1] + norm_ref[1:2]).astype(bf16)
    grad_rows, gain, shift = norm_backward(hat, scale, norm_ref[0:1], grad_first)
    g_norm[0] += gain
    g_norm[1] += shift
    before_ref[...] = grad_middle + grad_rows

    @pl.when(step == pl.num_programs(0) - 1)
    def _():
        weight_grads(
            first_all, packed_all, mixture_all, attn_all, second_all, hidden_all, active_all,
            branch_all, storing(plan, 0, outs, g_norm),
        )


def spatial_backward(plan, x, grad, kept, weights, norms):
    packed, soft, mixture, middle, active, slope = kept
    grad_specs, grad_shapes = grad_outputs(plan, weights)
    tokens, width = x.shape
    hidden = weights[2].shape[1]
    frame = soft.shape[2]
    tile = SPATIAL_TILE
    return pl.pallas_call(
        partial(spatial_backward_kernel, plan),
        grid=(tokens // tile,),
        in_specs=[
            tiles(tile, width),
            tiles(tile, width),
            tiles(tile, 3 * width),
            tiles(tile // frame, HEADS, frame, frame),
            tiles(tile, width),
            tiles(tile, hidden),
            whole(mixture.shape),
            whole(active.shape),
        ]
        + [whole(w.shape) for w in weights]
        + [whole(norms.shape)],
        out_specs=[tiles(tile, width)]
        + grad_specs
        + [whole((4, 8, width))],
        out_shape=[jax.ShapeDtypeStruct((tokens, width), f32)]
        + grad_shapes
        + [jax.ShapeDtypeStruct((4, 8, width), f32)],
        scratch_shapes=[
            pltpu.VMEM((tile, width), bf16),
            pltpu.VMEM((tokens, width), bf16),
            pltpu.VMEM((tokens, 3 * width), bf16),
            pltpu.VMEM((tokens, width), bf16),
            pltpu.VMEM((tokens, width), bf16),
            pltpu.VMEM((tokens, hidden), bf16),
            pltpu.VMEM((tokens, width), bf16),
        ],
        compiler_params=pltpu.CompilerParams(vmem_limit_bytes=62 * MIB),
    )(x, grad, packed, soft, middle, slope, mixture, active, *weights, norms)


def unpack(flat_weights, model_width, hidden_width):
    cut_qkv = 3 * model_width * model_width
    cut_out = 4 * model_width * model_width
    cut_up = cut_out + model_width * hidden_width
    return (
        flat_weights[:cut_qkv].reshape(model_width, 3 * model_width),
        flat_weights[cut_qkv:cut_out].reshape(model_width, model_width),
        flat_weights[cut_out:cut_up].reshape(model_width, hidden_width),
        flat_weights[cut_up:].reshape(hidden_width, model_width),
    )


def adamw(param_value, moment, second, grad_total, step_value, rate, decay_rate):
    moment_next = beta_first * moment + (1.0 - beta_first) * grad_total
    second_next = beta_second * second + (1.0 - beta_second) * grad_total * grad_total
    moment_hat = moment_next / (1.0 - beta_first**step_value)
    second_hat = second_next / (1.0 - beta_second**step_value)
    param_next = param_value - rate * (
        moment_hat / (jnp.sqrt(second_hat) + adam_floor) + decay_rate * param_value
    )
    return (param_next, moment_next, second_next)


def on_device(
    clip_tokens,
    cotangent,
    lengths,
    params,
    param_moment,
    param_second,
    norm_par,
    norm_moment,
    norm_second,
):
    clip_count, step_slots, patch_count, model_width = clip_tokens.shape
    shards = lax.axis_size("dp")
    plan = shard_plan(shards, model_width, FF) if shards == 32 else None
    if plan is None:
        gathered = lax.all_gather(params.astype(bf16), "dp", axis=1, tiled=True)
        norm_whole = lax.all_gather(norm_par.astype(bf16), "dp", axis=0, tiled=True)
        norm_table = norm_whole.astype(f32).reshape(2, 4, model_width)
        spatial_weights = unpack(gathered[0], model_width, FF)
        temporal_weights = unpack(gathered[1], model_width, FF)
    else:
        spatial_weights, temporal_weights, norm_table = gather_weights(
            plan, params, norm_par, model_width, FF
        )
    x = clip_tokens.reshape(-1, model_width)
    *kept, after = spatial_forward(x, spatial_weights, norm_table[0], patch_count)
    result, grad_after, *temporal_grads, temporal_norm = temporal_block(
        plan,
        lengths,
        after.reshape(step_slots, patch_count, model_width),
        cotangent.reshape(step_slots, patch_count, model_width),
        temporal_weights,
        norm_table[1],
    )
    grad_before, *spatial_grads, spatial_norm = spatial_backward(
        plan, x, grad_after.reshape(-1, model_width), kept, spatial_weights, norm_table[0]
    )

    if plan is None:

        def scatter(grads):
            flat = jnp.concatenate([g.reshape(-1) for g in grads])
            return lax.psum_scatter(flat, "dp", scatter_dimension=0, tiled=True).astype(f32)

        weight_sum = jnp.stack([scatter(spatial_grads), scatter(temporal_grads)])
        norm_grad = jnp.stack([spatial_norm, temporal_norm]).sum(axis=2).reshape(-1)
        norm_sum = lax.psum_scatter(norm_grad, "dp", scatter_dimension=0, tiled=True)
    else:
        weight_sum, norm_sum = scatter_grads(plan, (spatial_grads[0], temporal_grads[0]))
    step_value = float(STEP)
    new_params, new_moment, new_second = adamw(
        params, param_moment, param_second, weight_sum, step_value, learn_rate, weight_decay
    )
    new_norm, new_norm_moment, new_norm_second = adamw(
        norm_par, norm_moment, norm_second, norm_sum, step_value, norm_rate, 0.0
    )
    return (
        result.reshape(clip_tokens.shape),
        grad_before.reshape(clip_tokens.shape),
        new_params,
        new_moment,
        new_second,
        new_params.astype(bf16),
        new_norm,
        new_norm_moment,
        new_norm_second,
    )


def solution(mesh):
    placed = (
        P("dp", None, None, None),
        P("dp", None, None, None),
        P("dp"),
        P(None, "dp"),
        P(None, "dp"),
        P(None, "dp"),
        P("dp"),
        P("dp"),
        P("dp"),
    )
    return jax.shard_map(
        on_device,
        mesh=mesh,
        in_specs=placed,
        out_specs=(
            P("dp", None, None, None),
            P("dp", None, None, None),
            P(None, "dp"),
            P(None, "dp"),
            P(None, "dp"),
            P(None, "dp"),
            P("dp"),
            P("dp"),
            P("dp"),
        ),
        check_vma=False,
    )
```

```python
from functools import partial

import jax
import jax.numpy as jnp
from jax import lax
from jax.experimental import pallas as pl
from jax.experimental.pallas import tpu as pltpu
from jax.sharding import PartitionSpec as P

HEADS = 8
HEAD_DIM = 64
FF = 2048
STEP = 7

norm_epsilon = 1e-05
beta_first = 0.9
beta_second = 0.999
learn_rate = 0.05
norm_rate = 0.5
weight_decay = 0.1
adam_floor = 1e-08
masked_score = -1e30

bf16 = jnp.bfloat16
f32 = jnp.float32
MIB = 2**20

SPATIAL_TILE = 256
TEMPORAL_TILE = 256
PATCH_GROUP = 16


def dot_nn(left, right):
    return lax.dot_general(left, right, (((1,), (0,)), ((), ())), preferred_element_type=f32)


def dot_nt(left, right):
    return lax.dot_general(left, right, (((1,), (1,)), ((), ())), preferred_element_type=f32)


def dot_tn(left, right):
    return lax.dot_general(left, right, (((0,), (0,)), ((), ())), preferred_element_type=f32)


def normalise(rows):
    center = rows - jnp.mean(rows, axis=-1, keepdims=True)
    spread = jnp.mean(center * center, axis=-1, keepdims=True)
    scale = lax.rsqrt(spread + norm_epsilon)
    return center * scale, scale


def fold_rows(rows):
    return jnp.sum(rows.reshape(-1, 8, rows.shape[-1]), axis=0)


def norm_backward(hat, scale, gain, grad):
    weighted = grad * gain
    mean_first = jnp.mean(weighted, axis=-1, keepdims=True)
    mean_second = jnp.mean(weighted * hat, axis=-1, keepdims=True)
    grad_rows = scale * (weighted - mean_first - hat * mean_second)
    return grad_rows, fold_rows(grad * hat), fold_rows(grad)


def gelu_pair(value):
    cumulative = 0.5 + 0.5 * lax.erf(value * 0.7071067811865476)
    density = jnp.exp(-0.5 * value * value) * 0.3989422804014327
    return value * cumulative, cumulative + value * density


def lane_halves(count):
    lane = lax.broadcasted_iota(jnp.int32, (count, 2 * HEAD_DIM), 1)
    return lane < HEAD_DIM


def two_heads(pair, low_half):
    zero = jnp.zeros_like(pair)
    return jnp.concatenate([jnp.where(low_half, pair, zero), jnp.where(low_half, zero, pair)], axis=0)


def own_columns(stacked, low_half):
    rows = stacked.shape[0] // 2
    return jnp.where(low_half, stacked[:rows], stacked[rows:]).astype(bf16)


ROW_CHUNK = 64


def attend(units, scores, soft, low_half, bias):
    rows, double = scores.shape[1:]
    keys = double // 2
    for unit, (query, key, value, put) in enumerate(units):
        scaled = query() * jnp.asarray(HEAD_DIM**-0.5, bf16)
        scores[unit] = dot_nt(scaled, two_heads(key(), low_half))
    for unit in range(len(units)):
        for start in range(0, rows, ROW_CHUNK):
            span = slice(start, start + ROW_CHUNK)
            for half in range(2):
                columns = slice(half * keys, (half + 1) * keys)
                part = scores[unit, span, columns]
                if bias is not None:
                    part = part + bias[span]
                powers = jnp.exp(part - jnp.max(part, axis=-1, keepdims=True))
                part = powers * (1.0 / jnp.sum(powers, axis=-1, keepdims=True))
                soft[unit, span, columns] = part.astype(bf16)
    for unit, (query, key, value, put) in enumerate(units):
        put(dot_nn(soft[unit], two_heads(value(), low_half)).astype(bf16))


def attend_backward(units, scores, soft, grad_scores, low_half):
    rows, double = scores.shape[1:]
    keys = double // 2
    scale = jnp.asarray(HEAD_DIM**-0.5, bf16)
    for unit, (query, key, value, grad, put) in enumerate(units):
        scores[unit] = dot_nt(grad(), two_heads(value(), low_half))
    for unit in range(len(units)):
        for start in range(0, rows, ROW_CHUNK):
            span = slice(start, start + ROW_CHUNK)
            for half in range(2):
                columns = slice(half * keys, (half + 1) * keys)
                wide = soft[unit, span, columns].astype(f32)
                product = scores[unit, span, columns] * wide
                inner = jnp.sum(product, axis=-1, keepdims=True)
                grad_scores[unit, span, columns] = (product - wide * inner).astype(bf16)
    for unit, (query, key, value, grad, put) in enumerate(units):
        grad_value = own_columns(dot_tn(soft[unit], grad()), low_half)
        grad_query = dot_nn(grad_scores[unit], two_heads(key() * scale, low_half)).astype(bf16)
        grad_key = own_columns(dot_tn(grad_scores[unit], query() * scale), low_half)
        put(grad_query, grad_key, grad_value)


def feed_forward(second, w_up, w_down, active_ref, slope_ref, chunk=512):
    hidden = w_up.shape[1]
    for start in range(0, hidden, chunk):
        active, slope = gelu_pair(dot_nn(second, w_up[:, start : start + chunk]))
        active_ref[:, start : start + chunk] = active.astype(bf16)
        slope_ref[:, start : start + chunk] = slope.astype(bf16)
    return dot_nn(active_ref[...], w_down[...])


def hidden_backward(branch, w_down, slope_ref, hidden_ref, chunk=512):
    hidden = w_down.shape[0]
    for start in range(0, hidden, chunk):
        grad = dot_nt(branch, w_down[start : start + chunk, :])
        slope = slope_ref[:, start : start + chunk].astype(f32)
        hidden_ref[:, start : start + chunk] = (grad * slope).astype(bf16)


def spatial_forward_kernel(plan, x_ref, *refs):
    step, last = pl.program_id(1), pl.num_programs(1) - 1
    opening = pl.program_id(0) == 0
    if plan is None:
        w_qkv, w_out, w_up, w_down, norm_ref = refs[:5]
        refs = refs[5:]
        packed_ref, weights_ref, mixture_ref, middle_ref, active_ref, slope_ref, after_ref = refs[:7]
        scores, mixture_all = refs[7:]
    else:
        shard_ref, norm_par_ref = refs[:2]
        refs = refs[2:]
        packed_ref, weights_ref, mixture_ref, middle_ref, active_ref, slope_ref, after_ref = refs[:7]
        held_out, held_next, norm_ref = refs[7:10]
        scores, mixture_all, w_qkv, w_out, w_up, w_down, held, staged, send, recv, local = refs[10:]
        matrices = (w_qkv, w_out, w_up, w_down)
        place = Place(lax.axis_index("dp"))
        now = Gather(place, held, send.at[0], recv.at[0])
        later = Gather(place, held_next, send.at[1], recv.at[1])
        keep = pltpu.make_async_copy(held, held_out, local.at[0])

        def gathered(*planes):
            for q in planes:
                now.finish(q)
            assemble(plan, held, matrices, planes)
            assemble_norms(len(plan), held, norm_ref, planes)

        @pl.when(opening & (step == 0))
        def _():
            enter(place)
            load_shard(plan, place.me, shard_ref.at[0], norm_par_ref, held.at[place.z, place.y, place.x, place.c])
            now.start_z()
            load_shard(plan, place.me, shard_ref.at[1], norm_par_ref, staged)
            copy = pltpu.make_async_copy(
                staged, held_next.at[place.z, place.y, place.x, place.c], local.at[1]
            )
            copy.start()
            copy.wait()
            now.begin_first(0)
            now.begin_second(0)
            for q in range(1, 4):
                now.begin_first(q)
            now.begin_third(0)
            later.start_z()
            gathered(0)

        @pl.when(opening & (step == 1))
        def _():
            now.begin_second(1)
            now.begin_second(2)

        @pl.when(opening & (step == 2))
        def _():
            now.begin_second(3)

        @pl.when(opening & (step == 3))
        def _():
            now.begin_third(1)
            for q in range(4):
                later.begin_first(q)

        @pl.when(opening & (step == 4))
        def _():
            now.begin_third(2)
            later.begin_second(0)

        @pl.when(opening & (step == 6))
        def _():
            now.begin_third(3)
            later.begin_second(1)

        @pl.when(jnp.logical_not(opening) & (step == 0))
        def _():
            later.begin_second(2)
            later.begin_second(3)
            gathered(1, 2, 3)
            keep.start()

        for q in range(4):

            @pl.when(jnp.logical_not(opening) & (step == 2 * q + 1))
            def _(q=q):
                later.begin_third(q)

    tile, width = x_ref.shape
    here = pl.ds(pl.multiple_of(step * tile, tile), tile)

    @pl.when(opening)
    def _():
        hat, _ = normalise(x_ref[...].astype(f32))
        first = (hat * norm_ref[0:1] + norm_ref[1:2]).astype(bf16)
        for start in range(0, 3 * width, 512):
            packed_ref[:, start : start + 512] = dot_nn(first, w_qkv[:, start : start + 512]).astype(bf16)
        frame = weights_ref.shape[2]
        low_half = lane_halves(frame)
        for item in range(weights_ref.shape[0]):
            span = slice(item * frame, (item + 1) * frame)
            units = []
            for pair in range(HEADS // 2):

                def cut(part, pair=pair, span=span):
                    start = part * width + 128 * pair
                    return packed_ref[span, start : start + 128]

                def put(value, pair=pair, span=span):
                    mixture_ref[span, 128 * pair : 128 * (pair + 1)] = value

                units.append((partial(cut, 0), partial(cut, 1), partial(cut, 2), put))
            attend(units, scores, weights_ref.at[item], low_half, None)
        mixture_all[here, :] = mixture_ref[...]

    @pl.when(jnp.logical_not(opening))
    def _():
        middle = x_ref[...].astype(f32) + dot_nn(mixture_all[here, :], w_out[...])
        middle_ref[...] = middle
        hat, _ = normalise(middle)
        second = (hat * norm_ref[2:3] + norm_ref[3:4]).astype(bf16)
        after_ref[...] = middle + feed_forward(second, w_up, w_down, active_ref, slope_ref)

    if plan is not None:

        @pl.when(jnp.logical_not(opening) & (step == last))
        def _():
            for q in range(4):
                later.finish(q)
            keep.wait()
            now.drain()
            later.drain()


def whole(shape):
    return pl.BlockSpec(shape, lambda *_: (0,) * len(shape), pipeline_mode=pl.Buffered(1))


def tiles(tile, *rest):
    return pl.BlockSpec((tile, *rest), lambda i: (i,) + (0,) * len(rest))


def spatial_forward(plan, x, sources, frame, hidden):
    tokens, width = x.shape
    tile = SPATIAL_TILE
    frames = tile // frame
    count = tokens // tile

    def opening(*rest):
        return pl.BlockSpec(rest, lambda p, i: (i + p * (count - 1 - i),) + (0,) * (len(rest) - 1))

    def closing(*rest):
        return pl.BlockSpec(rest, lambda p, i: (i * p,) + (0,) * (len(rest) - 1))

    out_specs = [
        opening(tile, 3 * width),
        opening(frames, HEADS // 2, frame, 2 * frame),
        opening(tile, width),
        closing(tile, width),
        closing(tile, hidden),
        closing(tile, hidden),
        closing(tile, width),
    ]
    out_shape = [
        jax.ShapeDtypeStruct((tokens, 3 * width), bf16),
        jax.ShapeDtypeStruct((tokens // frame, HEADS // 2, frame, 2 * frame), bf16),
        jax.ShapeDtypeStruct((tokens, width), bf16),
        jax.ShapeDtypeStruct((tokens, width), f32),
        jax.ShapeDtypeStruct((tokens, hidden), bf16),
        jax.ShapeDtypeStruct((tokens, hidden), bf16),
        jax.ShapeDtypeStruct((tokens, width), f32),
    ]
    scratch = [pltpu.VMEM((HEADS // 2, frame, 2 * frame), f32), pltpu.VMEM((tokens, width), bf16)]
    params = dict(vmem_limit_bytes=60 * MIB)
    if plan is not None:
        held = (4, 2, 2, 2, SHARD, LANES)
        out_specs += [pl.BlockSpec(memory_space=pl.ANY)] * 2 + [whole((8, width))]
        out_shape += [jax.ShapeDtypeStruct(held, bf16)] * 2 + [jax.ShapeDtypeStruct((8, width), f32)]
        scratch += [pltpu.VMEM(shape, bf16) for shape in matrix_shapes(width, hidden)]
        scratch += [
            pltpu.VMEM(held, bf16),
            pltpu.VMEM((SHARD, LANES), bf16),
            pltpu.SemaphoreType.DMA((2, 6, 4)),
            pltpu.SemaphoreType.DMA((2, 6, 4)),
            pltpu.SemaphoreType.DMA((2,)),
        ]
        params |= dict(collective_id=0, has_side_effects=True)
    return pl.pallas_call(
        partial(spatial_forward_kernel, plan),
        grid=(2, count),
        in_specs=[pl.BlockSpec((tile, width), lambda p, i: (i, 0))] + [whole(a.shape) for a in sources],
        out_specs=out_specs,
        out_shape=out_shape,
        scratch_shapes=scratch,
        compiler_params=pltpu.CompilerParams(**params),
    )(x, *sources)


MESH_IDS = pl.DeviceIdType.MESH
LANES = 128
ROW_TILE = 16


def matrix_shapes(width, hidden):
    return ((width, 3 * width), (width, width), (width, hidden), (hidden, width))


def shard_plan(shards, width, hidden):
    plan = []
    base = 0
    regions = []
    for index, (rows, columns) in enumerate(matrix_shapes(width, hidden)):
        regions.append((index, base, rows, columns))
        base += rows * columns
    if base % shards:
        return None
    size = base // shards
    for device in range(shards):
        low, high = device * size, (device + 1) * size
        halves = ([], [])
        for index, start, rows, columns in regions:
            first, last = max(low, start), min(high, start + rows * columns)
            if first >= last:
                continue
            if (first - start) % columns or (last - start) % columns:
                return None
            row, count = (first - start) // columns, (last - first) // columns
            if row % ROW_TILE or count % ROW_TILE:
                return None
            stride = columns // LANES
            for block in range(stride):
                halves[2 * block // stride].append(
                    (index, row, count, block, (first - low) // LANES + block, stride)
                )
        place = 0
        entries = []
        for item in halves[0] + halves[1]:
            entries.append(item + (place,))
            place += item[2]
        plan.append(entries)
    return plan


def by_pattern(plan):
    groups = {}
    for device, entries in enumerate(plan):
        layout = tuple((e[2], e[4], e[5], e[6]) for e in entries)
        ranges = groups.setdefault(layout, [])
        if ranges and ranges[-1][1] == device:
            ranges[-1][1] = device + 1
        else:
            ranges.append([device, device + 1])
    return list(groups.items())


def on_pattern(plan, me, body):
    for layout, ranges in by_pattern(plan):
        inside = None
        for low, high in ranges:
            test = (me >= low) & (me < high)
            inside = test if inside is None else inside | test

        @pl.when(inside)
        def _(layout=layout):
            body(layout)


class Place:
    def __init__(self, me):
        self.me = me
        self.c = lax.rem(me, 2)
        self.x = lax.rem(me // 2, 2)
        self.y = lax.rem(me // 4, 2)
        self.z = me // 8

    def device(self, z, y, x, c):
        return ((z * 2 + y) * 2 + x) * 2 + c

    @property
    def sibling(self):
        return self.device(self.z, self.y, self.x, 1 - self.c)

    @property
    def across_x(self):
        return self.device(self.z, self.y, 1 - self.x, self.c)

    @property
    def across_y(self):
        return self.device(self.z, 1 - self.y, self.x, self.c)

    def plane(self, z):
        return self.device(z, self.y, self.x, self.c)


def remote(src, dst, send, recv, device):
    return pltpu.make_async_remote_copy(
        src_ref=src, dst_ref=dst, send_sem=send, recv_sem=recv, device_id=(device,), device_id_type=MESH_IDS
    )


def enter(place):
    barrier = pltpu.get_barrier_semaphore()
    partners = [place.sibling, place.across_x, place.across_y]
    partners += [place.plane(lax.rem(place.z + k, 4)) for k in range(1, 4)]
    for device in partners:
        pl.semaphore_signal(barrier, inc=1, device_id=(device,), device_id_type=MESH_IDS)
    pl.semaphore_wait(barrier, len(partners))


HALF = 384
SHARD = 784


class Gather:
    SEMS = 9

    def __init__(self, place, held, send, recv):
        self.p, self.held, self.send, self.recv = place, held, send, recv

    def along_z(self, k):
        p = self.p
        here = self.held.at[p.z, p.y, p.x, p.c]
        return remote(here, here, self.send.at[0, k - 1], self.recv.at[0, p.z], p.plane(lax.rem(p.z + k, 4)))

    def start_z(self):
        for k in range(1, 4):
            self.along_z(k).start()

    def wait_z(self, q):
        p = self.p

        @pl.when(q != p.z)
        def _():
            there = self.held.at[q, p.y, p.x, p.c]
            remote(there, there, self.send.at[0, 0], self.recv.at[0, q], p.me).wait_recv()

    def first(self, q):
        p, h = self.p, self.held
        a = h.at[q, p.y, p.x, p.c, pl.ds(0, HALF)]
        b = h.at[q, p.y, p.x, p.c, pl.ds(HALF, SHARD - HALF)]
        return (
            remote(a, a, self.send.at[1, q], self.recv.at[1, q], p.across_x),
            remote(b, b, self.send.at[2, q], self.recv.at[2, q], p.across_y),
        )

    def second(self, q):
        p, h = self.p, self.held
        a = h.at[q, p.y, :, p.c, pl.ds(0, HALF)]
        b = h.at[q, :, p.x, p.c, pl.ds(HALF, SHARD - HALF)]
        return (
            remote(a, a, self.send.at[3, q], self.recv.at[3, q], p.across_y),
            remote(b, b, self.send.at[4, q], self.recv.at[4, q], p.across_x),
        )

    def third(self, q):
        p, h = self.p, self.held
        a = h.at[q, :, :, p.c]
        return (remote(a, a, self.send.at[5, q], self.recv.at[5, q], p.sibling),)

    def begin_first(self, q):
        self.wait_z(q)
        for copy in self.first(q):
            copy.start()

    def begin_second(self, q):
        for copy in self.first(q):
            copy.wait_recv()
        for copy in self.second(q):
            copy.start()

    def begin_third(self, q):
        for copy in self.second(q):
            copy.wait_recv()
        for copy in self.third(q):
            copy.start()

    def finish(self, q):
        for copy in self.third(q):
            copy.wait_recv()

    def drain(self):
        for k in range(1, 4):
            self.along_z(k).wait_send()
        for q in range(4):
            for copy in self.first(q) + self.second(q) + self.third(q):
                copy.wait_send()


def load_shard(plan, me, shard_ref, norm_ref, held_here):
    def body(layout):
        for count, flat, stride, place in layout:
            held_here[pl.ds(place, count), :] = shard_ref[pl.ds(flat, count, stride), :].astype(bf16)

    on_pattern(plan, me, body)
    held_here[SHARD - ROW_TILE :, :] = jnp.broadcast_to(norm_ref[...], (ROW_TILE, LANES)).astype(bf16)


def coordinates(device):
    return device // 8, device // 4 % 2, device // 2 % 2, device % 2


def assemble(plan, held, outs, planes):
    for device, entries in enumerate(plan):
        z, y, x, c = coordinates(device)
        if z not in planes:
            continue
        for index, row, count, block, _, _, place in entries:
            outs[index][row : row + count, LANES * block : LANES * (block + 1)] = held[
                z, y, x, c, place : place + count, :
            ]


def assemble_norms(shards, held, norm_out, planes):
    per_row = norm_out.shape[1] // LANES
    for device in range(shards):
        z, y, x, c = coordinates(device)
        if z not in planes:
            continue
        row, column = device // per_row, device % per_row
        norm_out[row : row + 1, LANES * column : LANES * (column + 1)] = held[
            z, y, x, c, SHARD - ROW_TILE : SHARD, :
        ].astype(f32)[0:1]


class Scatter:
    def __init__(self, place, own, r1, r2a, r2b, r3, r4, send, recv):
        self.p, self.own = place, own
        self.r1, self.r2a, self.r2b, self.r3, self.r4 = r1, r2a, r2b, r3, r4
        self.send, self.recv = send, recv

    def first(self, q):
        p = self.p
        return (
            remote(
                self.own.at[q, :, :, 1 - p.c], self.r1.at[q], self.send.at[0, q], self.recv.at[0, q], p.sibling
            ),
        )

    def second(self, q):
        p = self.p
        low, high = pl.ds(0, HALF), pl.ds(HALF, SHARD - HALF)
        return (
            remote(
                self.r1.at[q, :, 1 - p.x, low], self.r2a.at[q], self.send.at[1, q], self.recv.at[1, q], p.across_x
            ),
            remote(
                self.r1.at[q, 1 - p.y, :, high], self.r2b.at[q], self.send.at[2, q], self.recv.at[2, q], p.across_y
            ),
        )

    def third(self, q):
        p = self.p
        low, high = pl.ds(0, HALF), pl.ds(HALF, SHARD - HALF)
        return (
            remote(
                self.r2a.at[q, 1 - p.y], self.r3.at[q, low], self.send.at[3, q], self.recv.at[3, q], p.across_y
            ),
            remote(
                self.r2b.at[q, 1 - p.x], self.r3.at[q, high], self.send.at[4, q], self.recv.at[4, q], p.across_x
            ),
        )

    def along_z(self, q):
        p = self.p
        return remote(self.r3.at[q], self.r4.at[p.z], self.send.at[5, q], self.recv.at[5, p.z], p.plane(q))

    def begin_first(self, q):
        for copy in self.first(q):
            copy.start()

    def begin_second(self, q, mine):
        for copy in self.first(q):
            copy.wait_recv()
        for y in range(2):
            for x in range(2):
                self.r1[q, y, x] = (self.r1[q, y, x].astype(f32) + mine[y, x].astype(f32)).astype(bf16)
        for copy in self.second(q):
            copy.start()

    def begin_third(self, q):
        p = self.p
        for copy in self.second(q):
            copy.wait_recv()
        low, high = pl.ds(0, HALF), pl.ds(HALF, SHARD - HALF)
        for k in range(2):
            self.r2a[q, k] = (self.r2a[q, k].astype(f32) + self.r1[q, k, p.x, low].astype(f32)).astype(bf16)
            self.r2b[q, k] = (self.r2b[q, k].astype(f32) + self.r1[q, p.y, k, high].astype(f32)).astype(bf16)
        for copy in self.third(q):
            copy.start()

    def begin_z(self, q):
        p = self.p
        for copy in self.third(q):
            copy.wait_recv()
        low, high = pl.ds(0, HALF), pl.ds(HALF, SHARD - HALF)
        self.r3[q, low] = (self.r3[q, low].astype(f32) + self.r2a[q, p.y].astype(f32)).astype(bf16)
        self.r3[q, high] = (self.r3[q, high].astype(f32) + self.r2b[q, p.x].astype(f32)).astype(bf16)

        @pl.when(q != p.z)
        def _():
            self.along_z(q).start()

    def finish(self, total):
        p = self.p
        for k in range(1, 4):
            z = lax.rem(p.z + k, 4)
            remote(self.r3.at[0], self.r4.at[z], self.send.at[5, 0], self.recv.at[5, z], p.me).wait_recv()
        total[...] = self.r3[p.z].astype(f32)
        for k in range(1, 4):
            total[...] += self.r4[lax.rem(p.z + k, 4)].astype(f32)

    def drain(self):
        for q in range(4):
            for copy in self.first(q) + self.second(q) + self.third(q):
                copy.wait_send()

            @pl.when(q != self.p.z)
            def _(q=q):
                self.along_z(q).wait_send()


SCATTER_SCRATCH = [
    pltpu.VMEM((4, 2, 2, SHARD, LANES), bf16),
    pltpu.VMEM((4, 2, HALF, LANES), bf16),
    pltpu.VMEM((4, 2, SHARD - HALF, LANES), bf16),
    pltpu.VMEM((4, SHARD, LANES), bf16),
    pltpu.VMEM((4, SHARD, LANES), bf16),
    pltpu.SemaphoreType.DMA((6, 4)),
    pltpu.SemaphoreType.DMA((6, 4)),
]


def unload_shard(plan, me, total, flat_ref):
    def body(layout):
        for count, flat, stride, place in layout:
            flat_ref[pl.ds(flat, count, stride), :] = total[pl.ds(place, count), :]

    on_pattern(plan, me, body)


def scatter_kernel(plan, g0, g1, flat0, flat1, norm_out, total, mine, load, *rest):
    place = Place(lax.axis_index("dp"))
    enter(place)
    count = len(SCATTER_SCRATCH)
    scatters = []
    for b, own in ((1, g1), (0, g0)):
        s = Scatter(place, own, *rest[b * count : (b + 1) * count])
        scatters.append((b, s, own))
    for b, s, own in scatters:
        for q in range(4):
            s.begin_first(q)
    for b, s, own in scatters:
        for q in range(4):
            copy = pltpu.make_async_copy(own.at[q, :, :, place.c], mine.at[b, q], load.at[b, q])
            copy.start()
        for q in range(4):
            pltpu.make_async_copy(own.at[q, :, :, place.c], mine.at[b, q], load.at[b, q]).wait()
            s.begin_second(q, mine.at[b, q])
        for q in range(4):
            s.begin_third(q)
        for q in range(4):
            s.begin_z(q)
    for b, s, own in scatters:
        s.finish(total)
        unload_shard(plan, place.me, total, (flat0, flat1)[b])
        if b == 1:
            norm_out[...] = total[SHARD - ROW_TILE : SHARD - ROW_TILE + 8]
        else:
            norm_out[...] += total[SHARD - ROW_TILE : SHARD - ROW_TILE + 8]
    for b, s, own in scatters:
        s.drain()


def scatter_grads(plan, grads):
    vmem = pl.BlockSpec(memory_space=pltpu.VMEM)
    rows = SHARD - ROW_TILE
    flat0, flat1, norm = pl.pallas_call(
        partial(scatter_kernel, plan),
        in_specs=[pl.BlockSpec(memory_space=pl.ANY)] * 2,
        out_specs=[vmem] * 3,
        out_shape=[
            jax.ShapeDtypeStruct((rows, LANES), f32),
            jax.ShapeDtypeStruct((rows, LANES), f32),
            jax.ShapeDtypeStruct((8, LANES), f32),
        ],
        scratch_shapes=[
            pltpu.VMEM((SHARD, LANES), f32),
            pltpu.VMEM((2, 4, 2, 2, SHARD, LANES), bf16),
            pltpu.SemaphoreType.DMA((2, 4)),
        ]
        + SCATTER_SCRATCH * 2,
        compiler_params=pltpu.CompilerParams(
            collective_id=1, has_side_effects=True, vmem_limit_bytes=48 * MIB
        ),
    )(*grads)
    return jnp.stack([flat0.reshape(-1), flat1.reshape(-1)]), norm[0] + norm[1]


def store_travel(plan, own, index, start, value):
    for device, entries in enumerate(plan):
        z, y, x, c = coordinates(device)
        for entry, row, count, block, _, _, place in entries:
            column = LANES * block - start
            if entry == index and 0 <= column < value.shape[1]:
                own[z, y, x, c, place : place + count, :] = value[row : row + count, column : column + LANES]


def store_norms(plan, own, block, sums):
    width = sums.shape[2]
    per_row = width // LANES
    line = lax.broadcasted_iota(jnp.int32, (ROW_TILE, LANES), 0)
    for device in range(len(plan)):
        z, y, x, c = coordinates(device)
        row = device // per_row - 4 * block
        if 0 <= row < 4:
            column = LANES * (device % per_row)
            value = jnp.sum(sums[row, :, column : column + LANES], axis=0, keepdims=True)
            coarse = value.astype(bf16).astype(f32)
            rows = jnp.where(line == 0, coarse, jnp.where(line == 1, value - coarse, 0.0))
        else:
            rows = jnp.zeros((ROW_TILE, LANES), f32)
        own[z, y, x, c, SHARD - ROW_TILE : SHARD, :] = rows.astype(bf16)


def weight_grads(first, grad_packed, mixture, attn, second, grad_hidden, active, branch, store, chunk=512):
    sides = ((first, grad_packed), (mixture, attn), (second, grad_hidden), (active, branch))
    for index, (left, right) in enumerate(sides):
        for start in range(0, right.shape[1], chunk):
            store(index, start, dot_tn(left[...], right[:, start : start + chunk]).astype(bf16))


def grad_outputs(plan, width, hidden):
    shapes = matrix_shapes(width, hidden) if plan is None else [(4, 2, 2, 2, SHARD, LANES)]
    return [whole(s) for s in shapes], [jax.ShapeDtypeStruct(s, bf16) for s in shapes]


def storing(plan, block, outs, sums):
    if plan is None:
        def store(index, start, value):
            outs[index][:, start : start + value.shape[1]] = value
        return store
    store_norms(plan, outs[0], block, sums)
    return partial(store_travel, plan, outs[0])


def temporal_kernel(
    plan, length_ref, rows_ref, cotangent_ref, *refs
):
    sources = 5 if plan is None else 2
    refs, sources = refs[sources:], refs[:sources]
    result_ref, before_ref, *refs = refs
    if plan is None:
        w_qkv, w_out, w_up, w_down, norm_ref = sources
    else:
        *refs, w_qkv, w_out, w_up, w_down, local = refs
        norm_ref = sources[1]
    outs, g_norm = refs[:-15], refs[-15]
    packed, slope, weights_buf, grad_mix, scores, grad_scores = refs[-14:-8]
    first_all, packed_all, mixture_all, attn_all, second_all, hidden_all, active_all, branch_all = refs[-8:]
    step = pl.program_id(0)
    steps, patches, width = rows_ref.shape
    tile = steps * patches
    here = pl.ds(pl.multiple_of(step * tile, tile), tile)
    length = length_ref[0]
    group = PATCH_GROUP
    count = steps * group

    @pl.when(step == 0)
    def _():
        g_norm[...] = jnp.zeros_like(g_norm)
        if plan is not None:
            load_weights(plan, sources[0], outs[0], (w_qkv, w_out, w_up, w_down), local)

    row = lax.broadcasted_iota(jnp.int32, (count, count), 0)
    column = lax.broadcasted_iota(jnp.int32, (count, count), 1)
    seen = (row % group == column % group) & (column // group <= row // group)
    seen = seen & (column // group < length)
    bias = jnp.where(seen, 0.0, masked_score)
    low_half = lane_halves(count)

    rows = rows_ref[...].reshape(tile, width)
    hat, _ = normalise(rows)
    first = (hat * norm_ref[0:1] + norm_ref[1:2]).astype(bf16)
    first_all[here, :] = first
    packed[...] = dot_nn(first, w_qkv[...]).astype(bf16).reshape(packed.shape)

    mixture_view = mixture_all.at[here, :]

    def cut(source, part, place, pair):
        start = part * width + 128 * pair
        return source[:, place : place + group, start : start + 128].reshape(count, 128)

    def units_of(backward):
        units = []
        for place in range(0, patches, group):
            for pair in range(HEADS // 2):

                def put(*values, place=place, pair=pair):
                    for part, value in enumerate(values):
                        start = part * width + 128 * pair
                        into = packed if backward else grad_mix
                        into[:, place : place + group, start : start + 128] = value.reshape(steps, group, 128)

                gets = [partial(cut, packed, part, place, pair) for part in range(3)]
                if backward:
                    gets.append(partial(cut, grad_mix, 0, place, pair))
                units.append((*gets, put))
        return units

    attend(units_of(False), scores, weights_buf, low_half, bias)
    mixture = grad_mix[...].reshape(tile, width)
    mixture_all[here, :] = mixture
    middle = rows + dot_nn(mixture, w_out[...])
    hat, scale = normalise(middle)
    second = (hat * norm_ref[2:3] + norm_ref[3:4]).astype(bf16)
    second_all[here, :] = second
    after = middle + feed_forward(second, w_up, w_down, active_all.at[here, :], slope)
    result_ref[...] = after.reshape(result_ref.shape)

    slot = lax.broadcasted_iota(jnp.int32, rows_ref.shape, 0)
    live = (slot < length).astype(f32)
    grad_after = (cotangent_ref[...].astype(f32) * live).reshape(tile, width)
    branch = grad_after.astype(bf16)
    branch_all[here, :] = branch
    hidden_backward(branch, w_down, slope, hidden_all.at[here, :])
    grad_second = dot_nt(hidden_all[here, :], w_up[...])
    hat, scale = normalise(middle)
    grad_rows, gain, shift = norm_backward(hat, scale, norm_ref[2:3], grad_second)
    g_norm[2] += gain
    g_norm[3] += shift
    grad_middle = grad_after + grad_rows
    attn = grad_middle.astype(bf16)
    attn_all[here, :] = attn
    grad_mix[...] = dot_nt(attn, w_out[...]).astype(bf16).reshape(grad_mix.shape)
    attend_backward(units_of(True), scores, weights_buf, grad_scores, low_half)
    grad_packed = packed[...].reshape(tile, 3 * width)
    packed_all[here, :] = grad_packed
    grad_first = dot_nt(grad_packed, w_qkv[...])
    hat, scale = normalise(rows)
    grad_rows, gain, shift = norm_backward(hat, scale, norm_ref[0:1], grad_first)
    g_norm[0] += gain
    g_norm[1] += shift
    before_ref[...] = (grad_middle + grad_rows).reshape(before_ref.shape)

    @pl.when(step == pl.num_programs(0) - 1)
    def _():
        weight_grads(
            first_all, packed_all, mixture_all, attn_all, second_all, hidden_all, active_all,
            branch_all, storing(plan, 1, outs, g_norm),
        )


def load_weights(plan, held, room, matrices, local):
    copy = pltpu.make_async_copy(held, room, local.at[0])
    copy.start()
    copy.wait()
    assemble(plan, room, matrices, range(4))


def weight_sources(plan, weights, norms, hidden):
    width = norms.shape[1]
    if plan is None:
        return [*weights, norms], [whole(a.shape) for a in (*weights, norms)], []
    scratch = [pltpu.VMEM(shape, bf16) for shape in matrix_shapes(width, hidden)]
    scratch.append(pltpu.SemaphoreType.DMA((1,)))
    return [weights, norms], [pl.BlockSpec(memory_space=pl.ANY), whole(norms.shape)], scratch


def temporal_block(plan, length, rows, cotangent, weights, norms, hidden):
    grad_specs, grad_shapes = grad_outputs(plan, norms.shape[1], hidden)
    operands, specs, extra = weight_sources(plan, weights, norms, hidden)
    steps, patches, width = rows.shape
    tokens = steps * patches
    part = TEMPORAL_TILE // steps
    count = steps * PATCH_GROUP
    unit_shape = (part // PATCH_GROUP * (HEADS // 2), count, 2 * count)
    slab = pl.BlockSpec((steps, part, width), lambda i: (0, i, 0))
    return pl.pallas_call(
        partial(temporal_kernel, plan),
        grid=(patches // part,),
        in_specs=[pl.BlockSpec(memory_space=pltpu.SMEM), slab, slab] + specs,
        out_specs=[slab, slab] + grad_specs + [whole((4, 8, width))],
        out_shape=[
            jax.ShapeDtypeStruct(rows.shape, f32),
            jax.ShapeDtypeStruct(rows.shape, f32),
        ]
        + grad_shapes
        + [jax.ShapeDtypeStruct((4, 8, width), f32)],
        scratch_shapes=[
            pltpu.VMEM((steps, part, 3 * width), bf16),
            pltpu.VMEM((TEMPORAL_TILE, hidden), bf16),
            pltpu.VMEM(unit_shape, bf16),
            pltpu.VMEM((steps, part, width), bf16),
            pltpu.VMEM(unit_shape, f32),
            pltpu.VMEM(unit_shape, bf16),
            pltpu.VMEM((tokens, width), bf16),
            pltpu.VMEM((tokens, 3 * width), bf16),
            pltpu.VMEM((tokens, width), bf16),
            pltpu.VMEM((tokens, width), bf16),
            pltpu.VMEM((tokens, width), bf16),
            pltpu.VMEM((tokens, hidden), bf16),
            pltpu.VMEM((tokens, hidden), bf16),
            pltpu.VMEM((tokens, width), bf16),
        ]
        + extra,
        compiler_params=pltpu.CompilerParams(vmem_limit_bytes=62 * MIB),
    )(length, rows, cotangent, *operands)


def spatial_backward_kernel(
    plan, x_ref, grad_ref, packed_ref, weights_ref, middle_ref, slope_ref, mixture_all, active_all, *refs
):
    sources = 5 if plan is None else 2
    refs, sources = refs[sources:], refs[:sources]
    before_ref, *refs = refs
    if plan is None:
        w_qkv, w_out, w_up, w_down, norm_ref = sources
    else:
        *refs, w_qkv, w_out, w_up, w_down, local = refs
        norm_ref = sources[1]
    outs, g_norm = refs[:-10], refs[-10]
    scores, grad_scores, grad_mix, first_all, packed_all, attn_all, second_all, hidden_all, branch_all = refs[-9:]
    step = pl.program_id(0)
    tile, width = x_ref.shape
    here = pl.ds(pl.multiple_of(step * tile, tile), tile)

    @pl.when(step == 0)
    def _():
        g_norm[...] = jnp.zeros_like(g_norm)
        if plan is not None:
            load_weights(plan, sources[0], outs[0], (w_qkv, w_out, w_up, w_down), local)

    grad_after = grad_ref[...]
    branch = grad_after.astype(bf16)
    branch_all[here, :] = branch
    hidden_backward(branch, w_down, slope_ref, hidden_all.at[here, :])
    grad_second = dot_nt(hidden_all[here, :], w_up[...])
    hat, scale = normalise(middle_ref[...])
    second_all[here, :] = (hat * norm_ref[2:3] + norm_ref[3:4]).astype(bf16)
    grad_rows, gain, shift = norm_backward(hat, scale, norm_ref[2:3], grad_second)
    g_norm[2] += gain
    g_norm[3] += shift
    grad_middle = grad_after + grad_rows
    attn = grad_middle.astype(bf16)
    attn_all[here, :] = attn
    grad_mix[...] = dot_nt(attn, w_out[...]).astype(bf16)
    frame = weights_ref.shape[2]
    low_half = lane_halves(frame)
    for item in range(weights_ref.shape[0]):
        span = slice(item * frame, (item + 1) * frame)
        there = pl.ds(pl.multiple_of(step * tile + item * frame, frame), frame)
        units = []
        for pair in range(HEADS // 2):

            def cut(part, pair=pair, span=span):
                start = part * width + 128 * pair
                return packed_ref[span, start : start + 128]

            def cut_grad(pair=pair, span=span):
                return grad_mix[span, 128 * pair : 128 * (pair + 1)]

            def put(*values, pair=pair, there=there):
                for part, value in enumerate(values):
                    start = part * width + 128 * pair
                    packed_all[there, start : start + 128] = value

            units.append((partial(cut, 0), partial(cut, 1), partial(cut, 2), cut_grad, put))
        attend_backward(units, scores, weights_ref.at[item], grad_scores, low_half)
    grad_first = dot_nt(packed_all[here, :], w_qkv[...])
    hat, scale = normalise(x_ref[...].astype(f32))
    first_all[here, :] = (hat * norm_ref[0:1] + norm_ref[1:2]).astype(bf16)
    grad_rows, gain, shift = norm_backward(hat, scale, norm_ref[0:1], grad_first)
    g_norm[0] += gain
    g_norm[1] += shift
    before_ref[...] = grad_middle + grad_rows

    @pl.when(step == pl.num_programs(0) - 1)
    def _():
        weight_grads(
            first_all, packed_all, mixture_all, attn_all, second_all, hidden_all, active_all,
            branch_all, storing(plan, 0, outs, g_norm),
        )


def spatial_backward(plan, x, grad, kept, weights, norms):
    packed, soft, mixture, middle, active, slope = kept
    tokens, width = x.shape
    hidden = active.shape[1]
    grad_specs, grad_shapes = grad_outputs(plan, width, hidden)
    operands, specs, extra = weight_sources(plan, weights, norms, hidden)
    frame = soft.shape[2]
    tile = SPATIAL_TILE
    return pl.pallas_call(
        partial(spatial_backward_kernel, plan),
        grid=(tokens // tile,),
        in_specs=[
            tiles(tile, width),
            tiles(tile, width),
            tiles(tile, 3 * width),
            tiles(tile // frame, HEADS // 2, frame, 2 * frame),
            tiles(tile, width),
            tiles(tile, hidden),
            whole(mixture.shape),
            whole(active.shape),
        ]
        + specs,
        out_specs=[tiles(tile, width)]
        + grad_specs
        + [whole((4, 8, width))],
        out_shape=[jax.ShapeDtypeStruct((tokens, width), f32)]
        + grad_shapes
        + [jax.ShapeDtypeStruct((4, 8, width), f32)],
        scratch_shapes=[
            pltpu.VMEM((HEADS // 2, frame, 2 * frame), f32),
            pltpu.VMEM((HEADS // 2, frame, 2 * frame), bf16),
            pltpu.VMEM((tile, width), bf16),
            pltpu.VMEM((tokens, width), bf16),
            pltpu.VMEM((tokens, 3 * width), bf16),
            pltpu.VMEM((tokens, width), bf16),
            pltpu.VMEM((tokens, width), bf16),
            pltpu.VMEM((tokens, hidden), bf16),
            pltpu.VMEM((tokens, width), bf16),
        ]
        + extra,
        compiler_params=pltpu.CompilerParams(vmem_limit_bytes=62 * MIB),
    )(x, grad, packed, soft, middle, slope, mixture, active, *operands)


def unpack(flat_weights, model_width, hidden_width):
    cut_qkv = 3 * model_width * model_width
    cut_out = 4 * model_width * model_width
    cut_up = cut_out + model_width * hidden_width
    return (
        flat_weights[:cut_qkv].reshape(model_width, 3 * model_width),
        flat_weights[cut_qkv:cut_out].reshape(model_width, model_width),
        flat_weights[cut_out:cut_up].reshape(model_width, hidden_width),
        flat_weights[cut_up:].reshape(hidden_width, model_width),
    )


def adamw(param_value, moment, second, grad_total, step_value, rate, decay_rate):
    moment_next = beta_first * moment + (1.0 - beta_first) * grad_total
    second_next = beta_second * second + (1.0 - beta_second) * grad_total * grad_total
    moment_hat = moment_next / (1.0 - beta_first**step_value)
    second_hat = second_next / (1.0 - beta_second**step_value)
    param_next = param_value - rate * (
        moment_hat / (jnp.sqrt(second_hat) + adam_floor) + decay_rate * param_value
    )
    return (param_next, moment_next, second_next)


def on_device(
    clip_tokens,
    cotangent,
    lengths,
    params,
    param_moment,
    param_second,
    norm_par,
    norm_moment,
    norm_second,
):
    clip_count, step_slots, patch_count, model_width = clip_tokens.shape
    shards = lax.axis_size("dp")
    plan = shard_plan(shards, model_width, FF) if shards == 32 else None
    x = clip_tokens.reshape(-1, model_width)
    if plan is None:
        gathered = lax.all_gather(params.astype(bf16), "dp", axis=1, tiled=True)
        norm_whole = lax.all_gather(norm_par.astype(bf16), "dp", axis=0, tiled=True)
        norm_table = norm_whole.astype(f32).reshape(2, 4, model_width)
        spatial_weights = unpack(gathered[0], model_width, FF)
        temporal_weights = unpack(gathered[1], model_width, FF)
        sources = (*spatial_weights, norm_table[0])
        *kept, after = spatial_forward(plan, x, sources, patch_count, FF)
    else:
        sources = (params.reshape(2, -1, LANES), norm_par.reshape(1, LANES))
        *kept, after, spatial_weights, temporal_weights, norm_table = spatial_forward(
            plan, x, sources, patch_count, FF
        )
        norm_table = norm_table.reshape(2, 4, model_width)
    result, grad_after, *temporal_grads, temporal_norm = temporal_block(
        plan,
        lengths,
        after.reshape(step_slots, patch_count, model_width),
        cotangent.reshape(step_slots, patch_count, model_width),
        temporal_weights,
        norm_table[1],
        FF,
    )
    grad_before, *spatial_grads, spatial_norm = spatial_backward(
        plan, x, grad_after.reshape(-1, model_width), kept, spatial_weights, norm_table[0]
    )

    if plan is None:

        def scatter(grads):
            flat = jnp.concatenate([g.reshape(-1) for g in grads])
            return lax.psum_scatter(flat, "dp", scatter_dimension=0, tiled=True).astype(f32)

        weight_sum = jnp.stack([scatter(spatial_grads), scatter(temporal_grads)])
        norm_grad = jnp.stack([spatial_norm, temporal_norm]).sum(axis=2).reshape(-1)
        norm_sum = lax.psum_scatter(norm_grad, "dp", scatter_dimension=0, tiled=True)
    else:
        weight_sum, norm_sum = scatter_grads(plan, (spatial_grads[0], temporal_grads[0]))
    step_value = float(STEP)
    new_params, new_moment, new_second = adamw(
        params, param_moment, param_second, weight_sum, step_value, learn_rate, weight_decay
    )
    new_norm, new_norm_moment, new_norm_second = adamw(
        norm_par, norm_moment, norm_second, norm_sum, step_value, norm_rate, 0.0
    )
    return (
        result.reshape(clip_tokens.shape),
        grad_before.reshape(clip_tokens.shape),
        new_params,
        new_moment,
        new_second,
        new_params.astype(bf16),
        new_norm,
        new_norm_moment,
        new_norm_second,
    )


def solution(mesh):
    placed = (
        P("dp", None, None, None),
        P("dp", None, None, None),
        P("dp"),
        P(None, "dp"),
        P(None, "dp"),
        P(None, "dp"),
        P("dp"),
        P("dp"),
        P("dp"),
    )
    return jax.shard_map(
        on_device,
        mesh=mesh,
        in_specs=placed,
        out_specs=(
            P("dp", None, None, None),
            P("dp", None, None, None),
            P(None, "dp"),
            P(None, "dp"),
            P(None, "dp"),
            P(None, "dp"),
            P("dp"),
            P("dp"),
            P("dp"),
        ),
        check_vma=False,
    )
```

```python
from functools import partial

import jax
import jax.numpy as jnp
from jax import lax
from jax.experimental import pallas as pl
from jax.experimental.pallas import tpu as pltpu
from jax.sharding import PartitionSpec as P

HEADS = 8
HEAD_DIM = 64
FF = 2048
STEP = 7

norm_epsilon = 1e-05
beta_first = 0.9
beta_second = 0.999
learn_rate = 0.05
norm_rate = 0.5
weight_decay = 0.1
adam_floor = 1e-08
masked_score = -1e30

bf16 = jnp.bfloat16
f32 = jnp.float32
MIB = 2**20

SPATIAL_TILE = 256
TEMPORAL_TILE = 256
PATCH_GROUP = 16


def dot_nn(left, right):
    return lax.dot_general(left, right, (((1,), (0,)), ((), ())), preferred_element_type=f32)


def dot_nt(left, right):
    return lax.dot_general(left, right, (((1,), (1,)), ((), ())), preferred_element_type=f32)


def dot_tn(left, right):
    return lax.dot_general(left, right, (((0,), (0,)), ((), ())), preferred_element_type=f32)


def normalise(rows):
    center = rows - jnp.mean(rows, axis=-1, keepdims=True)
    spread = jnp.mean(center * center, axis=-1, keepdims=True)
    scale = lax.rsqrt(spread + norm_epsilon)
    return center * scale, scale


def fold_rows(rows):
    return jnp.sum(rows.reshape(-1, 8, rows.shape[-1]), axis=0)


def norm_backward(hat, scale, gain, grad):
    weighted = grad * gain
    mean_first = jnp.mean(weighted, axis=-1, keepdims=True)
    mean_second = jnp.mean(weighted * hat, axis=-1, keepdims=True)
    grad_rows = scale * (weighted - mean_first - hat * mean_second)
    return grad_rows, fold_rows(grad * hat), fold_rows(grad)


def gelu_pair(value):
    cumulative = 0.5 + 0.5 * lax.erf(value * 0.7071067811865476)
    density = jnp.exp(-0.5 * value * value) * 0.3989422804014327
    return value * cumulative, cumulative + value * density


def lane_halves(count):
    lane = lax.broadcasted_iota(jnp.int32, (count, 2 * HEAD_DIM), 1)
    return lane < HEAD_DIM


def two_heads(pair, low_half):
    zero = jnp.zeros_like(pair)
    return jnp.concatenate([jnp.where(low_half, pair, zero), jnp.where(low_half, zero, pair)], axis=0)


def own_columns(stacked, low_half):
    rows = stacked.shape[0] // 2
    return jnp.where(low_half, stacked[:rows], stacked[rows:]).astype(bf16)


ROW_CHUNK = 64


def attend(units, scores, soft, low_half, bias):
    rows, double = scores.shape[1:]
    keys = double // 2
    for unit, (query, key, value, put) in enumerate(units):
        scaled = query() * jnp.asarray(HEAD_DIM**-0.5, bf16)
        scores[unit] = dot_nt(scaled, two_heads(key(), low_half))
    for unit in range(len(units)):
        for start in range(0, rows, ROW_CHUNK):
            span = slice(start, start + ROW_CHUNK)
            for half in range(2):
                columns = slice(half * keys, (half + 1) * keys)
                part = scores[unit, span, columns]
                if bias is not None:
                    part = part + bias[span]
                powers = jnp.exp(part - jnp.max(part, axis=-1, keepdims=True))
                part = powers * (1.0 / jnp.sum(powers, axis=-1, keepdims=True))
                soft[unit, span, columns] = part.astype(bf16)
    for unit, (query, key, value, put) in enumerate(units):
        put(dot_nn(soft[unit], two_heads(value(), low_half)).astype(bf16))


def attend_backward(units, scores, soft, grad_scores, low_half):
    rows, double = scores.shape[1:]
    keys = double // 2
    scale = jnp.asarray(HEAD_DIM**-0.5, bf16)
    for unit, (query, key, value, grad, put) in enumerate(units):
        scores[unit] = dot_nt(grad(), two_heads(value(), low_half))
    for unit in range(len(units)):
        for start in range(0, rows, ROW_CHUNK):
            span = slice(start, start + ROW_CHUNK)
            for half in range(2):
                columns = slice(half * keys, (half + 1) * keys)
                wide = soft[unit, span, columns].astype(f32)
                product = scores[unit, span, columns] * wide
                inner = jnp.sum(product, axis=-1, keepdims=True)
                grad_scores[unit, span, columns] = (product - wide * inner).astype(bf16)
    for unit, (query, key, value, grad, put) in enumerate(units):
        grad_value = own_columns(dot_tn(soft[unit], grad()), low_half)
        grad_query = dot_nn(grad_scores[unit], two_heads(key() * scale, low_half)).astype(bf16)
        grad_key = own_columns(dot_tn(grad_scores[unit], query() * scale), low_half)
        put(grad_query, grad_key, grad_value)


def feed_forward(second, w_up, w_down, active_ref, slope_ref, chunk=512):
    hidden = w_up.shape[1]
    for start in range(0, hidden, chunk):
        active, slope = gelu_pair(dot_nn(second, w_up[:, start : start + chunk]))
        active_ref[:, start : start + chunk] = active.astype(bf16)
        slope_ref[:, start : start + chunk] = slope.astype(bf16)
    return dot_nn(active_ref[...], w_down[...])


def hidden_backward(branch, w_down, slope_ref, hidden_ref, chunk=512):
    hidden = w_down.shape[0]
    for start in range(0, hidden, chunk):
        grad = dot_nt(branch, w_down[start : start + chunk, :])
        slope = slope_ref[:, start : start + chunk].astype(f32)
        hidden_ref[:, start : start + chunk] = (grad * slope).astype(bf16)


def spatial_forward_kernel(plan, x_ref, *refs):
    step, last = pl.program_id(1), pl.num_programs(1) - 1
    opening = pl.program_id(0) == 0
    if plan is None:
        w_qkv, w_out, w_up, w_down, norm_ref = refs[:5]
        refs = refs[5:]
        packed_ref, weights_ref, mixture_ref, middle_ref, active_ref, slope_ref, after_ref = refs[:7]
        scores, mixture_all = refs[7:]
    else:
        shard_ref, norm_par_ref = refs[:2]
        refs = refs[2:]
        packed_ref, weights_ref, mixture_ref, middle_ref, active_ref, slope_ref, after_ref = refs[:7]
        held_out, held_next, norm_ref = refs[7:10]
        scores, mixture_all, w_qkv, w_out, w_up, w_down, held, staged, send, recv, local = refs[10:]
        matrices = (w_qkv, w_out, w_up, w_down)
        place = Place(lax.axis_index("dp"))
        now = Gather(place, held, send.at[0], recv.at[0])
        later = Gather(place, held_next, send.at[1], recv.at[1])
        keep = pltpu.make_async_copy(held, held_out, local.at[0])

        def gathered(*planes):
            for q in planes:
                now.finish(q)
            assemble(plan, held, matrices, planes)
            assemble_norms(len(plan), held, norm_ref, planes)

        @pl.when(opening & (step == 0))
        def _():
            enter(place)
            load_shard(plan, place.me, shard_ref.at[0], norm_par_ref, held.at[place.z, place.y, place.x, place.c])
            now.start_z()
            load_shard(plan, place.me, shard_ref.at[1], norm_par_ref, staged)
            copy = pltpu.make_async_copy(
                staged, held_next.at[place.z, place.y, place.x, place.c], local.at[1]
            )
            copy.start()
            copy.wait()
            now.begin_first(0)
            now.begin_second(0)
            for q in range(1, 4):
                now.begin_first(q)
            now.begin_third(0)
            later.start_z()
            gathered(0)

        @pl.when(opening & (step == 1))
        def _():
            now.begin_second(1)
            now.begin_second(2)

        @pl.when(opening & (step == 2))
        def _():
            now.begin_second(3)

        @pl.when(opening & (step == 3))
        def _():
            now.begin_third(1)
            for q in range(4):
                later.begin_first(q)

        @pl.when(opening & (step == 4))
        def _():
            now.begin_third(2)
            later.begin_second(0)

        @pl.when(opening & (step == 6))
        def _():
            now.begin_third(3)
            later.begin_second(1)

        @pl.when(jnp.logical_not(opening) & (step == 0))
        def _():
            later.begin_second(2)
            later.begin_second(3)
            gathered(1, 2, 3)
            keep.start()

        for q in range(4):

            @pl.when(jnp.logical_not(opening) & (step == 2 * q + 1))
            def _(q=q):
                later.begin_third(q)

    tile, width = x_ref.shape
    here = pl.ds(pl.multiple_of(step * tile, tile), tile)

    @pl.when(opening)
    def _():
        hat, _ = normalise(x_ref[...].astype(f32))
        first = (hat * norm_ref[0:1] + norm_ref[1:2]).astype(bf16)
        for start in range(0, 3 * width, 512):
            packed_ref[:, start : start + 512] = dot_nn(first, w_qkv[:, start : start + 512]).astype(bf16)
        frame = weights_ref.shape[2]
        low_half = lane_halves(frame)
        for item in range(weights_ref.shape[0]):
            span = slice(item * frame, (item + 1) * frame)
            units = []
            for pair in range(HEADS // 2):

                def cut(part, pair=pair, span=span):
                    start = part * width + 128 * pair
                    return packed_ref[span, start : start + 128]

                def put(value, pair=pair, span=span):
                    mixture_ref[span, 128 * pair : 128 * (pair + 1)] = value

                units.append((partial(cut, 0), partial(cut, 1), partial(cut, 2), put))
            attend(units, scores, weights_ref.at[item], low_half, None)
        mixture_all[here, :] = mixture_ref[...]

    @pl.when(jnp.logical_not(opening))
    def _():
        middle = x_ref[...].astype(f32) + dot_nn(mixture_all[here, :], w_out[...])
        middle_ref[...] = middle
        hat, _ = normalise(middle)
        second = (hat * norm_ref[2:3] + norm_ref[3:4]).astype(bf16)
        after_ref[...] = middle + feed_forward(second, w_up, w_down, active_ref, slope_ref)

    if plan is not None:

        @pl.when(jnp.logical_not(opening) & (step == last))
        def _():
            for q in range(4):
                later.finish(q)
            keep.wait()
            now.drain()
            later.drain()


def whole(shape):
    return pl.BlockSpec(shape, lambda *_: (0,) * len(shape), pipeline_mode=pl.Buffered(1))


def tiles(tile, *rest):
    return pl.BlockSpec((tile, *rest), lambda i: (i,) + (0,) * len(rest))


def spatial_forward(plan, x, sources, frame, hidden):
    tokens, width = x.shape
    tile = SPATIAL_TILE
    frames = tile // frame
    count = tokens // tile

    def opening(*rest):
        return pl.BlockSpec(rest, lambda p, i: (i + p * (count - 1 - i),) + (0,) * (len(rest) - 1))

    def closing(*rest):
        return pl.BlockSpec(rest, lambda p, i: (i * p,) + (0,) * (len(rest) - 1))

    out_specs = [
        opening(tile, 3 * width),
        opening(frames, HEADS // 2, frame, 2 * frame),
        opening(tile, width),
        closing(tile, width),
        closing(tile, hidden),
        closing(tile, hidden),
        closing(tile, width),
    ]
    out_shape = [
        jax.ShapeDtypeStruct((tokens, 3 * width), bf16),
        jax.ShapeDtypeStruct((tokens // frame, HEADS // 2, frame, 2 * frame), bf16),
        jax.ShapeDtypeStruct((tokens, width), bf16),
        jax.ShapeDtypeStruct((tokens, width), f32),
        jax.ShapeDtypeStruct((tokens, hidden), bf16),
        jax.ShapeDtypeStruct((tokens, hidden), bf16),
        jax.ShapeDtypeStruct((tokens, width), f32),
    ]
    scratch = [pltpu.VMEM((HEADS // 2, frame, 2 * frame), f32), pltpu.VMEM((tokens, width), bf16)]
    params = dict(vmem_limit_bytes=60 * MIB)
    if plan is not None:
        held = (4, 2, 2, 2, SHARD, LANES)
        out_specs += [pl.BlockSpec(memory_space=pl.ANY)] * 2 + [whole((8, width))]
        out_shape += [jax.ShapeDtypeStruct(held, bf16)] * 2 + [jax.ShapeDtypeStruct((8, width), f32)]
        scratch += [pltpu.VMEM(shape, bf16) for shape in matrix_shapes(width, hidden)]
        scratch += [
            pltpu.VMEM(held, bf16),
            pltpu.VMEM((SHARD, LANES), bf16),
            pltpu.SemaphoreType.DMA((2, 6, 4)),
            pltpu.SemaphoreType.DMA((2, 6, 4)),
            pltpu.SemaphoreType.DMA((2,)),
        ]
        params |= dict(collective_id=0, has_side_effects=True)
    return pl.pallas_call(
        partial(spatial_forward_kernel, plan),
        grid=(2, count),
        in_specs=[pl.BlockSpec((tile, width), lambda p, i: (i, 0))] + [whole(a.shape) for a in sources],
        out_specs=out_specs,
        out_shape=out_shape,
        scratch_shapes=scratch,
        compiler_params=pltpu.CompilerParams(**params),
    )(x, *sources)


MESH_IDS = pl.DeviceIdType.MESH
LANES = 128
ROW_TILE = 16


def matrix_shapes(width, hidden):
    return ((width, 3 * width), (width, width), (width, hidden), (hidden, width))


def shard_plan(shards, width, hidden):
    plan = []
    base = 0
    regions = []
    for index, (rows, columns) in enumerate(matrix_shapes(width, hidden)):
        regions.append((index, base, rows, columns))
        base += rows * columns
    if base % shards:
        return None
    size = base // shards
    for device in range(shards):
        low, high = device * size, (device + 1) * size
        halves = ([], [])
        for index, start, rows, columns in regions:
            first, last = max(low, start), min(high, start + rows * columns)
            if first >= last:
                continue
            if (first - start) % columns or (last - start) % columns:
                return None
            row, count = (first - start) // columns, (last - first) // columns
            if row % ROW_TILE or count % ROW_TILE:
                return None
            stride = columns // LANES
            for block in range(stride):
                halves[2 * block // stride].append(
                    (index, row, count, block, (first - low) // LANES + block, stride)
                )
        place = 0
        entries = []
        for item in halves[0] + halves[1]:
            entries.append(item + (place,))
            place += item[2]
        plan.append(entries)
    return plan


def by_pattern(plan):
    groups = {}
    for device, entries in enumerate(plan):
        layout = tuple((e[2], e[4], e[5], e[6]) for e in entries)
        ranges = groups.setdefault(layout, [])
        if ranges and ranges[-1][1] == device:
            ranges[-1][1] = device + 1
        else:
            ranges.append([device, device + 1])
    return list(groups.items())


def on_pattern(plan, me, body):
    for layout, ranges in by_pattern(plan):
        inside = None
        for low, high in ranges:
            test = (me >= low) & (me < high)
            inside = test if inside is None else inside | test

        @pl.when(inside)
        def _(layout=layout):
            body(layout)


class Place:
    def __init__(self, me):
        self.me = me
        self.c = lax.rem(me, 2)
        self.x = lax.rem(me // 2, 2)
        self.y = lax.rem(me // 4, 2)
        self.z = me // 8

    def device(self, z, y, x, c):
        return ((z * 2 + y) * 2 + x) * 2 + c

    @property
    def sibling(self):
        return self.device(self.z, self.y, self.x, 1 - self.c)

    @property
    def across_x(self):
        return self.device(self.z, self.y, 1 - self.x, self.c)

    @property
    def across_y(self):
        return self.device(self.z, 1 - self.y, self.x, self.c)

    def plane(self, z):
        return self.device(z, self.y, self.x, self.c)


def remote(src, dst, send, recv, device):
    return pltpu.make_async_remote_copy(
        src_ref=src, dst_ref=dst, send_sem=send, recv_sem=recv, device_id=(device,), device_id_type=MESH_IDS
    )


def enter(place):
    barrier = pltpu.get_barrier_semaphore()
    partners = [place.sibling, place.across_x, place.across_y]
    partners += [place.plane(lax.rem(place.z + k, 4)) for k in range(1, 4)]
    for device in partners:
        pl.semaphore_signal(barrier, inc=1, device_id=(device,), device_id_type=MESH_IDS)
    pl.semaphore_wait(barrier, len(partners))


HALF = 384
SHARD = 784


class Gather:
    SEMS = 9

    def __init__(self, place, held, send, recv):
        self.p, self.held, self.send, self.recv = place, held, send, recv

    def along_z(self, k):
        p = self.p
        here = self.held.at[p.z, p.y, p.x, p.c]
        return remote(here, here, self.send.at[0, k - 1], self.recv.at[0, p.z], p.plane(lax.rem(p.z + k, 4)))

    def start_z(self):
        for k in range(1, 4):
            self.along_z(k).start()

    def wait_z(self, q):
        p = self.p

        @pl.when(q != p.z)
        def _():
            there = self.held.at[q, p.y, p.x, p.c]
            remote(there, there, self.send.at[0, 0], self.recv.at[0, q], p.me).wait_recv()

    def first(self, q):
        p, h = self.p, self.held
        a = h.at[q, p.y, p.x, p.c, pl.ds(0, HALF)]
        b = h.at[q, p.y, p.x, p.c, pl.ds(HALF, SHARD - HALF)]
        return (
            remote(a, a, self.send.at[1, q], self.recv.at[1, q], p.across_x),
            remote(b, b, self.send.at[2, q], self.recv.at[2, q], p.across_y),
        )

    def second(self, q):
        p, h = self.p, self.held
        a = h.at[q, p.y, :, p.c, pl.ds(0, HALF)]
        b = h.at[q, :, p.x, p.c, pl.ds(HALF, SHARD - HALF)]
        return (
            remote(a, a, self.send.at[3, q], self.recv.at[3, q], p.across_y),
            remote(b, b, self.send.at[4, q], self.recv.at[4, q], p.across_x),
        )

    def third(self, q):
        p, h = self.p, self.held
        a = h.at[q, :, :, p.c]
        return (remote(a, a, self.send.at[5, q], self.recv.at[5, q], p.sibling),)

    def begin_first(self, q):
        self.wait_z(q)
        for copy in self.first(q):
            copy.start()

    def begin_second(self, q):
        for copy in self.first(q):
            copy.wait_recv()
        for copy in self.second(q):
            copy.start()

    def begin_third(self, q):
        for copy in self.second(q):
            copy.wait_recv()
        for copy in self.third(q):
            copy.start()

    def finish(self, q):
        for copy in self.third(q):
            copy.wait_recv()

    def drain(self):
        for k in range(1, 4):
            self.along_z(k).wait_send()
        for q in range(4):
            for copy in self.first(q) + self.second(q) + self.third(q):
                copy.wait_send()


def load_shard(plan, me, shard_ref, norm_ref, held_here):
    def body(layout):
        for count, flat, stride, place in layout:
            held_here[pl.ds(place, count), :] = shard_ref[pl.ds(flat, count, stride), :].astype(bf16)

    on_pattern(plan, me, body)
    held_here[SHARD - ROW_TILE :, :] = jnp.broadcast_to(norm_ref[...], (ROW_TILE, LANES)).astype(bf16)


def coordinates(device):
    return device // 8, device // 4 % 2, device // 2 % 2, device % 2


def assemble(plan, held, outs, planes):
    for device, entries in enumerate(plan):
        z, y, x, c = coordinates(device)
        if z not in planes:
            continue
        for index, row, count, block, _, _, place in entries:
            outs[index][row : row + count, LANES * block : LANES * (block + 1)] = held[
                z, y, x, c, place : place + count, :
            ]


def assemble_norms(shards, held, norm_out, planes):
    per_row = norm_out.shape[1] // LANES
    for device in range(shards):
        z, y, x, c = coordinates(device)
        if z not in planes:
            continue
        row, column = device // per_row, device % per_row
        norm_out[row : row + 1, LANES * column : LANES * (column + 1)] = held[
            z, y, x, c, SHARD - ROW_TILE : SHARD, :
        ].astype(f32)[0:1]


class Scatter:
    def __init__(self, place, own, room, send, recv, credit=None, leads=None):
        self.p, self.own = place, own
        rows, half = room[3].shape[1], room[1].shape[2]
        self.low, self.high = pl.ds(0, half), pl.ds(half, rows - half)
        self.r1, self.r2a, self.r2b, self.r3, self.r4 = room
        self.send, self.recv, self.credit, self.leads = send, recv, credit, leads

    def release(self, kind, q, device):
        if self.leads is True:
            pl.semaphore_signal(self.credit.at[kind, q], inc=1, device_id=(device,), device_id_type=MESH_IDS)

    def claim(self, kind, q):
        if self.leads is False:
            pl.semaphore_wait(self.credit.at[kind, q], 1)

    def first(self, q):
        p = self.p
        return (
            remote(
                self.own.at[q, :, :, 1 - p.c], self.r1.at[q], self.send.at[0, q], self.recv.at[0, q], p.sibling
            ),
        )

    def second(self, q):
        p = self.p
        low, high = self.low, self.high
        return (
            remote(
                self.r1.at[q, :, 1 - p.x, low], self.r2a.at[q], self.send.at[1, q], self.recv.at[1, q], p.across_x
            ),
            remote(
                self.r1.at[q, 1 - p.y, :, high], self.r2b.at[q], self.send.at[2, q], self.recv.at[2, q], p.across_y
            ),
        )

    def third(self, q):
        p = self.p
        low, high = self.low, self.high
        return (
            remote(
                self.r2a.at[q, 1 - p.y], self.r3.at[q, low], self.send.at[3, q], self.recv.at[3, q], p.across_y
            ),
            remote(
                self.r2b.at[q, 1 - p.x], self.r3.at[q, high], self.send.at[4, q], self.recv.at[4, q], p.across_x
            ),
        )

    def along_z(self, q):
        p = self.p
        return remote(self.r3.at[q], self.r4.at[p.z], self.send.at[5, q], self.recv.at[5, p.z], p.plane(q))

    def begin_first(self, q):
        self.claim(0, q)
        for copy in self.first(q):
            copy.start()

    def begin_second(self, q, mine):
        for copy in self.first(q):
            copy.wait_recv()
        for y in range(2):
            for x in range(2):
                self.r1[q, y, x] = self.r1[q, y, x] + mine(y, x)
        self.claim(1, q)
        self.claim(2, q)
        for copy in self.second(q):
            copy.start()

    def begin_third(self, q):
        p = self.p
        for copy in self.second(q):
            copy.wait_recv()
        low, high = self.low, self.high
        for k in range(2):
            self.r2a[q, k] = self.r2a[q, k] + self.r1[q, k, p.x, low]
            self.r2b[q, k] = self.r2b[q, k] + self.r1[q, p.y, k, high]
        for copy in self.third(q):
            copy.start()
        for copy in self.second(q):
            copy.wait_send()
        self.release(0, q, p.sibling)

    def begin_z(self, q, total):
        p = self.p
        for copy in self.third(q):
            copy.wait_recv()
        low, high = self.low, self.high
        self.r3[q, low] = self.r3[q, low] + self.r2a[q, p.y]
        self.r3[q, high] = self.r3[q, high] + self.r2b[q, p.x]

        @pl.when(q != p.z)
        def _():
            self.along_z(q).start()

        @pl.when(q == p.z)
        def _():
            total[...] = self.r3[q].astype(f32)

        for copy in self.third(q):
            copy.wait_send()
        self.release(1, q, p.across_x)
        self.release(2, q, p.across_y)

    def leave_z(self, q):
        p = self.p

        @pl.when(q != p.z)
        def _():
            self.along_z(q).wait_send()

    def finish(self, total):
        p = self.p
        planes = self.r3.shape[0]

        @pl.when(p.z < planes)
        def _():
            for k in range(1, 4):
                z = lax.rem(p.z + k, 4)
                remote(self.r3.at[0], self.r4.at[z], self.send.at[5, 0], self.recv.at[5, z], p.me).wait_recv()
            for k in range(1, 4):
                total[...] += self.r4[lax.rem(p.z + k, 4)].astype(f32)

        for q in range(planes):
            for copy in self.first(q):
                copy.wait_send()
            self.leave_z(q)


SCATTER_ROOM = [
    pltpu.VMEM((4, 2, 2, SHARD, LANES), bf16),
    pltpu.VMEM((4, 2, HALF, LANES), bf16),
    pltpu.VMEM((4, 2, SHARD - HALF, LANES), bf16),
    pltpu.VMEM((2, 4, SHARD, LANES), bf16),
    pltpu.VMEM((2, 4, SHARD, LANES), bf16),
]

SMALL = 2 * ROW_TILE
SMALL_ROOM = [
    pltpu.VMEM((1, 2, 2, 2, SMALL, LANES), bf16),
    pltpu.VMEM((1, 2, 2, SMALL, LANES), bf16),
    pltpu.VMEM((1, 2, ROW_TILE, LANES), bf16),
    pltpu.VMEM((1, 2, ROW_TILE, LANES), bf16),
    pltpu.VMEM((1, SMALL, LANES), bf16),
    pltpu.VMEM((4, SMALL, LANES), bf16),
    pltpu.VMEM((SMALL, LANES), f32),
    pltpu.SemaphoreType.DMA((6, 4)),
    pltpu.SemaphoreType.DMA((6, 4)),
]


def unload_shard(plan, me, total, flat_ref):
    def body(layout):
        for count, flat, stride, place in layout:
            flat_ref[pl.ds(flat, count, stride), :] = total[pl.ds(place, count), :]

    on_pattern(plan, me, body)


def store_travel(plan, own, index, top, start, value):
    for device, entries in enumerate(plan):
        z, y, x, c = coordinates(device)
        for entry, row, count, block, _, _, place in entries:
            column = LANES * block - start
            low, high = max(row, top), min(row + count, top + value.shape[0])
            if entry == index and 0 <= column < value.shape[1] and low < high:
                own[z, y, x, c, place + low - row : place + high - row, :] = value[
                    low - top : high - top, column : column + LANES
                ]


def store_norms(plan, own, block, sums, planes, first=SHARD - ROW_TILE):
    width = sums.shape[2]
    per_row = width // LANES
    line = lax.broadcasted_iota(jnp.int32, (ROW_TILE, LANES), 0)
    for device in range(len(plan)):
        z, y, x, c = coordinates(device)
        if z not in planes:
            continue
        row = device // per_row - 4 * block
        if 0 <= row < 4:
            column = LANES * (device % per_row)
            value = jnp.sum(sums[row, :, column : column + LANES], axis=0, keepdims=True)
            coarse = value.astype(bf16).astype(f32)
            rows = jnp.where(line == 0, coarse, jnp.where(line == 1, value - coarse, 0.0))
        else:
            rows = jnp.zeros((ROW_TILE, LANES), f32)
        own[z, y, x, c, first : first + ROW_TILE, :] = rows.astype(bf16)


def weight_grads(first, grad_packed, mixture, attn, second, grad_hidden, active, branch, store, chunk=512):
    sides = ((first, grad_packed), (mixture, attn), (second, grad_hidden), (active, branch))
    for index, (left, right) in enumerate(sides):
        for start in range(0, right.shape[1], chunk):
            store(index, 0, start, dot_tn(left[...], right[:, start : start + chunk]).astype(bf16))


def grad_outputs(plan, width, hidden):
    shapes = matrix_shapes(width, hidden) if plan is None else [(4, 2, 2, 2, SHARD, LANES)]
    return [whole(s) for s in shapes], [jax.ShapeDtypeStruct(s, bf16) for s in shapes]


def storing(plan, outs):
    if plan is None:
        def store(index, top, start, value):
            outs[index][top : top + value.shape[0], start : start + value.shape[1]] = value
        return store
    return partial(store_travel, plan, outs[0])


def temporal_kernel(
    plan, length_ref, rows_ref, cotangent_ref, *refs
):
    sources = 5 if plan is None else 2
    refs, sources = refs[sources:], refs[:sources]
    result_ref, before_ref, *refs = refs
    if plan is None:
        w_qkv, w_out, w_up, w_down, norm_ref = sources
    else:
        *refs, w_qkv, w_out, w_up, w_down, local = refs
        norm_ref = sources[1]
    outs, g_norm = refs[:-15], refs[-15]
    packed, slope, weights_buf, grad_mix, scores, grad_scores = refs[-14:-8]
    first_all, packed_all, mixture_all, attn_all, second_all, hidden_all, active_all, branch_all = refs[-8:]
    step = pl.program_id(0)
    steps, patches, width = rows_ref.shape
    tile = steps * patches
    here = pl.ds(pl.multiple_of(step * tile, tile), tile)
    length = length_ref[0]
    group = PATCH_GROUP
    count = steps * group

    @pl.when(step == 0)
    def _():
        g_norm[...] = jnp.zeros_like(g_norm)
        if plan is not None:
            load_weights(plan, sources[0], outs[0], (w_qkv, w_out, w_up, w_down), local)

    row = lax.broadcasted_iota(jnp.int32, (count, count), 0)
    column = lax.broadcasted_iota(jnp.int32, (count, count), 1)
    seen = (row % group == column % group) & (column // group <= row // group)
    seen = seen & (column // group < length)
    bias = jnp.where(seen, 0.0, masked_score)
    low_half = lane_halves(count)

    rows = rows_ref[...].reshape(tile, width)
    hat, _ = normalise(rows)
    first = (hat * norm_ref[0:1] + norm_ref[1:2]).astype(bf16)
    first_all[here, :] = first
    packed[...] = dot_nn(first, w_qkv[...]).astype(bf16).reshape(packed.shape)

    mixture_view = mixture_all.at[here, :]

    def cut(source, part, place, pair):
        start = part * width + 128 * pair
        return source[:, place : place + group, start : start + 128].reshape(count, 128)

    def units_of(backward):
        units = []
        for place in range(0, patches, group):
            for pair in range(HEADS // 2):

                def put(*values, place=place, pair=pair):
                    for part, value in enumerate(values):
                        start = part * width + 128 * pair
                        into = packed if backward else grad_mix
                        into[:, place : place + group, start : start + 128] = value.reshape(steps, group, 128)

                gets = [partial(cut, packed, part, place, pair) for part in range(3)]
                if backward:
                    gets.append(partial(cut, grad_mix, 0, place, pair))
                units.append((*gets, put))
        return units

    attend(units_of(False), scores, weights_buf, low_half, bias)
    mixture = grad_mix[...].reshape(tile, width)
    mixture_all[here, :] = mixture
    middle = rows + dot_nn(mixture, w_out[...])
    hat, scale = normalise(middle)
    second = (hat * norm_ref[2:3] + norm_ref[3:4]).astype(bf16)
    second_all[here, :] = second
    after = middle + feed_forward(second, w_up, w_down, active_all.at[here, :], slope)
    result_ref[...] = after.reshape(result_ref.shape)

    slot = lax.broadcasted_iota(jnp.int32, rows_ref.shape, 0)
    live = (slot < length).astype(f32)
    grad_after = (cotangent_ref[...].astype(f32) * live).reshape(tile, width)
    branch = grad_after.astype(bf16)
    branch_all[here, :] = branch
    hidden_backward(branch, w_down, slope, hidden_all.at[here, :])
    grad_second = dot_nt(hidden_all[here, :], w_up[...])
    hat, scale = normalise(middle)
    grad_rows, gain, shift = norm_backward(hat, scale, norm_ref[2:3], grad_second)
    g_norm[2] += gain
    g_norm[3] += shift
    grad_middle = grad_after + grad_rows
    attn = grad_middle.astype(bf16)
    attn_all[here, :] = attn
    grad_mix[...] = dot_nt(attn, w_out[...]).astype(bf16).reshape(grad_mix.shape)
    attend_backward(units_of(True), scores, weights_buf, grad_scores, low_half)
    grad_packed = packed[...].reshape(tile, 3 * width)
    packed_all[here, :] = grad_packed
    grad_first = dot_nt(grad_packed, w_qkv[...])
    hat, scale = normalise(rows)
    grad_rows, gain, shift = norm_backward(hat, scale, norm_ref[0:1], grad_first)
    g_norm[0] += gain
    g_norm[1] += shift
    before_ref[...] = (grad_middle + grad_rows).reshape(before_ref.shape)

    @pl.when(step == pl.num_programs(0) - 1)
    def _():
        if plan is not None:
            store_norms(plan, outs[0], 1, g_norm, range(4))
        weight_grads(
            first_all, packed_all, mixture_all, attn_all, second_all, hidden_all, active_all,
            branch_all, storing(plan, outs),
        )


def load_weights(plan, held, room, matrices, local):
    copy = pltpu.make_async_copy(held, room, local.at[0])
    copy.start()
    copy.wait()
    assemble(plan, room, matrices, range(4))


def weight_sources(plan, weights, norms, hidden):
    width = norms.shape[1]
    if plan is None:
        return [*weights, norms], [whole(a.shape) for a in (*weights, norms)], []
    scratch = [pltpu.VMEM(shape, bf16) for shape in matrix_shapes(width, hidden)]
    scratch.append(pltpu.SemaphoreType.DMA((1,)))
    return [weights, norms], [pl.BlockSpec(memory_space=pl.ANY), whole(norms.shape)], scratch


def temporal_block(plan, length, rows, cotangent, weights, norms, hidden):
    grad_specs, grad_shapes = grad_outputs(plan, norms.shape[1], hidden)
    operands, specs, extra = weight_sources(plan, weights, norms, hidden)
    steps, patches, width = rows.shape
    tokens = steps * patches
    part = TEMPORAL_TILE // steps
    count = steps * PATCH_GROUP
    unit_shape = (part // PATCH_GROUP * (HEADS // 2), count, 2 * count)
    slab = pl.BlockSpec((steps, part, width), lambda i: (0, i, 0))
    return pl.pallas_call(
        partial(temporal_kernel, plan),
        grid=(patches // part,),
        in_specs=[pl.BlockSpec(memory_space=pltpu.SMEM), slab, slab] + specs,
        out_specs=[slab, slab] + grad_specs + [whole((4, 8, width))],
        out_shape=[
            jax.ShapeDtypeStruct(rows.shape, f32),
            jax.ShapeDtypeStruct(rows.shape, f32),
        ]
        + grad_shapes
        + [jax.ShapeDtypeStruct((4, 8, width), f32)],
        scratch_shapes=[
            pltpu.VMEM((steps, part, 3 * width), bf16),
            pltpu.VMEM((TEMPORAL_TILE, hidden), bf16),
            pltpu.VMEM(unit_shape, bf16),
            pltpu.VMEM((steps, part, width), bf16),
            pltpu.VMEM(unit_shape, f32),
            pltpu.VMEM(unit_shape, bf16),
            pltpu.VMEM((tokens, width), bf16),
            pltpu.VMEM((tokens, 3 * width), bf16),
            pltpu.VMEM((tokens, width), bf16),
            pltpu.VMEM((tokens, width), bf16),
            pltpu.VMEM((tokens, width), bf16),
            pltpu.VMEM((tokens, hidden), bf16),
            pltpu.VMEM((tokens, hidden), bf16),
            pltpu.VMEM((tokens, width), bf16),
        ]
        + extra,
        compiler_params=pltpu.CompilerParams(vmem_limit_bytes=62 * MIB),
    )(length, rows, cotangent, *operands)


def spatial_backward_kernel(
    plan, x_ref, grad_ref, packed_ref, weights_ref, middle_ref, slope_ref, mixture_hbm, active_hbm, *refs
):
    step, last = pl.program_id(1), pl.num_programs(1) - 1
    opening, midway, closing = [pl.program_id(0) == k for k in range(3)]
    if plan is None:
        w_qkv, w_out, w_up, w_down, norm_ref, before_ref, *outs, g_norm = refs[:11]
        refs = refs[11:]
    else:
        held, norm_ref, own_next, before_ref, flat0, flat1, norm_out = refs[:7]
        own_small, *room_small, total_small, send_small, recv_small = refs[-len(SMALL_ROOM) :]
        *refs, total, total_rest, own, mine, load, send, recv, credit = refs[7 : -len(SMALL_ROOM)]
        room, refs = refs[-5:], refs[:-5]
        *refs, g_norm, w_qkv, w_out, w_up, w_down, local = refs
        outs = [own]
        place = Place(lax.axis_index("dp"))
        rooms = [(*room[:3], room[3].at[k], room[4].at[k]) for k in range(2)]
        lead = Scatter(place, own_next, rooms[0], send.at[0], recv.at[0], credit, True)
        rest = Scatter(place, own, rooms[1], send.at[1], recv.at[1], credit, False)
        small = Scatter(place, own_small, room_small, send_small, recv_small)
    scores, grad_scores, grad_mix, middle_all, second_all, hidden_all, attn_all, branch_all, side, side_sem = refs
    store = storing(plan, outs)
    tile, width = x_ref.shape
    hidden = slope_ref.shape[1]
    here = pl.ds(pl.multiple_of(step * tile, tile), tile)

    def own_shards(q):
        return pltpu.make_async_copy(own_next.at[q, :, :, place.c], mine.at[q % 2], load.at[q % 2])

    def lead_second(q):
        own_shards(q).wait()
        lead.begin_second(q, lambda y, x: mine[q % 2, y, x])
        if q < 2:
            own_shards(q + 2).start()

    def rest_second(q):
        rest.begin_second(q, lambda y, x: own[q, y, x, place.c])

    def at(passing, when, *actions):
        @pl.when(passing & (step == when))
        def _():
            for action, *q in actions:
                action(*q)

    def begin():
        enter(place)
        for q in range(4):
            lead.begin_first(q)
        own_shards(0).start()
        own_shards(1).start()
        load_weights(plan, held, own, (w_qkv, w_out, w_up, w_down), local)
        lead_second(0)
        lead_second(1)

    def lead_finish():
        lead.finish(total)
        unload_shard(plan, place.me, total, flat1)
        norm_out[...] = total[SHARD - ROW_TILE : SHARD - ROW_TILE + 8]

    @pl.when(opening & (step == 0))
    def _():
        g_norm[...] = jnp.zeros_like(g_norm)

    if plan is not None:
        at(opening, 0, (begin,))
        at(opening, 1, (lead_second, 2))
        at(opening, 2, (lead_second, 3))
        at(opening, 3, (lead.begin_third, 0))
        at(opening, 5, (lead.begin_third, 1))
        at(opening, 7, (lead.begin_z, 0, total))
        at(midway, 0, (lead.begin_z, 3, total))
        at(midway, 1, (rest_second, 3))
        at(midway, 3, (rest.begin_third, 1))
        at(midway, 5, (rest.begin_third, 2))
        at(midway, 7, (rest.begin_z, 1, total_rest))
        at(closing, 1, (rest_second, 0))
        at(closing, 3, (rest.begin_z, 3, total_rest))
        at(closing, 5, (rest.begin_third, 0))

    def side_copy(k):
        source = mixture_hbm if k == 0 else active_hbm.at[:, pl.ds((k - 1) * width, width)]
        return pltpu.make_async_copy(source, side.at[k % 2], side_sem.at[k % 2])

    @pl.when(opening & (step == last))
    def _():
        side_copy(0).start()
        side_copy(1).start()

    @pl.when(opening)
    def _():
        grad_after = grad_ref[...]
        branch = grad_after.astype(bf16)
        branch_all[here, :] = branch
        hidden_backward(branch, w_down, slope_ref, hidden_all.at[here, :])
        grad_second = dot_nt(hidden_all[here, :], w_up[...])
        hat, scale = normalise(middle_ref[...])
        second_all[here, :] = (hat * norm_ref[2:3] + norm_ref[3:4]).astype(bf16)
        grad_rows, gain, shift = norm_backward(hat, scale, norm_ref[2:3], grad_second)
        g_norm[2] += gain
        g_norm[3] += shift
        grad_middle = grad_after + grad_rows
        middle_all[here, :] = grad_middle
        attn_all[here, :] = grad_middle.astype(bf16)

    @pl.when(opening & (step == last))
    def _():
        if plan is not None:
            lead.begin_third(2)
        for start in range(0, hidden, width):
            value = dot_tn(second_all[...], hidden_all[:, start : start + width])
            store(2, 0, start, value.astype(bf16))
        if plan is not None:
            lead.begin_third(3)
        side_copy(0).wait()
        store(1, 0, 0, dot_tn(side[0], attn_all[...]).astype(bf16))
        if plan is not None:
            store_norms(plan, own, 0, g_norm, (0, 1, 2, 3))
            rest.begin_first(1)
            lead.begin_z(1, total)
        count = hidden // width
        for k in range(1, count + 1):
            if k < count:
                side_copy(k + 1).start()
            side_copy(k).wait()
            store(3, (k - 1) * width, 0, dot_tn(side[k % 2], branch_all[...]).astype(bf16))
            if plan is not None:
                if k == 1:
                    rest.begin_first(2)
                if k == 2:
                    lead.begin_z(2, total)
                    rest_second(1)
        if plan is not None:
            rest.begin_first(3)
            rest_second(2)

    @pl.when(midway)
    def _():
        hat, _ = normalise(x_ref[...].astype(f32))
        second_all[here, :] = (hat * norm_ref[0:1] + norm_ref[1:2]).astype(bf16)
        grad_mix[...] = dot_nt(attn_all[here, :], w_out[...]).astype(bf16)
        frame = weights_ref.shape[2]
        low_half = lane_halves(frame)
        for item in range(weights_ref.shape[0]):
            span = slice(item * frame, (item + 1) * frame)
            there = pl.ds(pl.multiple_of(step * tile + item * frame, frame), frame)
            units = []
            for pair in range(HEADS // 2):

                def cut(part, pair=pair, span=span):
                    start = part * width + 128 * pair
                    return packed_ref[span, start : start + 128]

                def cut_grad(pair=pair, span=span):
                    return grad_mix[span, 128 * pair : 128 * (pair + 1)]

                def put(*values, pair=pair, there=there):
                    for part, value in enumerate(values):
                        start = part * width + 128 * pair
                        hidden_all[there, start : start + 128] = value

                units.append((partial(cut, 0), partial(cut, 1), partial(cut, 2), cut_grad, put))
            attend_backward(units, scores, weights_ref.at[item], grad_scores, low_half)

    @pl.when(midway & (step == last))
    def _():
        for start in range(0, 3 * width, width):
            value = dot_tn(second_all[...], hidden_all[:, start : start + width])
            store(0, 0, start, value.astype(bf16))
        if plan is not None:
            rest.begin_first(0)
            rest.begin_third(3)
            rest.begin_z(2, total_rest)
            lead_finish()

    @pl.when(closing)
    def _():
        grad_first = dot_nt(hidden_all[here, 0 : 3 * width], w_qkv[...])
        hat, scale = normalise(x_ref[...].astype(f32))
        grad_rows, gain, shift = norm_backward(hat, scale, norm_ref[0:1], grad_first)
        g_norm[0] += gain
        g_norm[1] += shift
        before_ref[...] = middle_all[here, :] + grad_rows

    if plan is not None:

        @pl.when(closing & (step == last))
        def _():
            own_small[...] = jnp.zeros_like(own_small)
            store_norms(plan, own_small, 0, g_norm, (0,), 0)
            small.begin_first(0)
            rest.begin_z(0, total_rest)
            small.begin_second(0, lambda y, x: own_small[0, y, x, place.c])
            small.begin_third(0)
            total_small[...] = jnp.zeros_like(total_small)
            small.begin_z(0, total_small)
            small.finish(total_small)
            rest.finish(total_rest)
            unload_shard(plan, place.me, total_rest, flat0)
            norm_out[...] += total_rest[SHARD - ROW_TILE : SHARD - ROW_TILE + 8]

            @pl.when(place.z == 0)
            def _():
                norm_out[...] += total_small[0:8]


def spatial_backward(plan, x, grad, kept, weights, norms, own_next):
    packed, soft, mixture, middle, active, slope = kept
    tokens, width = x.shape
    hidden = active.shape[1]
    operands, specs, extra = weight_sources(plan, weights, norms, hidden)
    frame = soft.shape[2]
    tile = SPATIAL_TILE
    count = tokens // tile

    def opening(*rest):
        return pl.BlockSpec(rest, lambda p, i: (i + (p + 1) // 2 * (count - 1 - i),) + (0,) * (len(rest) - 1))

    def midway(*rest):
        return pl.BlockSpec(rest, lambda p, i: (p * (2 - p) * i + p // 2 * (count - 1),) + (0,) * (len(rest) - 1))

    def closing(*rest):
        return pl.BlockSpec(rest, lambda p, i: (p // 2 * i,) + (0,) * (len(rest) - 1))

    anywhere = pl.BlockSpec(memory_space=pl.ANY)
    norm_sums = (4, 8, width)
    out_specs, out_shape = [closing(tile, width)], [jax.ShapeDtypeStruct((tokens, width), f32)]
    scratch = [
        pltpu.VMEM((HEADS // 2, frame, 2 * frame), f32),
        pltpu.VMEM((HEADS // 2, frame, 2 * frame), bf16),
        pltpu.VMEM((tile, width), bf16),
        pltpu.VMEM((tokens, width), f32),
        pltpu.VMEM((tokens, width), bf16),
        pltpu.VMEM((tokens, hidden), bf16),
        pltpu.VMEM((tokens, width), bf16),
        pltpu.VMEM((tokens, width), bf16),
        pltpu.VMEM((2, tokens, width), bf16),
        pltpu.SemaphoreType.DMA((2,)),
    ]
    params = dict(vmem_limit_bytes=63 * MIB)
    if plan is None:
        grad_specs, grad_shapes = grad_outputs(plan, width, hidden)
        out_specs += grad_specs + [whole(norm_sums)]
        out_shape += grad_shapes + [jax.ShapeDtypeStruct(norm_sums, f32)]
    else:
        rows = SHARD - ROW_TILE
        for shape in ((rows, LANES), (rows, LANES), (8, LANES)):
            out_specs.append(whole(shape))
            out_shape.append(jax.ShapeDtypeStruct(shape, f32))
        scratch += [pltpu.VMEM(norm_sums, f32)] + extra + SCATTER_ROOM
        scratch += [
            pltpu.VMEM((SHARD, LANES), f32),
            pltpu.VMEM((SHARD, LANES), f32),
            pltpu.VMEM((4, 2, 2, 2, SHARD, LANES), bf16),
            pltpu.VMEM((2, 2, 2, SHARD, LANES), bf16),
            pltpu.SemaphoreType.DMA((2,)),
            pltpu.SemaphoreType.DMA((2, 6, 4)),
            pltpu.SemaphoreType.DMA((2, 6, 4)),
            pltpu.SemaphoreType.REGULAR((3, 4)),
        ]
        scratch += SMALL_ROOM
        operands, specs = operands + [own_next], specs + [anywhere]
        params |= dict(collective_id=1, has_side_effects=True)
    return pl.pallas_call(
        partial(spatial_backward_kernel, plan),
        grid=(3, count),
        in_specs=[
            pl.BlockSpec((tile, width), lambda p, i: ((p + 1) // 2 * i, 0)),
            opening(tile, width),
            midway(tile, 3 * width),
            midway(tile // frame, HEADS // 2, frame, 2 * frame),
            opening(tile, width),
            opening(tile, hidden),
            anywhere,
            anywhere,
        ]
        + specs,
        out_specs=out_specs,
        out_shape=out_shape,
        scratch_shapes=scratch,
        compiler_params=pltpu.CompilerParams(**params),
    )(x, grad, packed, soft, middle, slope, mixture, active, *operands)


def unpack(flat_weights, model_width, hidden_width):
    cut_qkv = 3 * model_width * model_width
    cut_out = 4 * model_width * model_width
    cut_up = cut_out + model_width * hidden_width
    return (
        flat_weights[:cut_qkv].reshape(model_width, 3 * model_width),
        flat_weights[cut_qkv:cut_out].reshape(model_width, model_width),
        flat_weights[cut_out:cut_up].reshape(model_width, hidden_width),
        flat_weights[cut_up:].reshape(hidden_width, model_width),
    )


def adamw(param_value, moment, second, grad_total, step_value, rate, decay_rate):
    moment_next = beta_first * moment + (1.0 - beta_first) * grad_total
    second_next = beta_second * second + (1.0 - beta_second) * grad_total * grad_total
    moment_hat = moment_next / (1.0 - beta_first**step_value)
    second_hat = second_next / (1.0 - beta_second**step_value)
    param_next = param_value - rate * (
        moment_hat / (jnp.sqrt(second_hat) + adam_floor) + decay_rate * param_value
    )
    return (param_next, moment_next, second_next)


def on_device(
    clip_tokens,
    cotangent,
    lengths,
    params,
    param_moment,
    param_second,
    norm_par,
    norm_moment,
    norm_second,
):
    clip_count, step_slots, patch_count, model_width = clip_tokens.shape
    shards = lax.axis_size("dp")
    plan = shard_plan(shards, model_width, FF) if shards == 32 else None
    x = clip_tokens.reshape(-1, model_width)
    if plan is None:
        gathered = lax.all_gather(params.astype(bf16), "dp", axis=1, tiled=True)
        norm_whole = lax.all_gather(norm_par.astype(bf16), "dp", axis=0, tiled=True)
        norm_table = norm_whole.astype(f32).reshape(2, 4, model_width)
        spatial_weights = unpack(gathered[0], model_width, FF)
        temporal_weights = unpack(gathered[1], model_width, FF)
        sources = (*spatial_weights, norm_table[0])
        *kept, after = spatial_forward(plan, x, sources, patch_count, FF)
    else:
        sources = (params.reshape(2, -1, LANES), norm_par.reshape(1, LANES))
        *kept, after, spatial_weights, temporal_weights, norm_table = spatial_forward(
            plan, x, sources, patch_count, FF
        )
        norm_table = norm_table.reshape(2, 4, model_width)
    result, grad_after, *temporal_grads, temporal_norm = temporal_block(
        plan,
        lengths,
        after.reshape(step_slots, patch_count, model_width),
        cotangent.reshape(step_slots, patch_count, model_width),
        temporal_weights,
        norm_table[1],
        FF,
    )
    grad_before, *spatial_grads, spatial_norm = spatial_backward(
        plan, x, grad_after.reshape(-1, model_width), kept, spatial_weights, norm_table[0], temporal_grads[0]
    )
    if plan is None:

        def scatter(grads):
            flat = jnp.concatenate([g.reshape(-1) for g in grads])
            return lax.psum_scatter(flat, "dp", scatter_dimension=0, tiled=True).astype(f32)

        weight_sum = jnp.stack([scatter(spatial_grads), scatter(temporal_grads)])
        norm_grad = jnp.stack([spatial_norm, temporal_norm]).sum(axis=2).reshape(-1)
        norm_sum = lax.psum_scatter(norm_grad, "dp", scatter_dimension=0, tiled=True)
    else:
        weight_sum = jnp.stack([g.reshape(-1) for g in spatial_grads])
        norm_sum = spatial_norm[0] + spatial_norm[1]
    step_value = float(STEP)
    new_params, new_moment, new_second = adamw(
        params, param_moment, param_second, weight_sum, step_value, learn_rate, weight_decay
    )
    new_norm, new_norm_moment, new_norm_second = adamw(
        norm_par, norm_moment, norm_second, norm_sum, step_value, norm_rate, 0.0
    )
    return (
        result.reshape(clip_tokens.shape),
        grad_before.reshape(clip_tokens.shape),
        new_params,
        new_moment,
        new_second,
        new_params.astype(bf16),
        new_norm,
        new_norm_moment,
        new_norm_second,
    )


def solution(mesh):
    placed = (
        P("dp", None, None, None),
        P("dp", None, None, None),
        P("dp"),
        P(None, "dp"),
        P(None, "dp"),
        P(None, "dp"),
        P("dp"),
        P("dp"),
        P("dp"),
    )
    return jax.shard_map(
        on_device,
        mesh=mesh,
        in_specs=placed,
        out_specs=(
            P("dp", None, None, None),
            P("dp", None, None, None),
            P(None, "dp"),
            P(None, "dp"),
            P(None, "dp"),
            P(None, "dp"),
            P("dp"),
            P("dp"),
            P("dp"),
        ),
        check_vma=False,
    )
```

```python
from functools import partial

import jax
import jax.numpy as jnp
from jax import lax
from jax.experimental import pallas as pl
from jax.experimental.pallas import tpu as pltpu
from jax.sharding import PartitionSpec as P

HEADS = 8
HEAD_DIM = 64
FF = 2048
STEP = 7

norm_epsilon = 1e-05
beta_first = 0.9
beta_second = 0.999
learn_rate = 0.05
norm_rate = 0.5
weight_decay = 0.1
adam_floor = 1e-08
masked_score = -1e30

bf16 = jnp.bfloat16
f32 = jnp.float32
MIB = 2**20

SPATIAL_TILE = 256
TEMPORAL_TILE = 256
PATCH_GROUP = 16


def dot_nn(left, right):
    return lax.dot_general(left, right, (((1,), (0,)), ((), ())), preferred_element_type=f32)


def dot_nt(left, right):
    return lax.dot_general(left, right, (((1,), (1,)), ((), ())), preferred_element_type=f32)


def dot_tn(left, right):
    return lax.dot_general(left, right, (((0,), (0,)), ((), ())), preferred_element_type=f32)


def normalise(rows):
    center = rows - jnp.mean(rows, axis=-1, keepdims=True)
    spread = jnp.mean(center * center, axis=-1, keepdims=True)
    scale = lax.rsqrt(spread + norm_epsilon)
    return center * scale, scale


def fold_rows(rows):
    return jnp.sum(rows.reshape(-1, 8, rows.shape[-1]), axis=0)


def norm_backward(hat, scale, gain, grad):
    weighted = grad * gain
    mean_first = jnp.mean(weighted, axis=-1, keepdims=True)
    mean_second = jnp.mean(weighted * hat, axis=-1, keepdims=True)
    grad_rows = scale * (weighted - mean_first - hat * mean_second)
    return grad_rows, fold_rows(grad * hat), fold_rows(grad)


def gelu_pair(value):
    cumulative = 0.5 + 0.5 * lax.erf(value * 0.7071067811865476)
    density = jnp.exp(-0.5 * value * value) * 0.3989422804014327
    return value * cumulative, cumulative + value * density


def lane_halves(count):
    lane = lax.broadcasted_iota(jnp.int32, (count, 2 * HEAD_DIM), 1)
    return lane < HEAD_DIM


def two_heads(pair, low_half):
    zero = jnp.zeros_like(pair)
    return jnp.concatenate([jnp.where(low_half, pair, zero), jnp.where(low_half, zero, pair)], axis=0)


def own_columns(stacked, low_half):
    rows = stacked.shape[0] // 2
    return jnp.where(low_half, stacked[:rows], stacked[rows:]).astype(bf16)


ROW_CHUNK = 64


def attend(units, scores, soft, low_half, bias):
    rows, double = scores.shape[1:]
    keys = double // 2
    for unit, (query, key, value, put) in enumerate(units):
        scaled = query() * jnp.asarray(HEAD_DIM**-0.5, bf16)
        scores[unit] = dot_nt(scaled, two_heads(key(), low_half))
    for unit in range(len(units)):
        for start in range(0, rows, ROW_CHUNK):
            span = slice(start, start + ROW_CHUNK)
            for half in range(2):
                columns = slice(half * keys, (half + 1) * keys)
                part = scores[unit, span, columns]
                if bias is not None:
                    part = part + bias[span]
                powers = jnp.exp(part - jnp.max(part, axis=-1, keepdims=True))
                part = powers * (1.0 / jnp.sum(powers, axis=-1, keepdims=True))
                soft[unit, span, columns] = part.astype(bf16)
    for unit, (query, key, value, put) in enumerate(units):
        put(dot_nn(soft[unit], two_heads(value(), low_half)).astype(bf16))


def attend_backward(units, scores, soft, grad_scores, low_half):
    rows, double = scores.shape[1:]
    keys = double // 2
    scale = jnp.asarray(HEAD_DIM**-0.5, bf16)
    for unit, (query, key, value, grad, put) in enumerate(units):
        scores[unit] = dot_nt(grad(), two_heads(value(), low_half))
    for unit in range(len(units)):
        for start in range(0, rows, ROW_CHUNK):
            span = slice(start, start + ROW_CHUNK)
            for half in range(2):
                columns = slice(half * keys, (half + 1) * keys)
                wide = soft[unit, span, columns].astype(f32)
                product = scores[unit, span, columns] * wide
                inner = jnp.sum(product, axis=-1, keepdims=True)
                grad_scores[unit, span, columns] = (product - wide * inner).astype(bf16)
    for unit, (query, key, value, grad, put) in enumerate(units):
        grad_value = own_columns(dot_tn(soft[unit], grad()), low_half)
        grad_query = dot_nn(grad_scores[unit], two_heads(key() * scale, low_half)).astype(bf16)
        grad_key = own_columns(dot_tn(grad_scores[unit], query() * scale), low_half)
        put(grad_query, grad_key, grad_value)


def feed_forward(second, w_up, w_down, active_ref, slope_ref, chunk=512):
    hidden = w_up.shape[1]
    for start in range(0, hidden, chunk):
        active, slope = gelu_pair(dot_nn(second, w_up[:, start : start + chunk]))
        active_ref[:, start : start + chunk] = active.astype(bf16)
        slope_ref[:, start : start + chunk] = slope.astype(bf16)
    return dot_nn(active_ref[...], w_down[...])


def hidden_backward(branch, w_down, slope_ref, hidden_ref, chunk=512):
    hidden = w_down.shape[0]
    for start in range(0, hidden, chunk):
        grad = dot_nt(branch, w_down[start : start + chunk, :])
        slope = slope_ref[:, start : start + chunk].astype(f32)
        hidden_ref[:, start : start + chunk] = (grad * slope).astype(bf16)


def spatial_forward_kernel(plan, x_ref, *refs):
    step, last = pl.program_id(1), pl.num_programs(1) - 1
    opening = pl.program_id(0) == 0
    if plan is None:
        w_qkv, w_out, w_up, w_down, norm_ref = refs[:5]
        refs = refs[5:]
        packed_ref, weights_ref, mixture_ref, middle_ref, active_ref, slope_ref, after_ref = refs[:7]
        scores, mixture_all = refs[7:]
    else:
        shard_ref, norm_par_ref = refs[:2]
        refs = refs[2:]
        packed_ref, weights_ref, mixture_ref, middle_ref, active_ref, slope_ref, after_ref = refs[:7]
        held_out, held_next, norm_ref = refs[7:10]
        scores, mixture_all, w_qkv, w_out, w_up, w_down, held, staged, send, recv, local = refs[10:]
        matrices = (w_qkv, w_out, w_up, w_down)
        place = Place(lax.axis_index("dp"))
        now = Gather(place, held, send.at[0], recv.at[0])
        later = Gather(place, held_next, send.at[1], recv.at[1])
        keep = pltpu.make_async_copy(held, held_out, local.at[0])

        def gathered(*planes):
            for q in planes:
                now.finish(q)
            assemble(plan, held, matrices, planes)
            assemble_norms(len(plan), held, norm_ref, planes)

        @pl.when(opening & (step == 0))
        def _():
            enter(place)
            load_shard(plan, place.me, 0, shard_ref, norm_par_ref, held.at[place.z, place.y, place.x, place.c])
            now.start_z()
            load_shard(plan, place.me, 1, shard_ref, norm_par_ref, staged)
            copy = pltpu.make_async_copy(
                staged, held_next.at[place.z, place.y, place.x, place.c], local.at[1]
            )
            copy.start()
            copy.wait()
            now.begin_first(0)
            now.begin_second(0)
            for q in range(1, 4):
                now.begin_first(q)
            later.start_z()
            now.begin_third(0)
            gathered(0)

        @pl.when(opening & (step == 1))
        def _():
            now.begin_second(1)
            now.begin_second(2)

        @pl.when(opening & (step == 2))
        def _():
            now.begin_second(3)

        @pl.when(opening & (step == 4))
        def _():
            now.begin_third(1)
            now.begin_third(2)

        @pl.when(opening & (step == 5))
        def _():
            for q in range(4):
                later.begin_first(q)

        @pl.when(opening & (step == 7))
        def _():
            now.begin_third(3)

        @pl.when(jnp.logical_not(opening) & (step == 0))
        def _():
            gathered(1, 2, 3)
            keep.start()

        for q in range(4):

            @pl.when(jnp.logical_not(opening) & (step == q + 1))
            def _(q=q):
                later.begin_second(q)

        for q in range(3):

            @pl.when(jnp.logical_not(opening) & (step == q + 5))
            def _(q=q):
                later.begin_third(q)

    tile, width = x_ref.shape
    here = pl.ds(pl.multiple_of(step * tile, tile), tile)

    @pl.when(opening)
    def _():
        hat, _ = normalise(x_ref[...].astype(f32))
        first = (hat * norm_ref[0:1] + norm_ref[1:2]).astype(bf16)
        for start in range(0, 3 * width, 512):
            packed_ref[:, start : start + 512] = dot_nn(first, w_qkv[:, start : start + 512]).astype(bf16)
        frame = weights_ref.shape[2]
        low_half = lane_halves(frame)
        for item in range(weights_ref.shape[0]):
            span = slice(item * frame, (item + 1) * frame)
            units = []
            for pair in range(HEADS // 2):

                def cut(part, pair=pair, span=span):
                    start = part * width + 128 * pair
                    return packed_ref[span, start : start + 128]

                def put(value, pair=pair, span=span):
                    mixture_ref[span, 128 * pair : 128 * (pair + 1)] = value

                units.append((partial(cut, 0), partial(cut, 1), partial(cut, 2), put))
            attend(units, scores, weights_ref.at[item], low_half, None)
        mixture_all[here, :] = mixture_ref[...]

    @pl.when(jnp.logical_not(opening))
    def _():
        middle = x_ref[...].astype(f32) + dot_nn(mixture_all[here, :], w_out[...])
        middle_ref[...] = middle
        hat, _ = normalise(middle)
        second = (hat * norm_ref[2:3] + norm_ref[3:4]).astype(bf16)
        after_ref[...] = middle + feed_forward(second, w_up, w_down, active_ref, slope_ref)

    if plan is not None:

        @pl.when(jnp.logical_not(opening) & (step == last))
        def _():
            later.begin_third(3)
            for q in range(4):
                later.finish(q)
            keep.wait()
            now.drain()
            later.drain()


def whole(shape):
    return pl.BlockSpec(shape, lambda *_: (0,) * len(shape), pipeline_mode=pl.Buffered(1))


def tiles(tile, *rest):
    return pl.BlockSpec((tile, *rest), lambda i: (i,) + (0,) * len(rest))


def spatial_forward(plan, x, sources, frame, hidden):
    tokens, width = x.shape
    tile = SPATIAL_TILE
    frames = tile // frame
    count = tokens // tile

    def opening(*rest):
        return pl.BlockSpec(rest, lambda p, i: (i + p * (count - 1 - i),) + (0,) * (len(rest) - 1))

    def closing(*rest):
        return pl.BlockSpec(rest, lambda p, i: (i * p,) + (0,) * (len(rest) - 1))

    out_specs = [
        opening(tile, 3 * width),
        opening(frames, HEADS // 2, frame, 2 * frame),
        opening(tile, width),
        closing(tile, width),
        closing(tile, hidden),
        closing(tile, hidden),
        closing(tile, width),
    ]
    out_shape = [
        jax.ShapeDtypeStruct((tokens, 3 * width), bf16),
        jax.ShapeDtypeStruct((tokens // frame, HEADS // 2, frame, 2 * frame), bf16),
        jax.ShapeDtypeStruct((tokens, width), bf16),
        jax.ShapeDtypeStruct((tokens, width), f32),
        jax.ShapeDtypeStruct((tokens, hidden), bf16),
        jax.ShapeDtypeStruct((tokens, hidden), bf16),
        jax.ShapeDtypeStruct((tokens, width), f32),
    ]
    scratch = [pltpu.VMEM((HEADS // 2, frame, 2 * frame), f32), pltpu.VMEM((tokens, width), bf16)]
    params = dict(vmem_limit_bytes=60 * MIB)
    if plan is not None:
        held = (4, 2, 2, 2, SHARD, LANES)
        out_specs += [pl.BlockSpec(memory_space=pl.ANY)] * 2 + [whole((8, width))]
        out_shape += [jax.ShapeDtypeStruct(held, bf16)] * 2 + [jax.ShapeDtypeStruct((8, width), f32)]
        scratch += [pltpu.VMEM(shape, bf16) for shape in matrix_shapes(width, hidden)]
        scratch += [
            pltpu.VMEM(held, bf16),
            pltpu.VMEM((SHARD, LANES), bf16),
            pltpu.SemaphoreType.DMA((2, 6, 4)),
            pltpu.SemaphoreType.DMA((2, 6, 4)),
            pltpu.SemaphoreType.DMA((2,)),
        ]
        params |= dict(collective_id=0, has_side_effects=True)
    return pl.pallas_call(
        partial(spatial_forward_kernel, plan),
        grid=(2, count),
        in_specs=[pl.BlockSpec((tile, width), lambda p, i: (i, 0))] + [whole(a.shape) for a in sources],
        out_specs=out_specs,
        out_shape=out_shape,
        scratch_shapes=scratch,
        compiler_params=pltpu.CompilerParams(**params),
    )(x, *sources)


MESH_IDS = pl.DeviceIdType.MESH
LANES = 128
ROW_TILE = 16


def matrix_shapes(width, hidden):
    return ((width, 3 * width), (width, width), (width, hidden), (hidden, width))


def shard_plan(shards, width, hidden):
    plan = []
    base = 0
    regions = []
    for index, (rows, columns) in enumerate(matrix_shapes(width, hidden)):
        regions.append((index, base, rows, columns))
        base += rows * columns
    if base % shards:
        return None
    size = base // shards
    for device in range(shards):
        low, high = device * size, (device + 1) * size
        halves = ([], [])
        for index, start, rows, columns in regions:
            first, last = max(low, start), min(high, start + rows * columns)
            if first >= last:
                continue
            if (first - start) % columns or (last - start) % columns:
                return None
            row, count = (first - start) // columns, (last - first) // columns
            if row % ROW_TILE or count % ROW_TILE:
                return None
            stride = columns // LANES
            for block in range(stride):
                halves[2 * block // stride].append(
                    (index, row, count, block, (first - low) // LANES + block, stride)
                )
        place = 0
        entries = []
        for item in halves[0] + halves[1]:
            entries.append(item + (place,))
            place += item[2]
        plan.append(entries)
    return plan


def by_pattern(plan):
    groups = {}
    for device, entries in enumerate(plan):
        layout = tuple((e[2], e[4], e[5], e[6]) for e in entries)
        ranges = groups.setdefault(layout, [])
        if ranges and ranges[-1][1] == device:
            ranges[-1][1] = device + 1
        else:
            ranges.append([device, device + 1])
    return list(groups.items())


def on_pattern(plan, me, body):
    for layout, ranges in by_pattern(plan):
        inside = None
        for low, high in ranges:
            test = (me >= low) & (me < high)
            inside = test if inside is None else inside | test

        @pl.when(inside)
        def _(layout=layout):
            body(layout)


class Place:
    def __init__(self, me):
        self.me = me
        self.c = lax.rem(me, 2)
        self.x = lax.rem(me // 2, 2)
        self.y = lax.rem(me // 4, 2)
        self.z = me // 8

    def device(self, z, y, x, c):
        return ((z * 2 + y) * 2 + x) * 2 + c

    @property
    def sibling(self):
        return self.device(self.z, self.y, self.x, 1 - self.c)

    @property
    def across_x(self):
        return self.device(self.z, self.y, 1 - self.x, self.c)

    @property
    def across_y(self):
        return self.device(self.z, 1 - self.y, self.x, self.c)

    def plane(self, z):
        return self.device(z, self.y, self.x, self.c)


def remote(src, dst, send, recv, device):
    return pltpu.make_async_remote_copy(
        src_ref=src, dst_ref=dst, send_sem=send, recv_sem=recv, device_id=(device,), device_id_type=MESH_IDS
    )


def enter(place):
    barrier = pltpu.get_barrier_semaphore()
    partners = [place.sibling, place.across_x, place.across_y]
    partners += [place.plane(lax.rem(place.z + k, 4)) for k in range(1, 4)]
    for device in partners:
        pl.semaphore_signal(barrier, inc=1, device_id=(device,), device_id_type=MESH_IDS)
    pl.semaphore_wait(barrier, len(partners))


HALF = 384
SHARD = 784


class Gather:
    SEMS = 9

    def __init__(self, place, held, send, recv):
        self.p, self.held, self.send, self.recv = place, held, send, recv

    def along_z(self, k):
        p = self.p
        here = self.held.at[p.z, p.y, p.x, p.c]
        return remote(here, here, self.send.at[0, k - 1], self.recv.at[0, p.z], p.plane(lax.rem(p.z + k, 4)))

    def start_z(self):
        for k in range(1, 4):
            self.along_z(k).start()

    def wait_z(self, q):
        p = self.p

        @pl.when(q != p.z)
        def _():
            there = self.held.at[q, p.y, p.x, p.c]
            remote(there, there, self.send.at[0, 0], self.recv.at[0, q], p.me).wait_recv()

    def first(self, q):
        p, h = self.p, self.held
        a = h.at[q, p.y, p.x, p.c, pl.ds(0, HALF)]
        b = h.at[q, p.y, p.x, p.c, pl.ds(HALF, SHARD - HALF)]
        return (
            remote(a, a, self.send.at[1, q], self.recv.at[1, q], p.across_x),
            remote(b, b, self.send.at[2, q], self.recv.at[2, q], p.across_y),
        )

    def second(self, q):
        p, h = self.p, self.held
        a = h.at[q, p.y, :, p.c, pl.ds(0, HALF)]
        b = h.at[q, :, p.x, p.c, pl.ds(HALF, SHARD - HALF)]
        return (
            remote(a, a, self.send.at[3, q], self.recv.at[3, q], p.across_y),
            remote(b, b, self.send.at[4, q], self.recv.at[4, q], p.across_x),
        )

    def third(self, q):
        p, h = self.p, self.held
        a = h.at[q, :, :, p.c]
        return (remote(a, a, self.send.at[5, q], self.recv.at[5, q], p.sibling),)

    def begin_first(self, q):
        self.wait_z(q)
        for copy in self.first(q):
            copy.start()

    def begin_second(self, q):
        for copy in self.first(q):
            copy.wait_recv()
        for copy in self.second(q):
            copy.start()

    def begin_third(self, q):
        for copy in self.second(q):
            copy.wait_recv()
        for copy in self.third(q):
            copy.start()

    def finish(self, q):
        for copy in self.third(q):
            copy.wait_recv()

    def drain(self):
        for k in range(1, 4):
            self.along_z(k).wait_send()
        for q in range(4):
            for copy in self.first(q) + self.second(q) + self.third(q):
                copy.wait_send()


def load_shard(plan, me, block, shard_ref, norm_ref, held_here):
    def body(layout):
        for count, flat, stride, place in layout:
            held_here[pl.ds(place, count), :] = shard_ref[pl.ds(2 * flat + block, count, 2 * stride), :].astype(bf16)

    on_pattern(plan, me, body)
    held_here[SHARD - ROW_TILE :, :] = jnp.broadcast_to(norm_ref[...], (ROW_TILE, LANES)).astype(bf16)


def coordinates(device):
    return device // 8, device // 4 % 2, device // 2 % 2, device % 2


def assemble(plan, held, outs, planes):
    for device, entries in enumerate(plan):
        z, y, x, c = coordinates(device)
        if z not in planes:
            continue
        for index, row, count, block, _, _, place in entries:
            outs[index][row : row + count, LANES * block : LANES * (block + 1)] = held[
                z, y, x, c, place : place + count, :
            ]


def assemble_norms(shards, held, norm_out, planes):
    per_row = norm_out.shape[1] // LANES
    for device in range(shards):
        z, y, x, c = coordinates(device)
        if z not in planes:
            continue
        row, column = device // per_row, device % per_row
        norm_out[row : row + 1, LANES * column : LANES * (column + 1)] = held[
            z, y, x, c, SHARD - ROW_TILE : SHARD, :
        ].astype(f32)[0:1]


def accumulate(into, part, chunk):
    def body(i, _):
        span = pl.ds(pl.multiple_of(i * chunk, ROW_TILE), chunk)
        into[span, :] = into[span, :] + part[span, :]
        return 0

    lax.fori_loop(0, into.shape[0] // chunk, body, 0)


class Scatter:
    def __init__(self, place, own, room, send, recv, credit=None, leads=None):
        self.p, self.own = place, own
        rows, half = room[3].shape[1], room[1].shape[2]
        self.low, self.high = pl.ds(0, half), pl.ds(half, rows - half)
        self.chunk, self.chunk_low, self.chunk_high = (112, 128, 80) if rows == SHARD else (ROW_TILE,) * 3
        self.r1, self.r2a, self.r2b, self.r3, self.r4 = room
        self.send, self.recv, self.credit, self.leads = send, recv, credit, leads

    def release(self, kind, q, device):
        if self.leads is True:
            pl.semaphore_signal(self.credit.at[kind, q], inc=1, device_id=(device,), device_id_type=MESH_IDS)

    def claim(self, kind, q):
        if self.leads is False:
            pl.semaphore_wait(self.credit.at[kind, q], 1)

    def first(self, q):
        p = self.p
        return (
            remote(
                self.own.at[q, :, :, 1 - p.c], self.r1.at[q], self.send.at[0, q], self.recv.at[0, q], p.sibling
            ),
        )

    def second(self, q):
        p = self.p
        low, high = self.low, self.high
        return (
            remote(
                self.r1.at[q, :, 1 - p.x, low], self.r2a.at[q], self.send.at[1, q], self.recv.at[1, q], p.across_x
            ),
            remote(
                self.r1.at[q, 1 - p.y, :, high], self.r2b.at[q], self.send.at[2, q], self.recv.at[2, q], p.across_y
            ),
        )

    def third(self, q):
        p = self.p
        low, high = self.low, self.high
        return (
            remote(
                self.r2a.at[q, 1 - p.y], self.r3.at[q, low], self.send.at[3, q], self.recv.at[3, q], p.across_y
            ),
            remote(
                self.r2b.at[q, 1 - p.x], self.r3.at[q, high], self.send.at[4, q], self.recv.at[4, q], p.across_x
            ),
        )

    def along_z(self, q):
        p = self.p
        return remote(self.r3.at[q], self.r4.at[p.z], self.send.at[5, q], self.recv.at[5, p.z], p.plane(q))

    def begin_first(self, q):
        self.claim(0, q)
        for copy in self.first(q):
            copy.start()

    def begin_second(self, q, mine):
        for copy in self.first(q):
            copy.wait_recv()
        for y in range(2):
            for x in range(2):
                accumulate(self.r1.at[q, y, x], mine(y, x), self.chunk)
        self.claim(1, q)
        self.claim(2, q)
        for copy in self.second(q):
            copy.start()

    def begin_third(self, q):
        p = self.p
        for copy in self.second(q):
            copy.wait_recv()
        low, high = self.low, self.high
        for k in range(2):
            accumulate(self.r2a.at[q, k], self.r1.at[q, k, p.x, low], self.chunk_low)
            accumulate(self.r2b.at[q, k], self.r1.at[q, p.y, k, high], self.chunk_high)
        for copy in self.third(q):
            copy.start()
        for copy in self.second(q):
            copy.wait_send()
        self.release(0, q, p.sibling)

    def begin_z(self, q, total):
        p = self.p
        for copy in self.third(q):
            copy.wait_recv()
        low, high = self.low, self.high
        accumulate(self.r3.at[q, low], self.r2a.at[q, p.y], self.chunk_low)
        accumulate(self.r3.at[q, high], self.r2b.at[q, p.x], self.chunk_high)

        @pl.when(q != p.z)
        def _():
            self.along_z(q).start()

        @pl.when(q == p.z)
        def _():
            total[...] = self.r3[q].astype(f32)

        for copy in self.third(q):
            copy.wait_send()
        self.release(1, q, p.across_x)
        self.release(2, q, p.across_y)

    def leave_z(self, q):
        p = self.p

        @pl.when(q != p.z)
        def _():
            self.along_z(q).wait_send()

    def finish(self, total):
        p = self.p
        planes = self.r3.shape[0]

        @pl.when(p.z < planes)
        def _():
            for k in range(1, 4):
                z = lax.rem(p.z + k, 4)
                remote(self.r3.at[0], self.r4.at[z], self.send.at[5, 0], self.recv.at[5, z], p.me).wait_recv()
            for k in range(1, 4):
                total[...] += self.r4[lax.rem(p.z + k, 4)].astype(f32)

        for q in range(planes):
            for copy in self.first(q):
                copy.wait_send()
            self.leave_z(q)


SCATTER_ROOM = [
    pltpu.VMEM((4, 2, 2, SHARD, LANES), bf16),
    pltpu.VMEM((4, 2, HALF, LANES), bf16),
    pltpu.VMEM((4, 2, SHARD - HALF, LANES), bf16),
    pltpu.VMEM((2, 4, SHARD, LANES), bf16),
    pltpu.VMEM((2, 4, SHARD, LANES), bf16),
]

SMALL = 2 * ROW_TILE
SMALL_ROOM = [
    pltpu.VMEM((1, 2, 2, 2, SMALL, LANES), bf16),
    pltpu.VMEM((1, 2, 2, SMALL, LANES), bf16),
    pltpu.VMEM((1, 2, ROW_TILE, LANES), bf16),
    pltpu.VMEM((1, 2, ROW_TILE, LANES), bf16),
    pltpu.VMEM((1, SMALL, LANES), bf16),
    pltpu.VMEM((4, SMALL, LANES), bf16),
    pltpu.VMEM((SMALL, LANES), f32),
    pltpu.SemaphoreType.DMA((6, 4)),
    pltpu.SemaphoreType.DMA((6, 4)),
]


def unload_shard(plan, me, block, total, flat_ref):
    def body(layout):
        for count, flat, stride, place in layout:
            flat_ref[pl.ds(2 * flat + block, count, 2 * stride), :] = total[pl.ds(place, count), :]

    on_pattern(plan, me, body)


def store_travel(plan, own, index, top, start, value):
    for device, entries in enumerate(plan):
        z, y, x, c = coordinates(device)
        for entry, row, count, block, _, _, place in entries:
            column = LANES * block - start
            low, high = max(row, top), min(row + count, top + value.shape[0])
            if entry == index and 0 <= column < value.shape[1] and low < high:
                own[z, y, x, c, place + low - row : place + high - row, :] = value[
                    low - top : high - top, column : column + LANES
                ]


def store_norms(plan, own, block, sums, planes, first=SHARD - ROW_TILE):
    width = sums.shape[2]
    per_row = width // LANES
    line = lax.broadcasted_iota(jnp.int32, (ROW_TILE, LANES), 0)
    for device in range(len(plan)):
        z, y, x, c = coordinates(device)
        if z not in planes:
            continue
        row = device // per_row - 4 * block
        if 0 <= row < 4:
            column = LANES * (device % per_row)
            value = jnp.sum(sums[row, :, column : column + LANES], axis=0, keepdims=True)
            coarse = value.astype(bf16).astype(f32)
            rows = jnp.where(line == 0, coarse, jnp.where(line == 1, value - coarse, 0.0))
        else:
            rows = jnp.zeros((ROW_TILE, LANES), f32)
        own[z, y, x, c, first : first + ROW_TILE, :] = rows.astype(bf16)


def weight_grads(first, grad_packed, mixture, attn, second, grad_hidden, active, branch, store, chunk=512):
    sides = ((first, grad_packed), (mixture, attn), (second, grad_hidden), (active, branch))
    for index, (left, right) in enumerate(sides):
        for start in range(0, right.shape[1], chunk):
            store(index, 0, start, dot_tn(left[...], right[:, start : start + chunk]).astype(bf16))


def grad_outputs(plan, width, hidden):
    shapes = matrix_shapes(width, hidden) if plan is None else [(4, 2, 2, 2, SHARD, LANES)]
    return [whole(s) for s in shapes], [jax.ShapeDtypeStruct(s, bf16) for s in shapes]


def storing(plan, outs):
    if plan is None:
        def store(index, top, start, value):
            outs[index][top : top + value.shape[0], start : start + value.shape[1]] = value
        return store
    return partial(store_travel, plan, outs[0])


def temporal_kernel(
    plan, length_ref, rows_ref, cotangent_ref, *refs
):
    sources = 5 if plan is None else 2
    refs, sources = refs[sources:], refs[:sources]
    result_ref, before_ref, *refs = refs
    if plan is None:
        w_qkv, w_out, w_up, w_down, norm_ref = sources
    else:
        *refs, w_qkv, w_out, w_up, w_down, local = refs
        norm_ref = sources[1].at[4:8]
    outs, g_norm = refs[:-15], refs[-15]
    packed, slope, weights_buf, grad_mix, scores, grad_scores = refs[-14:-8]
    first_all, packed_all, mixture_all, attn_all, second_all, hidden_all, active_all, branch_all = refs[-8:]
    step = pl.program_id(0)
    steps, patches, width = rows_ref.shape
    tile = steps * patches
    here = pl.ds(pl.multiple_of(step * tile, tile), tile)
    length = length_ref[0]
    group = PATCH_GROUP
    count = steps * group

    @pl.when(step == 0)
    def _():
        g_norm[...] = jnp.zeros_like(g_norm)
        if plan is not None:
            load_weights(plan, sources[0], outs[0], (w_qkv, w_out, w_up, w_down), local)

    row = lax.broadcasted_iota(jnp.int32, (count, count), 0)
    column = lax.broadcasted_iota(jnp.int32, (count, count), 1)
    seen = (row % group == column % group) & (column // group <= row // group)
    seen = seen & (column // group < length)
    bias = jnp.where(seen, 0.0, masked_score)
    low_half = lane_halves(count)

    rows = rows_ref[...].reshape(tile, width)
    hat, _ = normalise(rows)
    first = (hat * norm_ref[0:1] + norm_ref[1:2]).astype(bf16)
    first_all[here, :] = first
    packed[...] = dot_nn(first, w_qkv[...]).astype(bf16).reshape(packed.shape)

    mixture_view = mixture_all.at[here, :]

    def cut(source, part, place, pair):
        start = part * width + 128 * pair
        return source[:, place : place + group, start : start + 128].reshape(count, 128)

    def units_of(backward):
        units = []
        for place in range(0, patches, group):
            for pair in range(HEADS // 2):

                def put(*values, place=place, pair=pair):
                    for part, value in enumerate(values):
                        start = part * width + 128 * pair
                        into = packed if backward else grad_mix
                        into[:, place : place + group, start : start + 128] = value.reshape(steps, group, 128)

                gets = [partial(cut, packed, part, place, pair) for part in range(3)]
                if backward:
                    gets.append(partial(cut, grad_mix, 0, place, pair))
                units.append((*gets, put))
        return units

    attend(units_of(False), scores, weights_buf, low_half, bias)
    mixture = grad_mix[...].reshape(tile, width)
    mixture_all[here, :] = mixture
    middle = rows + dot_nn(mixture, w_out[...])
    hat, scale = normalise(middle)
    second = (hat * norm_ref[2:3] + norm_ref[3:4]).astype(bf16)
    second_all[here, :] = second
    after = middle + feed_forward(second, w_up, w_down, active_all.at[here, :], slope)
    result_ref[...] = after.reshape(result_ref.shape)

    slot = lax.broadcasted_iota(jnp.int32, rows_ref.shape, 0)
    live = (slot < length).astype(f32)
    grad_after = (cotangent_ref[...].astype(f32) * live).reshape(tile, width)
    branch = grad_after.astype(bf16)
    branch_all[here, :] = branch
    hidden_backward(branch, w_down, slope, hidden_all.at[here, :])
    grad_second = dot_nt(hidden_all[here, :], w_up[...])
    hat, scale = normalise(middle)
    grad_rows, gain, shift = norm_backward(hat, scale, norm_ref[2:3], grad_second)
    g_norm[2] += gain
    g_norm[3] += shift
    grad_middle = grad_after + grad_rows
    attn = grad_middle.astype(bf16)
    attn_all[here, :] = attn
    grad_mix[...] = dot_nt(attn, w_out[...]).astype(bf16).reshape(grad_mix.shape)
    attend_backward(units_of(True), scores, weights_buf, grad_scores, low_half)
    grad_packed = packed[...].reshape(tile, 3 * width)
    packed_all[here, :] = grad_packed
    grad_first = dot_nt(grad_packed, w_qkv[...])
    hat, scale = normalise(rows)
    grad_rows, gain, shift = norm_backward(hat, scale, norm_ref[0:1], grad_first)
    g_norm[0] += gain
    g_norm[1] += shift
    before_ref[...] = (grad_middle + grad_rows).reshape(before_ref.shape)

    @pl.when(step == pl.num_programs(0) - 1)
    def _():
        if plan is not None:
            store_norms(plan, outs[0], 1, g_norm, range(4))
        weight_grads(
            first_all, packed_all, mixture_all, attn_all, second_all, hidden_all, active_all,
            branch_all, storing(plan, outs),
        )


def load_weights(plan, held, room, matrices, local):
    copy = pltpu.make_async_copy(held, room, local.at[0])
    copy.start()
    copy.wait()
    assemble(plan, room, matrices, range(4))


def weight_sources(plan, weights, norms, hidden):
    width = norms.shape[1]
    if plan is None:
        return [*weights, norms], [whole(a.shape) for a in (*weights, norms)], []
    scratch = [pltpu.VMEM(shape, bf16) for shape in matrix_shapes(width, hidden)]
    scratch.append(pltpu.SemaphoreType.DMA((1,)))
    return [weights, norms], [pl.BlockSpec(memory_space=pl.ANY), whole(norms.shape)], scratch


def temporal_block(plan, length, rows, cotangent, weights, norms, hidden):
    grad_specs, grad_shapes = grad_outputs(plan, norms.shape[1], hidden)
    operands, specs, extra = weight_sources(plan, weights, norms, hidden)
    steps, patches, width = rows.shape
    tokens = steps * patches
    part = TEMPORAL_TILE // steps
    count = steps * PATCH_GROUP
    unit_shape = (part // PATCH_GROUP * (HEADS // 2), count, 2 * count)
    slab = pl.BlockSpec((steps, part, width), lambda i: (0, i, 0))
    return pl.pallas_call(
        partial(temporal_kernel, plan),
        grid=(patches // part,),
        in_specs=[pl.BlockSpec(memory_space=pltpu.SMEM), slab, slab] + specs,
        out_specs=[slab, slab] + grad_specs + [whole((4, 8, width))],
        out_shape=[
            jax.ShapeDtypeStruct(rows.shape, f32),
            jax.ShapeDtypeStruct(rows.shape, f32),
        ]
        + grad_shapes
        + [jax.ShapeDtypeStruct((4, 8, width), f32)],
        scratch_shapes=[
            pltpu.VMEM((steps, part, 3 * width), bf16),
            pltpu.VMEM((TEMPORAL_TILE, hidden), bf16),
            pltpu.VMEM(unit_shape, bf16),
            pltpu.VMEM((steps, part, width), bf16),
            pltpu.VMEM(unit_shape, f32),
            pltpu.VMEM(unit_shape, bf16),
            pltpu.VMEM((tokens, width), bf16),
            pltpu.VMEM((tokens, 3 * width), bf16),
            pltpu.VMEM((tokens, width), bf16),
            pltpu.VMEM((tokens, width), bf16),
            pltpu.VMEM((tokens, width), bf16),
            pltpu.VMEM((tokens, hidden), bf16),
            pltpu.VMEM((tokens, hidden), bf16),
            pltpu.VMEM((tokens, width), bf16),
        ]
        + extra,
        compiler_params=pltpu.CompilerParams(vmem_limit_bytes=62 * MIB),
    )(length, rows, cotangent, *operands)


def spatial_backward_kernel(
    plan, x_ref, grad_ref, packed_ref, weights_ref, middle_ref, slope_ref, mixture_hbm, active_hbm, *refs
):
    step, last = pl.program_id(1), pl.num_programs(1) - 1
    opening, midway, closing = [pl.program_id(0) == k for k in range(3)]
    if plan is None:
        w_qkv, w_out, w_up, w_down, norm_ref, before_ref, *outs, g_norm = refs[:11]
        refs = refs[11:]
    else:
        held, norm_ref, own_next, before_ref, flat, norm_out = refs[:6]
        own_small, *room_small, total_small, send_small, recv_small = refs[-len(SMALL_ROOM) :]
        *refs, total, total_rest, own, mine, load, send, recv, credit = refs[6 : -len(SMALL_ROOM)]
        room, refs = refs[-5:], refs[:-5]
        *refs, g_norm, w_qkv, w_out, w_up, w_down, local = refs
        outs = [own]
        place = Place(lax.axis_index("dp"))
        rooms = [(*room[:3], room[3].at[k], room[4].at[k]) for k in range(2)]
        lead = Scatter(place, own_next, rooms[0], send.at[0], recv.at[0], credit, True)
        rest = Scatter(place, own, rooms[1], send.at[1], recv.at[1], credit, False)
        small = Scatter(place, own_small, room_small, send_small, recv_small)
    scores, grad_scores, grad_mix, middle_all, second_all, hidden_all, attn_all, branch_all, side, side_sem = refs
    store = storing(plan, outs)
    tile, width = x_ref.shape
    hidden = slope_ref.shape[1]
    here = pl.ds(pl.multiple_of(step * tile, tile), tile)

    def own_shards(q):
        return pltpu.make_async_copy(own_next.at[q, :, :, place.c], mine.at[q % 2], load.at[q % 2])

    def lead_second(q):
        own_shards(q).wait()
        lead.begin_second(q, lambda y, x: mine.at[q % 2, y, x])
        if q < 2:
            own_shards(q + 2).start()

    def rest_second(q):
        rest.begin_second(q, lambda y, x: own.at[q, y, x, place.c])

    def at(passing, when, *actions):
        @pl.when(passing & (step == when))
        def _():
            for action, *q in actions:
                action(*q)

    def begin():
        enter(place)
        for q in range(4):
            lead.begin_first(q)
        own_shards(0).start()
        own_shards(1).start()
        load_weights(plan, held, own, (w_qkv, w_out, w_up, w_down), local)

    def lead_finish():
        lead.finish(total)
        unload_shard(plan, place.me, 1, total, flat)
        norm_out[...] = total[SHARD - ROW_TILE : SHARD - ROW_TILE + 8]

    @pl.when(opening & (step == 0))
    def _():
        g_norm[...] = jnp.zeros_like(g_norm)

    if plan is not None:
        at(opening, 0, (begin,))
        at(opening, 1, (lead_second, 0))
        at(opening, 2, (lead_second, 1))
        at(opening, 4, (lead.begin_third, 0))
        at(opening, 5, (lead_second, 2))
        at(opening, 6, (lead.begin_third, 1))
        at(opening, 7, (lead_second, 3))
        at(midway, 0, (lead.begin_z, 3, total), (rest_second, 2))
        at(midway, 2, (rest_second, 3))
        at(midway, 4, (rest.begin_third, 1))
        at(midway, 6, (rest.begin_third, 2))
        at(midway, 7, (rest.begin_z, 1, total_rest))
        at(closing, 1, (rest_second, 0))
        at(closing, 4, (rest.begin_z, 3, total_rest))
        at(closing, 7, (rest.begin_third, 0))

    def side_copy(k):
        source = mixture_hbm if k == 0 else active_hbm.at[:, pl.ds((k - 1) * width, width)]
        return pltpu.make_async_copy(source, side.at[k % 2], side_sem.at[k % 2])

    @pl.when(opening & (step == last))
    def _():
        side_copy(0).start()
        side_copy(1).start()

    @pl.when(opening)
    def _():
        grad_after = grad_ref[...]
        branch = grad_after.astype(bf16)
        branch_all[here, :] = branch
        hidden_backward(branch, w_down, slope_ref, hidden_all.at[here, :])
        grad_second = dot_nt(hidden_all[here, :], w_up[...])
        hat, scale = normalise(middle_ref[...])
        second_all[here, :] = (hat * norm_ref[2:3] + norm_ref[3:4]).astype(bf16)
        grad_rows, gain, shift = norm_backward(hat, scale, norm_ref[2:3], grad_second)
        g_norm[2] += gain
        g_norm[3] += shift
        grad_middle = grad_after + grad_rows
        middle_all[here, :] = grad_middle
        attn_all[here, :] = grad_middle.astype(bf16)

    @pl.when(opening & (step == last))
    def _():
        for start in range(0, hidden, width):
            value = dot_tn(second_all[...], hidden_all[:, start : start + width])
            store(2, 0, start, value.astype(bf16))
            if plan is not None and start == width:
                lead.begin_third(2)
                lead.begin_z(0, total)
        if plan is not None:
            lead.begin_z(1, total)
        side_copy(0).wait()
        store(1, 0, 0, dot_tn(side[0], attn_all[...]).astype(bf16))
        if plan is not None:
            store_norms(plan, own, 0, g_norm, (0, 1, 2, 3))
            rest.begin_first(1)
        count = hidden // width
        for k in range(1, count + 1):
            if k < count:
                side_copy(k + 1).start()
            side_copy(k).wait()
            store(3, (k - 1) * width, 0, dot_tn(side[k % 2], branch_all[...]).astype(bf16))
            if plan is not None:
                if k == 1:
                    rest.begin_first(2)
                    lead.begin_third(3)
                if k == 2:
                    lead.begin_z(2, total)
                if k == 3:
                    rest_second(1)
        if plan is not None:
            rest.begin_first(3)

    @pl.when(midway)
    def _():
        hat, _ = normalise(x_ref[...].astype(f32))
        second_all[here, :] = (hat * norm_ref[0:1] + norm_ref[1:2]).astype(bf16)
        grad_mix[...] = dot_nt(attn_all[here, :], w_out[...]).astype(bf16)
        frame = weights_ref.shape[2]
        low_half = lane_halves(frame)
        for item in range(weights_ref.shape[0]):
            span = slice(item * frame, (item + 1) * frame)
            there = pl.ds(pl.multiple_of(step * tile + item * frame, frame), frame)
            units = []
            for pair in range(HEADS // 2):

                def cut(part, pair=pair, span=span):
                    start = part * width + 128 * pair
                    return packed_ref[span, start : start + 128]

                def cut_grad(pair=pair, span=span):
                    return grad_mix[span, 128 * pair : 128 * (pair + 1)]

                def put(*values, pair=pair, there=there):
                    for part, value in enumerate(values):
                        start = part * width + 128 * pair
                        hidden_all[there, start : start + 128] = value

                units.append((partial(cut, 0), partial(cut, 1), partial(cut, 2), cut_grad, put))
            attend_backward(units, scores, weights_ref.at[item], grad_scores, low_half)

    @pl.when(midway & (step == last))
    def _():
        for start in range(0, 3 * width, width):
            value = dot_tn(second_all[...], hidden_all[:, start : start + width])
            store(0, 0, start, value.astype(bf16))
        if plan is not None:
            rest.begin_first(0)
            rest.begin_third(3)
            rest.begin_z(2, total_rest)
            lead_finish()

    @pl.when(closing)
    def _():
        grad_first = dot_nt(hidden_all[here, 0 : 3 * width], w_qkv[...])
        hat, scale = normalise(x_ref[...].astype(f32))
        grad_rows, gain, shift = norm_backward(hat, scale, norm_ref[0:1], grad_first)
        g_norm[0] += gain
        g_norm[1] += shift
        before_ref[...] = middle_all[here, :] + grad_rows

    if plan is not None:

        @pl.when(closing & (step == last))
        def _():
            own_small[...] = jnp.zeros_like(own_small)
            store_norms(plan, own_small, 0, g_norm, (0,), 0)
            small.begin_first(0)
            rest.begin_z(0, total_rest)
            small.begin_second(0, lambda y, x: own_small.at[0, y, x, place.c])
            small.begin_third(0)
            total_small[...] = jnp.zeros_like(total_small)
            small.begin_z(0, total_small)
            small.finish(total_small)
            rest.finish(total_rest)
            unload_shard(plan, place.me, 0, total_rest, flat)
            norm_out[...] += total_rest[SHARD - ROW_TILE : SHARD - ROW_TILE + 8]

            @pl.when(place.z == 0)
            def _():
                norm_out[...] += total_small[0:8]


def spatial_backward(plan, x, grad, kept, weights, norms, own_next):
    packed, soft, mixture, middle, active, slope = kept
    tokens, width = x.shape
    hidden = active.shape[1]
    operands, specs, extra = weight_sources(plan, weights, norms, hidden)
    frame = soft.shape[2]
    tile = SPATIAL_TILE
    count = tokens // tile

    def opening(*rest):
        return pl.BlockSpec(rest, lambda p, i: (i + (p + 1) // 2 * (count - 1 - i),) + (0,) * (len(rest) - 1))

    def midway(*rest):
        return pl.BlockSpec(rest, lambda p, i: (p * (2 - p) * i + p // 2 * (count - 1),) + (0,) * (len(rest) - 1))

    def closing(*rest):
        return pl.BlockSpec(rest, lambda p, i: (p // 2 * i,) + (0,) * (len(rest) - 1))

    anywhere = pl.BlockSpec(memory_space=pl.ANY)
    norm_sums = (4, 8, width)
    out_specs, out_shape = [closing(tile, width)], [jax.ShapeDtypeStruct((tokens, width), f32)]
    scratch = [
        pltpu.VMEM((HEADS // 2, frame, 2 * frame), f32),
        pltpu.VMEM((HEADS // 2, frame, 2 * frame), bf16),
        pltpu.VMEM((tile, width), bf16),
        pltpu.VMEM((tokens, width), f32),
        pltpu.VMEM((tokens, width), bf16),
        pltpu.VMEM((tokens, hidden), bf16),
        pltpu.VMEM((tokens, width), bf16),
        pltpu.VMEM((tokens, width), bf16),
        pltpu.VMEM((2, tokens, width), bf16),
        pltpu.SemaphoreType.DMA((2,)),
    ]
    params = dict(vmem_limit_bytes=63 * MIB)
    if plan is None:
        grad_specs, grad_shapes = grad_outputs(plan, width, hidden)
        out_specs += grad_specs + [whole(norm_sums)]
        out_shape += grad_shapes + [jax.ShapeDtypeStruct(norm_sums, f32)]
    else:
        rows = SHARD - ROW_TILE
        for shape in ((2 * rows, LANES), (8, LANES)):
            out_specs.append(whole(shape))
            out_shape.append(jax.ShapeDtypeStruct(shape, f32))
        scratch += [pltpu.VMEM(norm_sums, f32)] + extra + SCATTER_ROOM
        scratch += [
            pltpu.VMEM((SHARD, LANES), f32),
            pltpu.VMEM((SHARD, LANES), f32),
            pltpu.VMEM((4, 2, 2, 2, SHARD, LANES), bf16),
            pltpu.VMEM((2, 2, 2, SHARD, LANES), bf16),
            pltpu.SemaphoreType.DMA((2,)),
            pltpu.SemaphoreType.DMA((2, 6, 4)),
            pltpu.SemaphoreType.DMA((2, 6, 4)),
            pltpu.SemaphoreType.REGULAR((3, 4)),
        ]
        scratch += SMALL_ROOM
        operands, specs = operands + [own_next], specs + [anywhere]
        params |= dict(collective_id=1, has_side_effects=True)
    return pl.pallas_call(
        partial(spatial_backward_kernel, plan),
        grid=(3, count),
        in_specs=[
            pl.BlockSpec((tile, width), lambda p, i: ((p + 1) // 2 * i, 0)),
            opening(tile, width),
            midway(tile, 3 * width),
            midway(tile // frame, HEADS // 2, frame, 2 * frame),
            opening(tile, width),
            opening(tile, hidden),
            anywhere,
            anywhere,
        ]
        + specs,
        out_specs=out_specs,
        out_shape=out_shape,
        scratch_shapes=scratch,
        compiler_params=pltpu.CompilerParams(**params),
    )(x, grad, packed, soft, middle, slope, mixture, active, *operands)


def unpack(flat_weights, model_width, hidden_width):
    cut_qkv = 3 * model_width * model_width
    cut_out = 4 * model_width * model_width
    cut_up = cut_out + model_width * hidden_width
    return (
        flat_weights[:cut_qkv].reshape(model_width, 3 * model_width),
        flat_weights[cut_qkv:cut_out].reshape(model_width, model_width),
        flat_weights[cut_out:cut_up].reshape(model_width, hidden_width),
        flat_weights[cut_up:].reshape(hidden_width, model_width),
    )


def adamw(param_value, moment, second, grad_total, step_value, rate, decay_rate):
    moment_next = beta_first * moment + (1.0 - beta_first) * grad_total
    second_next = beta_second * second + (1.0 - beta_second) * grad_total * grad_total
    moment_hat = moment_next / (1.0 - beta_first**step_value)
    second_hat = second_next / (1.0 - beta_second**step_value)
    param_next = param_value - rate * (
        moment_hat / (jnp.sqrt(second_hat) + adam_floor) + decay_rate * param_value
    )
    return (param_next, moment_next, second_next)


def interleave(pair):
    return pair.reshape(2, -1, LANES).swapaxes(0, 1).reshape(-1, LANES)


def separate(rows):
    return rows.reshape(-1, 2, LANES).swapaxes(0, 1).reshape(2, -1)


def on_device(
    clip_tokens,
    cotangent,
    lengths,
    params,
    param_moment,
    param_second,
    norm_par,
    norm_moment,
    norm_second,
):
    clip_count, step_slots, patch_count, model_width = clip_tokens.shape
    shards = lax.axis_size("dp")
    plan = shard_plan(shards, model_width, FF) if shards == 32 else None
    x = clip_tokens.reshape(-1, model_width)
    if plan is None:
        gathered = lax.all_gather(params.astype(bf16), "dp", axis=1, tiled=True)
        norm_whole = lax.all_gather(norm_par.astype(bf16), "dp", axis=0, tiled=True)
        norm_table = norm_whole.astype(f32).reshape(2, 4, model_width)
        spatial_weights = unpack(gathered[0], model_width, FF)
        temporal_weights = unpack(gathered[1], model_width, FF)
        sources = (*spatial_weights, norm_table[0])
        *kept, after = spatial_forward(plan, x, sources, patch_count, FF)
    else:
        sources = (interleave(params), norm_par.reshape(1, LANES))
        *kept, after, spatial_weights, temporal_weights, norm_table = spatial_forward(
            plan, x, sources, patch_count, FF
        )
    result, grad_after, *temporal_grads, temporal_norm = temporal_block(
        plan,
        lengths,
        after.reshape(step_slots, patch_count, model_width),
        cotangent.reshape(step_slots, patch_count, model_width),
        temporal_weights,
        norm_table[1] if plan is None else norm_table,
        FF,
    )
    grad_before, *spatial_grads, spatial_norm = spatial_backward(
        plan, x, grad_after.reshape(-1, model_width), kept, spatial_weights, norm_table[0] if plan is None else norm_table,
        temporal_grads[0],
    )
    if plan is None:

        def scatter(grads):
            flat = jnp.concatenate([g.reshape(-1) for g in grads])
            return lax.psum_scatter(flat, "dp", scatter_dimension=0, tiled=True).astype(f32)

        weight_sum = jnp.stack([scatter(spatial_grads), scatter(temporal_grads)])
        norm_grad = jnp.stack([spatial_norm, temporal_norm]).sum(axis=2).reshape(-1)
        norm_sum = lax.psum_scatter(norm_grad, "dp", scatter_dimension=0, tiled=True)
    else:
        weight_sum = spatial_grads[0]
        norm_sum = spatial_norm[0] + spatial_norm[1]
    step_value = float(STEP)
    state = (params, param_moment, param_second)
    if plan is None:
        updated = adamw(*state, weight_sum, step_value, learn_rate, weight_decay)
        new_copy = updated[0].astype(bf16)
    else:
        state = lax.optimization_barrier([interleave(part) for part in state])
        updated = adamw(*state, weight_sum, step_value, learn_rate, weight_decay)
        new_copy = separate(updated[0].astype(bf16))
        updated = [separate(part) for part in updated]
    new_params, new_moment, new_second = updated
    new_norm, new_norm_moment, new_norm_second = adamw(
        norm_par, norm_moment, norm_second, norm_sum, step_value, norm_rate, 0.0
    )
    return (
        result.reshape(clip_tokens.shape),
        grad_before.reshape(clip_tokens.shape),
        new_params,
        new_moment,
        new_second,
        new_copy,
        new_norm,
        new_norm_moment,
        new_norm_second,
    )


def solution(mesh):
    placed = (
        P("dp", None, None, None),
        P("dp", None, None, None),
        P("dp"),
        P(None, "dp"),
        P(None, "dp"),
        P(None, "dp"),
        P("dp"),
        P("dp"),
        P("dp"),
    )
    return jax.shard_map(
        on_device,
        mesh=mesh,
        in_specs=placed,
        out_specs=(
            P("dp", None, None, None),
            P("dp", None, None, None),
            P(None, "dp"),
            P(None, "dp"),
            P(None, "dp"),
            P(None, "dp"),
            P("dp"),
            P("dp"),
            P("dp"),
        ),
        check_vma=False,
    )
```

```python
from functools import partial

import jax
import jax.numpy as jnp
from jax import lax
from jax.experimental import pallas as pl
from jax.experimental.pallas import tpu as pltpu
from jax.sharding import PartitionSpec as P

HEADS = 8
HEAD_DIM = 64
FF = 2048
STEP = 7

norm_epsilon = 1e-05
beta_first = 0.9
beta_second = 0.999
learn_rate = 0.05
norm_rate = 0.5
weight_decay = 0.1
adam_floor = 1e-08
masked_score = -1e30

bf16 = jnp.bfloat16
f32 = jnp.float32
MIB = 2**20

SPATIAL_TILE = 256
TEMPORAL_TILE = 256
PATCH_GROUP = 16


def dot_nn(left, right):
    return lax.dot_general(left, right, (((1,), (0,)), ((), ())), preferred_element_type=f32)


def dot_nt(left, right):
    return lax.dot_general(left, right, (((1,), (1,)), ((), ())), preferred_element_type=f32)


def dot_tn(left, right):
    return lax.dot_general(left, right, (((0,), (0,)), ((), ())), preferred_element_type=f32)


def normalise(rows):
    center = rows - jnp.mean(rows, axis=-1, keepdims=True)
    spread = jnp.mean(center * center, axis=-1, keepdims=True)
    scale = lax.rsqrt(spread + norm_epsilon)
    return center * scale, scale


def fold_rows(rows):
    return jnp.sum(rows.reshape(-1, 8, rows.shape[-1]), axis=0)


def norm_backward(hat, scale, gain, grad):
    weighted = grad * gain
    mean_first = jnp.mean(weighted, axis=-1, keepdims=True)
    mean_second = jnp.mean(weighted * hat, axis=-1, keepdims=True)
    grad_rows = scale * (weighted - mean_first - hat * mean_second)
    return grad_rows, fold_rows(grad * hat), fold_rows(grad)


def gelu_pair(value):
    cumulative = 0.5 + 0.5 * lax.erf(value * 0.7071067811865476)
    density = jnp.exp(-0.5 * value * value) * 0.3989422804014327
    return value * cumulative, cumulative + value * density


def lane_halves(count):
    lane = lax.broadcasted_iota(jnp.int32, (count, 2 * HEAD_DIM), 1)
    return lane < HEAD_DIM


def two_heads(pair, low_half):
    zero = jnp.zeros_like(pair)
    return jnp.concatenate([jnp.where(low_half, pair, zero), jnp.where(low_half, zero, pair)], axis=0)


def own_columns(stacked, low_half):
    rows = stacked.shape[0] // 2
    return jnp.where(low_half, stacked[:rows], stacked[rows:]).astype(bf16)


ROW_CHUNK = 64


def attend(units, scores, soft, low_half, bias):
    rows, double = scores.shape[1:]
    keys = double // 2
    for unit, (query, key, value, put) in enumerate(units):
        scaled = query() * jnp.asarray(HEAD_DIM**-0.5, bf16)
        scores[unit] = dot_nt(scaled, two_heads(key(), low_half))
    for unit in range(len(units)):
        for start in range(0, rows, ROW_CHUNK):
            span = slice(start, start + ROW_CHUNK)
            for half in range(2):
                columns = slice(half * keys, (half + 1) * keys)
                part = scores[unit, span, columns]
                if bias is not None:
                    part = part + bias[span]
                powers = jnp.exp(part - jnp.max(part, axis=-1, keepdims=True))
                part = powers * (1.0 / jnp.sum(powers, axis=-1, keepdims=True))
                soft[unit, span, columns] = part.astype(bf16)
    for unit, (query, key, value, put) in enumerate(units):
        put(dot_nn(soft[unit], two_heads(value(), low_half)).astype(bf16))


def attend_backward(units, scores, soft, grad_scores, low_half):
    rows, double = scores.shape[1:]
    keys = double // 2
    scale = jnp.asarray(HEAD_DIM**-0.5, bf16)
    for unit, (query, key, value, grad, put) in enumerate(units):
        scores[unit] = dot_nt(grad(), two_heads(value(), low_half))
    for unit in range(len(units)):
        for start in range(0, rows, ROW_CHUNK):
            span = slice(start, start + ROW_CHUNK)
            for half in range(2):
                columns = slice(half * keys, (half + 1) * keys)
                wide = soft[unit, span, columns].astype(f32)
                product = scores[unit, span, columns] * wide
                inner = jnp.sum(product, axis=-1, keepdims=True)
                grad_scores[unit, span, columns] = (product - wide * inner).astype(bf16)
    for unit, (query, key, value, grad, put) in enumerate(units):
        grad_value = own_columns(dot_tn(soft[unit], grad()), low_half)
        grad_query = dot_nn(grad_scores[unit], two_heads(key() * scale, low_half)).astype(bf16)
        grad_key = own_columns(dot_tn(grad_scores[unit], query() * scale), low_half)
        put(grad_query, grad_key, grad_value)


def feed_forward(second, w_up, w_down, active_ref, slope_ref, chunk=512):
    hidden = w_up.shape[1]
    for start in range(0, hidden, chunk):
        active, slope = gelu_pair(dot_nn(second, w_up[:, start : start + chunk]))
        active_ref[:, start : start + chunk] = active.astype(bf16)
        slope_ref[:, start : start + chunk] = slope.astype(bf16)
    return dot_nn(active_ref[...], w_down[...])


def hidden_backward(branch, w_down, slope_ref, hidden_ref, chunk=512):
    hidden = w_down.shape[0]
    for start in range(0, hidden, chunk):
        grad = dot_nt(branch, w_down[start : start + chunk, :])
        slope = slope_ref[:, start : start + chunk].astype(f32)
        hidden_ref[:, start : start + chunk] = (grad * slope).astype(bf16)


def spatial_forward_kernel(plan, x_ref, *refs):
    step, last = pl.program_id(1), pl.num_programs(1) - 1
    opening = pl.program_id(0) == 0
    if plan is None:
        w_qkv, w_out, w_up, w_down, norm_ref = refs[:5]
        refs = refs[5:]
        packed_ref, weights_ref, mixture_ref, middle_ref, active_ref, slope_ref, after_ref = refs[:7]
        scores, mixture_all = refs[7:]
    else:
        shard_ref, norm_par_ref = refs[:2]
        refs = refs[2:]
        packed_ref, weights_ref, mixture_ref, middle_ref, active_ref, slope_ref, after_ref = refs[:7]
        held_out, held_next, norm_ref = refs[7:10]
        scores, mixture_all, w_qkv, w_out, w_up, w_down, held, staged, send, recv, local = refs[10:]
        matrices = (w_qkv, w_out, w_up, w_down)
        place = Place(lax.axis_index("dp"))
        order = [place.z] + [k - (place.z + 4 - k) // 4 for k in range(1, 4)]
        now = Gather(place, held, send.at[0], recv.at[0])
        later = Gather(place, held_next, send.at[1], recv.at[1])
        keep = pltpu.make_async_copy(held, held_out, local.at[0])

        def gathered(*planes):
            for q in planes:
                now.finish(q)
            assemble(plan, held, matrices, planes)
            assemble_norms(len(plan), held, norm_ref, planes)

        @pl.when(opening & (step == 0))
        def _():
            enter(place)
            load_shard(plan, place.me, 0, shard_ref, norm_par_ref, held.at[place.z, place.y, place.x, place.c])
            now.start_z()
            load_shard(plan, place.me, 1, shard_ref, norm_par_ref, staged)
            copy = pltpu.make_async_copy(
                staged, held_next.at[place.z, place.y, place.x, place.c], local.at[1]
            )
            copy.start()
            copy.wait()
            now.begin_first(order[0])
            later.begin_first(order[0])
            now.begin_second(order[0])
            later.begin_second(order[0])
            now.begin_first(order[1])
            now.begin_third(order[0])
            now.begin_second(order[1])
            now.begin_third(order[1])
            now.begin_first(order[2])
            now.begin_first(order[3])
            later.start_z()
            gathered(0)

        def at(passing, when, *actions):
            @pl.when(passing & (step == when))
            def _():
                for action, k in actions:
                    action(order[k])

        closing = jnp.logical_not(opening)
        at(opening, 1, (now.begin_second, 2))
        at(opening, 2, (now.begin_second, 3))
        at(opening, 3, (now.begin_third, 2))
        at(opening, 4, (later.begin_first, 1), (later.begin_first, 2), (later.begin_first, 3))
        at(opening, 5, (now.begin_third, 3))
        at(opening, 6, (later.begin_second, 1), (later.begin_third, 0))
        at(opening, 7, (later.begin_second, 2))
        at(closing, 0, (later.begin_second, 3))
        at(closing, 1, (later.begin_third, 1))
        at(closing, 3, (later.begin_third, 2))
        at(closing, 6, (later.begin_third, 3))

        @pl.when(jnp.logical_not(opening) & (step == 0))
        def _():
            gathered(1, 2, 3)
            keep.start()

    tile, width = x_ref.shape
    here = pl.ds(pl.multiple_of(step * tile, tile), tile)

    @pl.when(opening)
    def _():
        hat, _ = normalise(x_ref[...].astype(f32))
        first = (hat * norm_ref[0:1] + norm_ref[1:2]).astype(bf16)
        for start in range(0, 3 * width, 512):
            packed_ref[:, start : start + 512] = dot_nn(first, w_qkv[:, start : start + 512]).astype(bf16)
        frame = weights_ref.shape[2]
        low_half = lane_halves(frame)
        for item in range(weights_ref.shape[0]):
            span = slice(item * frame, (item + 1) * frame)
            units = []
            for pair in range(HEADS // 2):

                def cut(part, pair=pair, span=span):
                    start = part * width + 128 * pair
                    return packed_ref[span, start : start + 128]

                def put(value, pair=pair, span=span):
                    mixture_ref[span, 128 * pair : 128 * (pair + 1)] = value

                units.append((partial(cut, 0), partial(cut, 1), partial(cut, 2), put))
            attend(units, scores, weights_ref.at[item], low_half, None)
        mixture_all[here, :] = mixture_ref[...]

    @pl.when(jnp.logical_not(opening))
    def _():
        middle = x_ref[...].astype(f32) + dot_nn(mixture_all[here, :], w_out[...])
        middle_ref[...] = middle
        hat, _ = normalise(middle)
        second = (hat * norm_ref[2:3] + norm_ref[3:4]).astype(bf16)
        after_ref[...] = middle + feed_forward(second, w_up, w_down, active_ref, slope_ref)

    if plan is not None:

        @pl.when(jnp.logical_not(opening) & (step == last))
        def _():
            for q in range(4):
                later.finish(q)
            keep.wait()
            now.drain()
            later.drain()


def whole(shape):
    return pl.BlockSpec(shape, lambda *_: (0,) * len(shape), pipeline_mode=pl.Buffered(1))


def tiles(tile, *rest):
    return pl.BlockSpec((tile, *rest), lambda i: (i,) + (0,) * len(rest))


def spatial_forward(plan, x, sources, frame, hidden):
    tokens, width = x.shape
    tile = SPATIAL_TILE
    frames = tile // frame
    count = tokens // tile

    def opening(*rest):
        return pl.BlockSpec(rest, lambda p, i: (i + p * (count - 1 - i),) + (0,) * (len(rest) - 1))

    def closing(*rest):
        return pl.BlockSpec(rest, lambda p, i: (i * p,) + (0,) * (len(rest) - 1))

    out_specs = [
        opening(tile, 3 * width),
        opening(frames, HEADS // 2, frame, 2 * frame),
        opening(tile, width),
        closing(tile, width),
        closing(tile, hidden),
        closing(tile, hidden),
        closing(tile, width),
    ]
    out_shape = [
        jax.ShapeDtypeStruct((tokens, 3 * width), bf16),
        jax.ShapeDtypeStruct((tokens // frame, HEADS // 2, frame, 2 * frame), bf16),
        jax.ShapeDtypeStruct((tokens, width), bf16),
        jax.ShapeDtypeStruct((tokens, width), f32),
        jax.ShapeDtypeStruct((tokens, hidden), bf16),
        jax.ShapeDtypeStruct((tokens, hidden), bf16),
        jax.ShapeDtypeStruct((tokens, width), f32),
    ]
    scratch = [pltpu.VMEM((HEADS // 2, frame, 2 * frame), f32), pltpu.VMEM((tokens, width), bf16)]
    params = dict(vmem_limit_bytes=60 * MIB)
    if plan is not None:
        held = (4, 2, 2, 2, SHARD, LANES)
        out_specs += [pl.BlockSpec(memory_space=pl.ANY)] * 2 + [whole((8, width))]
        out_shape += [jax.ShapeDtypeStruct(held, bf16)] * 2 + [jax.ShapeDtypeStruct((8, width), f32)]
        scratch += [pltpu.VMEM(shape, bf16) for shape in matrix_shapes(width, hidden)]
        scratch += [
            pltpu.VMEM(held, bf16),
            pltpu.VMEM((SHARD, LANES), bf16),
            pltpu.SemaphoreType.DMA((2, 6, 4)),
            pltpu.SemaphoreType.DMA((2, 6, 4)),
            pltpu.SemaphoreType.DMA((2,)),
        ]
        params |= dict(collective_id=0, has_side_effects=True)
    return pl.pallas_call(
        partial(spatial_forward_kernel, plan),
        grid=(2, count),
        in_specs=[pl.BlockSpec((tile, width), lambda p, i: (i, 0))] + [whole(a.shape) for a in sources],
        out_specs=out_specs,
        out_shape=out_shape,
        scratch_shapes=scratch,
        compiler_params=pltpu.CompilerParams(**params),
    )(x, *sources)


MESH_IDS = pl.DeviceIdType.MESH
LANES = 128
ROW_TILE = 16


def matrix_shapes(width, hidden):
    return ((width, 3 * width), (width, width), (width, hidden), (hidden, width))


def shard_plan(shards, width, hidden):
    plan = []
    base = 0
    regions = []
    for index, (rows, columns) in enumerate(matrix_shapes(width, hidden)):
        regions.append((index, base, rows, columns))
        base += rows * columns
    if base % shards:
        return None
    size = base // shards
    for device in range(shards):
        low, high = device * size, (device + 1) * size
        halves = ([], [])
        for index, start, rows, columns in regions:
            first, last = max(low, start), min(high, start + rows * columns)
            if first >= last:
                continue
            if (first - start) % columns or (last - start) % columns:
                return None
            row, count = (first - start) // columns, (last - first) // columns
            if row % ROW_TILE or count % ROW_TILE:
                return None
            stride = columns // LANES
            for block in range(stride):
                halves[2 * block // stride].append(
                    (index, row, count, block, (first - low) // LANES + block, stride)
                )
        place = 0
        entries = []
        for item in halves[0] + halves[1]:
            entries.append(item + (place,))
            place += item[2]
        plan.append(entries)
    return plan


def by_pattern(plan):
    groups = {}
    for device, entries in enumerate(plan):
        layout = tuple((e[2], e[4], e[5], e[6]) for e in entries)
        ranges = groups.setdefault(layout, [])
        if ranges and ranges[-1][1] == device:
            ranges[-1][1] = device + 1
        else:
            ranges.append([device, device + 1])
    return list(groups.items())


def on_pattern(plan, me, body):
    for layout, ranges in by_pattern(plan):
        inside = None
        for low, high in ranges:
            test = (me >= low) & (me < high)
            inside = test if inside is None else inside | test

        @pl.when(inside)
        def _(layout=layout):
            body(layout)


class Place:
    def __init__(self, me):
        self.me = me
        self.c = lax.rem(me, 2)
        self.x = lax.rem(me // 2, 2)
        self.y = lax.rem(me // 4, 2)
        self.z = me // 8

    def device(self, z, y, x, c):
        return ((z * 2 + y) * 2 + x) * 2 + c

    @property
    def sibling(self):
        return self.device(self.z, self.y, self.x, 1 - self.c)

    @property
    def across_x(self):
        return self.device(self.z, self.y, 1 - self.x, self.c)

    @property
    def across_y(self):
        return self.device(self.z, 1 - self.y, self.x, self.c)

    def plane(self, z):
        return self.device(z, self.y, self.x, self.c)


def remote(src, dst, send, recv, device):
    return pltpu.make_async_remote_copy(
        src_ref=src, dst_ref=dst, send_sem=send, recv_sem=recv, device_id=(device,), device_id_type=MESH_IDS
    )


def enter(place):
    barrier = pltpu.get_barrier_semaphore()
    partners = [place.sibling, place.across_x, place.across_y]
    partners += [place.plane(lax.rem(place.z + k, 4)) for k in range(1, 4)]
    for device in partners:
        pl.semaphore_signal(barrier, inc=1, device_id=(device,), device_id_type=MESH_IDS)
    pl.semaphore_wait(barrier, len(partners))


HALF = 384
SHARD = 784


class Gather:
    SEMS = 9

    def __init__(self, place, held, send, recv):
        self.p, self.held, self.send, self.recv = place, held, send, recv

    def along_z(self, k):
        p = self.p
        here = self.held.at[p.z, p.y, p.x, p.c]
        return remote(here, here, self.send.at[0, k - 1], self.recv.at[0, p.z], p.plane(lax.rem(p.z + k, 4)))

    def start_z(self):
        for k in range(1, 4):
            self.along_z(k).start()

    def wait_z(self, q):
        p = self.p

        @pl.when(q != p.z)
        def _():
            there = self.held.at[q, p.y, p.x, p.c]
            remote(there, there, self.send.at[0, 0], self.recv.at[0, q], p.me).wait_recv()

    def first(self, q):
        p, h = self.p, self.held
        a = h.at[q, p.y, p.x, p.c, pl.ds(0, HALF)]
        b = h.at[q, p.y, p.x, p.c, pl.ds(HALF, SHARD - HALF)]
        return (
            remote(a, a, self.send.at[1, q], self.recv.at[1, q], p.across_x),
            remote(b, b, self.send.at[2, q], self.recv.at[2, q], p.across_y),
        )

    def second(self, q):
        p, h = self.p, self.held
        a = h.at[q, p.y, :, p.c, pl.ds(0, HALF)]
        b = h.at[q, :, p.x, p.c, pl.ds(HALF, SHARD - HALF)]
        return (
            remote(a, a, self.send.at[3, q], self.recv.at[3, q], p.across_y),
            remote(b, b, self.send.at[4, q], self.recv.at[4, q], p.across_x),
        )

    def third(self, q):
        p, h = self.p, self.held
        a = h.at[q, :, :, p.c]
        return (remote(a, a, self.send.at[5, q], self.recv.at[5, q], p.sibling),)

    def begin_first(self, q):
        self.wait_z(q)
        for copy in self.first(q):
            copy.start()

    def begin_second(self, q):
        for copy in self.first(q):
            copy.wait_recv()
        for copy in self.second(q):
            copy.start()

    def begin_third(self, q):
        for copy in self.second(q):
            copy.wait_recv()
        for copy in self.third(q):
            copy.start()

    def finish(self, q):
        for copy in self.third(q):
            copy.wait_recv()

    def drain(self):
        for k in range(1, 4):
            self.along_z(k).wait_send()
        for q in range(4):
            for copy in self.first(q) + self.second(q) + self.third(q):
                copy.wait_send()


def load_shard(plan, me, block, shard_ref, norm_ref, held_here):
    def body(layout):
        for count, flat, stride, place in layout:
            held_here[pl.ds(place, count), :] = shard_ref[pl.ds(2 * flat + block, count, 2 * stride), :].astype(bf16)

    on_pattern(plan, me, body)
    held_here[SHARD - ROW_TILE :, :] = jnp.broadcast_to(norm_ref[...], (ROW_TILE, LANES)).astype(bf16)


def coordinates(device):
    return device // 8, device // 4 % 2, device // 2 % 2, device % 2


def assemble(plan, held, outs, planes):
    for device, entries in enumerate(plan):
        z, y, x, c = coordinates(device)
        if z not in planes:
            continue
        for index, row, count, block, _, _, place in entries:
            outs[index][row : row + count, LANES * block : LANES * (block + 1)] = held[
                z, y, x, c, place : place + count, :
            ]


def assemble_norms(shards, held, norm_out, planes):
    per_row = norm_out.shape[1] // LANES
    for device in range(shards):
        z, y, x, c = coordinates(device)
        if z not in planes:
            continue
        row, column = device // per_row, device % per_row
        norm_out[row : row + 1, LANES * column : LANES * (column + 1)] = held[
            z, y, x, c, SHARD - ROW_TILE : SHARD, :
        ].astype(f32)[0:1]


def accumulate(into, part, chunk):
    def body(i, _):
        span = pl.ds(pl.multiple_of(i * chunk, ROW_TILE), chunk)
        into[span, :] = into[span, :] + part[span, :]
        return 0

    lax.fori_loop(0, into.shape[0] // chunk, body, 0)


class Scatter:
    def __init__(self, place, own, room, send, recv, credit=None, leads=None):
        self.p, self.own = place, own
        rows, half = room[3].shape[1], room[1].shape[2]
        self.low, self.high = pl.ds(0, half), pl.ds(half, rows - half)
        self.chunk, self.chunk_low, self.chunk_high = (112, 128, 80) if rows == SHARD else (ROW_TILE,) * 3
        self.r1, self.r2a, self.r2b, self.r3, self.r4 = room
        self.send, self.recv, self.credit, self.leads = send, recv, credit, leads

    def release(self, kind, q, device):
        if self.leads is True:
            pl.semaphore_signal(self.credit.at[kind, q], inc=1, device_id=(device,), device_id_type=MESH_IDS)

    def claim(self, kind, q):
        if self.leads is False:
            pl.semaphore_wait(self.credit.at[kind, q], 1)

    def first(self, q):
        p = self.p
        return (
            remote(
                self.own.at[q, :, :, 1 - p.c], self.r1.at[q], self.send.at[0, q], self.recv.at[0, q], p.sibling
            ),
        )

    def second(self, q):
        p = self.p
        low, high = self.low, self.high
        return (
            remote(
                self.r1.at[q, :, 1 - p.x, low], self.r2a.at[q], self.send.at[1, q], self.recv.at[1, q], p.across_x
            ),
            remote(
                self.r1.at[q, 1 - p.y, :, high], self.r2b.at[q], self.send.at[2, q], self.recv.at[2, q], p.across_y
            ),
        )

    def third(self, q):
        p = self.p
        low, high = self.low, self.high
        return (
            remote(
                self.r2a.at[q, 1 - p.y], self.r3.at[q, low], self.send.at[3, q], self.recv.at[3, q], p.across_y
            ),
            remote(
                self.r2b.at[q, 1 - p.x], self.r3.at[q, high], self.send.at[4, q], self.recv.at[4, q], p.across_x
            ),
        )

    def along_z(self, q):
        p = self.p
        return remote(self.r3.at[q], self.r4.at[p.z], self.send.at[5, q], self.recv.at[5, p.z], p.plane(q))

    def begin_first(self, q):
        self.claim(0, q)
        for copy in self.first(q):
            copy.start()

    def begin_second(self, q, mine):
        for copy in self.first(q):
            copy.wait_recv()
        for y in range(2):
            for x in range(2):
                accumulate(self.r1.at[q, y, x], mine(y, x), self.chunk)
        self.claim(1, q)
        self.claim(2, q)
        for copy in self.second(q):
            copy.start()

    def begin_third(self, q):
        p = self.p
        for copy in self.second(q):
            copy.wait_recv()
        low, high = self.low, self.high
        for k in range(2):
            accumulate(self.r2a.at[q, k], self.r1.at[q, k, p.x, low], self.chunk_low)
            accumulate(self.r2b.at[q, k], self.r1.at[q, p.y, k, high], self.chunk_high)
        for copy in self.third(q):
            copy.start()
        for copy in self.second(q):
            copy.wait_send()
        self.release(0, q, p.sibling)

    def begin_z(self, q, total):
        p = self.p
        for copy in self.third(q):
            copy.wait_recv()
        low, high = self.low, self.high
        accumulate(self.r3.at[q, low], self.r2a.at[q, p.y], self.chunk_low)
        accumulate(self.r3.at[q, high], self.r2b.at[q, p.x], self.chunk_high)

        @pl.when(q != p.z)
        def _():
            self.along_z(q).start()

        @pl.when(q == p.z)
        def _():
            total[...] = self.r3[q].astype(f32)

        for copy in self.third(q):
            copy.wait_send()
        self.release(1, q, p.across_x)
        self.release(2, q, p.across_y)

    def leave_z(self, q):
        p = self.p

        @pl.when(q != p.z)
        def _():
            self.along_z(q).wait_send()

    def finish(self, total):
        p = self.p
        planes = self.r3.shape[0]

        @pl.when(p.z < planes)
        def _():
            for k in range(1, 4):
                z = lax.rem(p.z + k, 4)
                remote(self.r3.at[0], self.r4.at[z], self.send.at[5, 0], self.recv.at[5, z], p.me).wait_recv()
            for k in range(1, 4):
                total[...] += self.r4[lax.rem(p.z + k, 4)].astype(f32)

        for q in range(planes):
            for copy in self.first(q):
                copy.wait_send()
            self.leave_z(q)


SCATTER_ROOM = [
    pltpu.VMEM((4, 2, 2, SHARD, LANES), bf16),
    pltpu.VMEM((4, 2, HALF, LANES), bf16),
    pltpu.VMEM((4, 2, SHARD - HALF, LANES), bf16),
    pltpu.VMEM((2, 4, SHARD, LANES), bf16),
    pltpu.VMEM((2, 4, SHARD, LANES), bf16),
]

SMALL = 2 * ROW_TILE
SMALL_ROOM = [
    pltpu.VMEM((1, 2, 2, 2, SMALL, LANES), bf16),
    pltpu.VMEM((1, 2, 2, SMALL, LANES), bf16),
    pltpu.VMEM((1, 2, ROW_TILE, LANES), bf16),
    pltpu.VMEM((1, 2, ROW_TILE, LANES), bf16),
    pltpu.VMEM((1, SMALL, LANES), bf16),
    pltpu.VMEM((4, SMALL, LANES), bf16),
    pltpu.VMEM((SMALL, LANES), f32),
    pltpu.SemaphoreType.DMA((6, 4)),
    pltpu.SemaphoreType.DMA((6, 4)),
]


def unload_shard(plan, me, block, total, flat_ref):
    def body(layout):
        for count, flat, stride, place in layout:
            flat_ref[pl.ds(2 * flat + block, count, 2 * stride), :] = total[pl.ds(place, count), :]

    on_pattern(plan, me, body)


def store_travel(plan, own, index, top, start, value):
    for device, entries in enumerate(plan):
        z, y, x, c = coordinates(device)
        for entry, row, count, block, _, _, place in entries:
            column = LANES * block - start
            low, high = max(row, top), min(row + count, top + value.shape[0])
            if entry == index and 0 <= column < value.shape[1] and low < high:
                own[z, y, x, c, place + low - row : place + high - row, :] = value[
                    low - top : high - top, column : column + LANES
                ]


def store_norms(plan, own, block, sums, planes, first=SHARD - ROW_TILE):
    width = sums.shape[2]
    per_row = width // LANES
    line = lax.broadcasted_iota(jnp.int32, (ROW_TILE, LANES), 0)
    for device in range(len(plan)):
        z, y, x, c = coordinates(device)
        if z not in planes:
            continue
        row = device // per_row - 4 * block
        if 0 <= row < 4:
            column = LANES * (device % per_row)
            value = jnp.sum(sums[row, :, column : column + LANES], axis=0, keepdims=True)
            coarse = value.astype(bf16).astype(f32)
            rows = jnp.where(line == 0, coarse, jnp.where(line == 1, value - coarse, 0.0))
        else:
            rows = jnp.zeros((ROW_TILE, LANES), f32)
        own[z, y, x, c, first : first + ROW_TILE, :] = rows.astype(bf16)


def weight_grads(first, grad_packed, mixture, attn, second, grad_hidden, active, branch, store, chunk=512):
    sides = ((first, grad_packed), (mixture, attn), (second, grad_hidden), (active, branch))
    for index, (left, right) in enumerate(sides):
        for start in range(0, right.shape[1], chunk):
            store(index, 0, start, dot_tn(left[...], right[:, start : start + chunk]).astype(bf16))


def grad_outputs(plan, width, hidden):
    shapes = matrix_shapes(width, hidden) if plan is None else [(4, 2, 2, 2, SHARD, LANES)]
    return [whole(s) for s in shapes], [jax.ShapeDtypeStruct(s, bf16) for s in shapes]


def storing(plan, outs):
    if plan is None:
        def store(index, top, start, value):
            outs[index][top : top + value.shape[0], start : start + value.shape[1]] = value
        return store
    return partial(store_travel, plan, outs[0])


def temporal_kernel(
    plan, length_ref, rows_ref, cotangent_ref, *refs
):
    sources = 5 if plan is None else 2
    refs, sources = refs[sources:], refs[:sources]
    result_ref, before_ref, *refs = refs
    if plan is None:
        w_qkv, w_out, w_up, w_down, norm_ref = sources
    else:
        *refs, w_qkv, w_out, w_up, w_down, local = refs
        norm_ref = sources[1].at[4:8]
    outs, g_norm = refs[:-15], refs[-15]
    packed, slope, weights_buf, grad_mix, scores, grad_scores = refs[-14:-8]
    first_all, packed_all, mixture_all, attn_all, second_all, hidden_all, active_all, branch_all = refs[-8:]
    step = pl.program_id(0)
    steps, patches, width = rows_ref.shape
    tile = steps * patches
    here = pl.ds(pl.multiple_of(step * tile, tile), tile)
    length = length_ref[0]
    group = PATCH_GROUP
    count = steps * group

    @pl.when(step == 0)
    def _():
        g_norm[...] = jnp.zeros_like(g_norm)
        if plan is not None:
            load_weights(plan, sources[0], outs[0], (w_qkv, w_out, w_up, w_down), local)

    row = lax.broadcasted_iota(jnp.int32, (count, count), 0)
    column = lax.broadcasted_iota(jnp.int32, (count, count), 1)
    seen = (row % group == column % group) & (column // group <= row // group)
    seen = seen & (column // group < length)
    bias = jnp.where(seen, 0.0, masked_score)
    low_half = lane_halves(count)

    rows = rows_ref[...].reshape(tile, width)
    hat, _ = normalise(rows)
    first = (hat * norm_ref[0:1] + norm_ref[1:2]).astype(bf16)
    first_all[here, :] = first
    packed[...] = dot_nn(first, w_qkv[...]).astype(bf16).reshape(packed.shape)

    mixture_view = mixture_all.at[here, :]

    def cut(source, part, place, pair):
        start = part * width + 128 * pair
        return source[:, place : place + group, start : start + 128].reshape(count, 128)

    def units_of(backward):
        units = []
        for place in range(0, patches, group):
            for pair in range(HEADS // 2):

                def put(*values, place=place, pair=pair):
                    for part, value in enumerate(values):
                        start = part * width + 128 * pair
                        into = packed if backward else grad_mix
                        into[:, place : place + group, start : start + 128] = value.reshape(steps, group, 128)

                gets = [partial(cut, packed, part, place, pair) for part in range(3)]
                if backward:
                    gets.append(partial(cut, grad_mix, 0, place, pair))
                units.append((*gets, put))
        return units

    attend(units_of(False), scores, weights_buf, low_half, bias)
    mixture = grad_mix[...].reshape(tile, width)
    mixture_all[here, :] = mixture
    middle = rows + dot_nn(mixture, w_out[...])
    hat, scale = normalise(middle)
    second = (hat * norm_ref[2:3] + norm_ref[3:4]).astype(bf16)
    second_all[here, :] = second
    after = middle + feed_forward(second, w_up, w_down, active_all.at[here, :], slope)
    result_ref[...] = after.reshape(result_ref.shape)

    slot = lax.broadcasted_iota(jnp.int32, rows_ref.shape, 0)
    live = (slot < length).astype(f32)
    grad_after = (cotangent_ref[...].astype(f32) * live).reshape(tile, width)
    branch = grad_after.astype(bf16)
    branch_all[here, :] = branch
    hidden_backward(branch, w_down, slope, hidden_all.at[here, :])
    grad_second = dot_nt(hidden_all[here, :], w_up[...])
    hat, scale = normalise(middle)
    grad_rows, gain, shift = norm_backward(hat, scale, norm_ref[2:3], grad_second)
    g_norm[2] += gain
    g_norm[3] += shift
    grad_middle = grad_after + grad_rows
    attn = grad_middle.astype(bf16)
    attn_all[here, :] = attn
    grad_mix[...] = dot_nt(attn, w_out[...]).astype(bf16).reshape(grad_mix.shape)
    attend_backward(units_of(True), scores, weights_buf, grad_scores, low_half)
    grad_packed = packed[...].reshape(tile, 3 * width)
    packed_all[here, :] = grad_packed
    grad_first = dot_nt(grad_packed, w_qkv[...])
    hat, scale = normalise(rows)
    grad_rows, gain, shift = norm_backward(hat, scale, norm_ref[0:1], grad_first)
    g_norm[0] += gain
    g_norm[1] += shift
    before_ref[...] = (grad_middle + grad_rows).reshape(before_ref.shape)

    @pl.when(step == pl.num_programs(0) - 1)
    def _():
        if plan is not None:
            store_norms(plan, outs[0], 1, g_norm, range(4))
        weight_grads(
            first_all, packed_all, mixture_all, attn_all, second_all, hidden_all, active_all,
            branch_all, storing(plan, outs),
        )


def load_weights(plan, held, room, matrices, local):
    copy = pltpu.make_async_copy(held, room, local.at[0])
    copy.start()
    copy.wait()
    assemble(plan, room, matrices, range(4))


def weight_sources(plan, weights, norms, hidden):
    width = norms.shape[1]
    if plan is None:
        return [*weights, norms], [whole(a.shape) for a in (*weights, norms)], []
    scratch = [pltpu.VMEM(shape, bf16) for shape in matrix_shapes(width, hidden)]
    scratch.append(pltpu.SemaphoreType.DMA((1,)))
    return [weights, norms], [pl.BlockSpec(memory_space=pl.ANY), whole(norms.shape)], scratch


def temporal_block(plan, length, rows, cotangent, weights, norms, hidden):
    grad_specs, grad_shapes = grad_outputs(plan, norms.shape[1], hidden)
    operands, specs, extra = weight_sources(plan, weights, norms, hidden)
    steps, patches, width = rows.shape
    tokens = steps * patches
    part = TEMPORAL_TILE // steps
    count = steps * PATCH_GROUP
    unit_shape = (part // PATCH_GROUP * (HEADS // 2), count, 2 * count)
    slab = pl.BlockSpec((steps, part, width), lambda i: (0, i, 0))
    return pl.pallas_call(
        partial(temporal_kernel, plan),
        grid=(patches // part,),
        in_specs=[pl.BlockSpec(memory_space=pltpu.SMEM), slab, slab] + specs,
        out_specs=[slab, slab] + grad_specs + [whole((4, 8, width))],
        out_shape=[
            jax.ShapeDtypeStruct(rows.shape, f32),
            jax.ShapeDtypeStruct(rows.shape, f32),
        ]
        + grad_shapes
        + [jax.ShapeDtypeStruct((4, 8, width), f32)],
        scratch_shapes=[
            pltpu.VMEM((steps, part, 3 * width), bf16),
            pltpu.VMEM((TEMPORAL_TILE, hidden), bf16),
            pltpu.VMEM(unit_shape, bf16),
            pltpu.VMEM((steps, part, width), bf16),
            pltpu.VMEM(unit_shape, f32),
            pltpu.VMEM(unit_shape, bf16),
            pltpu.VMEM((tokens, width), bf16),
            pltpu.VMEM((tokens, 3 * width), bf16),
            pltpu.VMEM((tokens, width), bf16),
            pltpu.VMEM((tokens, width), bf16),
            pltpu.VMEM((tokens, width), bf16),
            pltpu.VMEM((tokens, hidden), bf16),
            pltpu.VMEM((tokens, hidden), bf16),
            pltpu.VMEM((tokens, width), bf16),
        ]
        + extra,
        compiler_params=pltpu.CompilerParams(vmem_limit_bytes=62 * MIB),
    )(length, rows, cotangent, *operands)


def spatial_backward_kernel(
    plan, x_ref, grad_ref, packed_ref, weights_ref, middle_ref, slope_ref, mixture_hbm, active_hbm, *refs
):
    step, last = pl.program_id(1), pl.num_programs(1) - 1
    opening, midway, closing = [pl.program_id(0) == k for k in range(3)]
    if plan is None:
        w_qkv, w_out, w_up, w_down, norm_ref, before_ref, *outs, g_norm = refs[:11]
        refs = refs[11:]
    else:
        held, norm_ref, own_next, before_ref, flat, norm_out = refs[:6]
        own_small, *room_small, total_small, send_small, recv_small = refs[-len(SMALL_ROOM) :]
        *refs, total, total_rest, own, mine, load, send, recv, credit = refs[6 : -len(SMALL_ROOM)]
        room, refs = refs[-5:], refs[:-5]
        *refs, g_norm, w_qkv, w_out, w_up, w_down, local = refs
        outs = [own]
        place = Place(lax.axis_index("dp"))
        rooms = [(*room[:3], room[3].at[k], room[4].at[k]) for k in range(2)]
        lead = Scatter(place, own_next, rooms[0], send.at[0], recv.at[0], credit, True)
        rest = Scatter(place, own, rooms[1], send.at[1], recv.at[1], credit, False)
        small = Scatter(place, own_small, room_small, send_small, recv_small)
    scores, grad_scores, grad_mix, middle_all, second_all, hidden_all, attn_all, branch_all, side, side_sem = refs
    store = storing(plan, outs)
    tile, width = x_ref.shape
    hidden = slope_ref.shape[1]
    here = pl.ds(pl.multiple_of(step * tile, tile), tile)

    def own_shards(q):
        return pltpu.make_async_copy(own_next.at[q, :, :, place.c], mine.at[q % 2], load.at[q % 2])

    def lead_second(q):
        own_shards(q).wait()
        lead.begin_second(q, lambda y, x: mine.at[q % 2, y, x])
        if q < 2:
            own_shards(q + 2).start()

    def rest_second(q):
        rest.begin_second(q, lambda y, x: own.at[q, y, x, place.c])

    def at(passing, when, *actions):
        @pl.when(passing & (step == when))
        def _():
            for action, *q in actions:
                action(*q)

    def begin():
        enter(place)
        for q in range(4):
            lead.begin_first(q)
        own_shards(0).start()
        own_shards(1).start()
        load_weights(plan, held, own, (w_qkv, w_out, w_up, w_down), local)

    def lead_finish():
        lead.finish(total)
        unload_shard(plan, place.me, 1, total, flat)
        norm_out[...] = total[SHARD - ROW_TILE : SHARD - ROW_TILE + 8]

    @pl.when(opening & (step == 0))
    def _():
        g_norm[...] = jnp.zeros_like(g_norm)

    if plan is not None:
        at(opening, 0, (begin,))
        at(opening, 1, (lead_second, 0))
        at(opening, 2, (lead_second, 1))
        at(opening, 4, (lead.begin_third, 0))
        at(opening, 5, (lead_second, 2))
        at(opening, 6, (lead.begin_third, 1))
        at(opening, 7, (lead_second, 3))
        at(midway, 0, (lead.begin_z, 3, total), (rest_second, 2))
        at(midway, 2, (rest_second, 3))
        at(midway, 4, (rest.begin_third, 1))
        at(midway, 6, (rest.begin_third, 2))
        at(midway, 7, (rest.begin_z, 1, total_rest))
        at(closing, 1, (rest_second, 0))
        at(closing, 4, (rest.begin_z, 3, total_rest))
        at(closing, 7, (rest.begin_third, 0))

    def side_copy(k):
        source = mixture_hbm if k == 0 else active_hbm.at[:, pl.ds((k - 1) * width, width)]
        return pltpu.make_async_copy(source, side.at[k % 2], side_sem.at[k % 2])

    @pl.when(opening & (step == last))
    def _():
        side_copy(0).start()
        side_copy(1).start()

    @pl.when(opening)
    def _():
        grad_after = grad_ref[...]
        branch = grad_after.astype(bf16)
        branch_all[here, :] = branch
        hidden_backward(branch, w_down, slope_ref, hidden_all.at[here, :])
        grad_second = dot_nt(hidden_all[here, :], w_up[...])
        hat, scale = normalise(middle_ref[...])
        second_all[here, :] = (hat * norm_ref[2:3] + norm_ref[3:4]).astype(bf16)
        grad_rows, gain, shift = norm_backward(hat, scale, norm_ref[2:3], grad_second)
        g_norm[2] += gain
        g_norm[3] += shift
        grad_middle = grad_after + grad_rows
        middle_all[here, :] = grad_middle
        attn_all[here, :] = grad_middle.astype(bf16)

    @pl.when(opening & (step == last))
    def _():
        for start in range(0, hidden, width):
            value = dot_tn(second_all[...], hidden_all[:, start : start + width])
            store(2, 0, start, value.astype(bf16))
            if plan is not None and start == width:
                lead.begin_third(2)
                lead.begin_z(0, total)
        if plan is not None:
            lead.begin_z(1, total)
        side_copy(0).wait()
        store(1, 0, 0, dot_tn(side[0], attn_all[...]).astype(bf16))
        if plan is not None:
            store_norms(plan, own, 0, g_norm, (0, 1, 2, 3))
            rest.begin_first(1)
        count = hidden // width
        for k in range(1, count + 1):
            if k < count:
                side_copy(k + 1).start()
            side_copy(k).wait()
            store(3, (k - 1) * width, 0, dot_tn(side[k % 2], branch_all[...]).astype(bf16))
            if plan is not None:
                if k == 1:
                    rest.begin_first(2)
                    lead.begin_third(3)
                if k == 2:
                    lead.begin_z(2, total)
                if k == 3:
                    rest_second(1)
        if plan is not None:
            rest.begin_first(3)

    @pl.when(midway)
    def _():
        hat, _ = normalise(x_ref[...].astype(f32))
        second_all[here, :] = (hat * norm_ref[0:1] + norm_ref[1:2]).astype(bf16)
        grad_mix[...] = dot_nt(attn_all[here, :], w_out[...]).astype(bf16)
        frame = weights_ref.shape[2]
        low_half = lane_halves(frame)
        for item in range(weights_ref.shape[0]):
            span = slice(item * frame, (item + 1) * frame)
            there = pl.ds(pl.multiple_of(step * tile + item * frame, frame), frame)
            units = []
            for pair in range(HEADS // 2):

                def cut(part, pair=pair, span=span):
                    start = part * width + 128 * pair
                    return packed_ref[span, start : start + 128]

                def cut_grad(pair=pair, span=span):
                    return grad_mix[span, 128 * pair : 128 * (pair + 1)]

                def put(*values, pair=pair, there=there):
                    for part, value in enumerate(values):
                        start = part * width + 128 * pair
                        hidden_all[there, start : start + 128] = value

                units.append((partial(cut, 0), partial(cut, 1), partial(cut, 2), cut_grad, put))
            attend_backward(units, scores, weights_ref.at[item], grad_scores, low_half)

    @pl.when(midway & (step == last))
    def _():
        for start in range(0, 3 * width, width):
            value = dot_tn(second_all[...], hidden_all[:, start : start + width])
            store(0, 0, start, value.astype(bf16))
        if plan is not None:
            rest.begin_first(0)
            rest.begin_third(3)
            rest.begin_z(2, total_rest)
            lead_finish()

    @pl.when(closing)
    def _():
        grad_first = dot_nt(hidden_all[here, 0 : 3 * width], w_qkv[...])
        hat, scale = normalise(x_ref[...].astype(f32))
        grad_rows, gain, shift = norm_backward(hat, scale, norm_ref[0:1], grad_first)
        g_norm[0] += gain
        g_norm[1] += shift
        before_ref[...] = middle_all[here, :] + grad_rows

    if plan is not None:

        @pl.when(closing & (step == last))
        def _():
            own_small[...] = jnp.zeros_like(own_small)
            store_norms(plan, own_small, 0, g_norm, (0,), 0)
            small.begin_first(0)
            rest.begin_z(0, total_rest)
            small.begin_second(0, lambda y, x: own_small.at[0, y, x, place.c])
            small.begin_third(0)
            total_small[...] = jnp.zeros_like(total_small)
            small.begin_z(0, total_small)
            small.finish(total_small)
            rest.finish(total_rest)
            unload_shard(plan, place.me, 0, total_rest, flat)
            norm_out[...] += total_rest[SHARD - ROW_TILE : SHARD - ROW_TILE + 8]

            @pl.when(place.z == 0)
            def _():
                norm_out[...] += total_small[0:8]


def spatial_backward(plan, x, grad, kept, weights, norms, own_next):
    packed, soft, mixture, middle, active, slope = kept
    tokens, width = x.shape
    hidden = active.shape[1]
    operands, specs, extra = weight_sources(plan, weights, norms, hidden)
    frame = soft.shape[2]
    tile = SPATIAL_TILE
    count = tokens // tile

    def opening(*rest):
        return pl.BlockSpec(rest, lambda p, i: (i + (p + 1) // 2 * (count - 1 - i),) + (0,) * (len(rest) - 1))

    def midway(*rest):
        return pl.BlockSpec(rest, lambda p, i: (p * (2 - p) * i + p // 2 * (count - 1),) + (0,) * (len(rest) - 1))

    def closing(*rest):
        return pl.BlockSpec(rest, lambda p, i: (p // 2 * i,) + (0,) * (len(rest) - 1))

    anywhere = pl.BlockSpec(memory_space=pl.ANY)
    norm_sums = (4, 8, width)
    out_specs, out_shape = [closing(tile, width)], [jax.ShapeDtypeStruct((tokens, width), f32)]
    scratch = [
        pltpu.VMEM((HEADS // 2, frame, 2 * frame), f32),
        pltpu.VMEM((HEADS // 2, frame, 2 * frame), bf16),
        pltpu.VMEM((tile, width), bf16),
        pltpu.VMEM((tokens, width), f32),
        pltpu.VMEM((tokens, width), bf16),
        pltpu.VMEM((tokens, hidden), bf16),
        pltpu.VMEM((tokens, width), bf16),
        pltpu.VMEM((tokens, width), bf16),
        pltpu.VMEM((2, tokens, width), bf16),
        pltpu.SemaphoreType.DMA((2,)),
    ]
    params = dict(vmem_limit_bytes=63 * MIB)
    if plan is None:
        grad_specs, grad_shapes = grad_outputs(plan, width, hidden)
        out_specs += grad_specs + [whole(norm_sums)]
        out_shape += grad_shapes + [jax.ShapeDtypeStruct(norm_sums, f32)]
    else:
        rows = SHARD - ROW_TILE
        for shape in ((2 * rows, LANES), (8, LANES)):
            out_specs.append(whole(shape))
            out_shape.append(jax.ShapeDtypeStruct(shape, f32))
        scratch += [pltpu.VMEM(norm_sums, f32)] + extra + SCATTER_ROOM
        scratch += [
            pltpu.VMEM((SHARD, LANES), f32),
            pltpu.VMEM((SHARD, LANES), f32),
            pltpu.VMEM((4, 2, 2, 2, SHARD, LANES), bf16),
            pltpu.VMEM((2, 2, 2, SHARD, LANES), bf16),
            pltpu.SemaphoreType.DMA((2,)),
            pltpu.SemaphoreType.DMA((2, 6, 4)),
            pltpu.SemaphoreType.DMA((2, 6, 4)),
            pltpu.SemaphoreType.REGULAR((3, 4)),
        ]
        scratch += SMALL_ROOM
        operands, specs = operands + [own_next], specs + [anywhere]
        params |= dict(collective_id=1, has_side_effects=True)
    return pl.pallas_call(
        partial(spatial_backward_kernel, plan),
        grid=(3, count),
        in_specs=[
            pl.BlockSpec((tile, width), lambda p, i: ((p + 1) // 2 * i, 0)),
            opening(tile, width),
            midway(tile, 3 * width),
            midway(tile // frame, HEADS // 2, frame, 2 * frame),
            opening(tile, width),
            opening(tile, hidden),
            anywhere,
            anywhere,
        ]
        + specs,
        out_specs=out_specs,
        out_shape=out_shape,
        scratch_shapes=scratch,
        compiler_params=pltpu.CompilerParams(**params),
    )(x, grad, packed, soft, middle, slope, mixture, active, *operands)


def unpack(flat_weights, model_width, hidden_width):
    cut_qkv = 3 * model_width * model_width
    cut_out = 4 * model_width * model_width
    cut_up = cut_out + model_width * hidden_width
    return (
        flat_weights[:cut_qkv].reshape(model_width, 3 * model_width),
        flat_weights[cut_qkv:cut_out].reshape(model_width, model_width),
        flat_weights[cut_out:cut_up].reshape(model_width, hidden_width),
        flat_weights[cut_up:].reshape(hidden_width, model_width),
    )


def adamw(param_value, moment, second, grad_total, step_value, rate, decay_rate):
    moment_next = beta_first * moment + (1.0 - beta_first) * grad_total
    second_next = beta_second * second + (1.0 - beta_second) * grad_total * grad_total
    moment_hat = moment_next / (1.0 - beta_first**step_value)
    second_hat = second_next / (1.0 - beta_second**step_value)
    param_next = param_value - rate * (
        moment_hat / (jnp.sqrt(second_hat) + adam_floor) + decay_rate * param_value
    )
    return (param_next, moment_next, second_next)


def interleave(pair):
    return pair.reshape(2, -1, LANES).swapaxes(0, 1).reshape(-1, LANES)


def separate(rows):
    return rows.reshape(-1, 2, LANES).swapaxes(0, 1).reshape(2, -1)


def on_device(
    clip_tokens,
    cotangent,
    lengths,
    params,
    param_moment,
    param_second,
    norm_par,
    norm_moment,
    norm_second,
):
    clip_count, step_slots, patch_count, model_width = clip_tokens.shape
    shards = lax.axis_size("dp")
    plan = shard_plan(shards, model_width, FF) if shards == 32 else None
    x = clip_tokens.reshape(-1, model_width)
    if plan is None:
        gathered = lax.all_gather(params.astype(bf16), "dp", axis=1, tiled=True)
        norm_whole = lax.all_gather(norm_par.astype(bf16), "dp", axis=0, tiled=True)
        norm_table = norm_whole.astype(f32).reshape(2, 4, model_width)
        spatial_weights = unpack(gathered[0], model_width, FF)
        temporal_weights = unpack(gathered[1], model_width, FF)
        sources = (*spatial_weights, norm_table[0])
        *kept, after = spatial_forward(plan, x, sources, patch_count, FF)
    else:
        sources = (interleave(params), norm_par.reshape(1, LANES))
        *kept, after, spatial_weights, temporal_weights, norm_table = spatial_forward(
            plan, x, sources, patch_count, FF
        )
    result, grad_after, *temporal_grads, temporal_norm = temporal_block(
        plan,
        lengths,
        after.reshape(step_slots, patch_count, model_width),
        cotangent.reshape(step_slots, patch_count, model_width),
        temporal_weights,
        norm_table[1] if plan is None else norm_table,
        FF,
    )
    grad_before, *spatial_grads, spatial_norm = spatial_backward(
        plan, x, grad_after.reshape(-1, model_width), kept, spatial_weights, norm_table[0] if plan is None else norm_table,
        temporal_grads[0],
    )
    if plan is None:

        def scatter(grads):
            flat = jnp.concatenate([g.reshape(-1) for g in grads])
            return lax.psum_scatter(flat, "dp", scatter_dimension=0, tiled=True).astype(f32)

        weight_sum = jnp.stack([scatter(spatial_grads), scatter(temporal_grads)])
        norm_grad = jnp.stack([spatial_norm, temporal_norm]).sum(axis=2).reshape(-1)
        norm_sum = lax.psum_scatter(norm_grad, "dp", scatter_dimension=0, tiled=True)
    else:
        weight_sum = spatial_grads[0]
        norm_sum = spatial_norm[0] + spatial_norm[1]
    step_value = float(STEP)
    state = (params, param_moment, param_second)
    if plan is None:
        updated = adamw(*state, weight_sum, step_value, learn_rate, weight_decay)
        new_copy = updated[0].astype(bf16)
    else:
        state = lax.optimization_barrier([interleave(part) for part in state])
        updated = adamw(*state, weight_sum, step_value, learn_rate, weight_decay)
        new_copy = separate(updated[0].astype(bf16))
        updated = [separate(part) for part in updated]
    new_params, new_moment, new_second = updated
    new_norm, new_norm_moment, new_norm_second = adamw(
        norm_par, norm_moment, norm_second, norm_sum, step_value, norm_rate, 0.0
    )
    return (
        result.reshape(clip_tokens.shape),
        grad_before.reshape(clip_tokens.shape),
        new_params,
        new_moment,
        new_second,
        new_copy,
        new_norm,
        new_norm_moment,
        new_norm_second,
    )


def solution(mesh):
    placed = (
        P("dp", None, None, None),
        P("dp", None, None, None),
        P("dp"),
        P(None, "dp"),
        P(None, "dp"),
        P(None, "dp"),
        P("dp"),
        P("dp"),
        P("dp"),
    )
    return jax.shard_map(
        on_device,
        mesh=mesh,
        in_specs=placed,
        out_specs=(
            P("dp", None, None, None),
            P("dp", None, None, None),
            P(None, "dp"),
            P(None, "dp"),
            P(None, "dp"),
            P(None, "dp"),
            P("dp"),
            P("dp"),
            P("dp"),
        ),
        check_vma=False,
    )
```

```python
from functools import partial

import jax
import jax.numpy as jnp
from jax import lax
from jax.experimental import pallas as pl
from jax.experimental.pallas import tpu as pltpu
from jax.sharding import PartitionSpec as P

HEADS = 8
HEAD_DIM = 64
FF = 2048
STEP = 7

norm_epsilon = 1e-05
beta_first = 0.9
beta_second = 0.999
learn_rate = 0.05
norm_rate = 0.5
weight_decay = 0.1
adam_floor = 1e-08
masked_score = -1e30

bf16 = jnp.bfloat16
f32 = jnp.float32
MIB = 2**20

SPATIAL_TILE = 256
TEMPORAL_TILE = 256
PATCH_GROUP = 16


def dot_nn(left, right):
    return lax.dot_general(left, right, (((1,), (0,)), ((), ())), preferred_element_type=f32)


def dot_nt(left, right):
    return lax.dot_general(left, right, (((1,), (1,)), ((), ())), preferred_element_type=f32)


def dot_tn(left, right):
    return lax.dot_general(left, right, (((0,), (0,)), ((), ())), preferred_element_type=f32)


def normalise(rows):
    center = rows - jnp.mean(rows, axis=-1, keepdims=True)
    spread = jnp.mean(center * center, axis=-1, keepdims=True)
    scale = lax.rsqrt(spread + norm_epsilon)
    return center * scale, scale


def fold_rows(rows):
    return jnp.sum(rows.reshape(-1, 8, rows.shape[-1]), axis=0)


def norm_backward(hat, scale, gain, grad):
    weighted = grad * gain
    mean_first = jnp.mean(weighted, axis=-1, keepdims=True)
    mean_second = jnp.mean(weighted * hat, axis=-1, keepdims=True)
    grad_rows = scale * (weighted - mean_first - hat * mean_second)
    return grad_rows, fold_rows(grad * hat), fold_rows(grad)


def gelu_pair(value):
    cumulative = 0.5 + 0.5 * lax.erf(value * 0.7071067811865476)
    density = jnp.exp(-0.5 * value * value) * 0.3989422804014327
    return value * cumulative, cumulative + value * density


def lane_halves(count):
    lane = lax.broadcasted_iota(jnp.int32, (count, 2 * HEAD_DIM), 1)
    return lane < HEAD_DIM


def two_heads(pair, low_half):
    zero = jnp.zeros_like(pair)
    return jnp.concatenate([jnp.where(low_half, pair, zero), jnp.where(low_half, zero, pair)], axis=0)


def own_columns(stacked, low_half):
    rows = stacked.shape[0] // 2
    return jnp.where(low_half, stacked[:rows], stacked[rows:]).astype(bf16)


ROW_CHUNK = 64


def attend(units, scores, soft, low_half, bias):
    rows, double = scores.shape[1:]
    keys = double // 2
    for unit, (query, key, value, put) in enumerate(units):
        scaled = query() * jnp.asarray(HEAD_DIM**-0.5, bf16)
        scores[unit] = dot_nt(scaled, two_heads(key(), low_half))
    for unit in range(len(units)):
        for start in range(0, rows, ROW_CHUNK):
            span = slice(start, start + ROW_CHUNK)
            for half in range(2):
                columns = slice(half * keys, (half + 1) * keys)
                part = scores[unit, span, columns]
                if bias is not None:
                    part = part + bias[span]
                powers = jnp.exp(part - jnp.max(part, axis=-1, keepdims=True))
                part = powers * (1.0 / jnp.sum(powers, axis=-1, keepdims=True))
                soft[unit, span, columns] = part.astype(bf16)
    for unit, (query, key, value, put) in enumerate(units):
        put(dot_nn(soft[unit], two_heads(value(), low_half)).astype(bf16))


def attend_backward(units, scores, soft, grad_scores, low_half):
    rows, double = scores.shape[1:]
    keys = double // 2
    scale = jnp.asarray(HEAD_DIM**-0.5, bf16)
    for unit, (query, key, value, grad, put) in enumerate(units):
        scores[unit] = dot_nt(grad(), two_heads(value(), low_half))
    for unit in range(len(units)):
        for start in range(0, rows, ROW_CHUNK):
            span = slice(start, start + ROW_CHUNK)
            for half in range(2):
                columns = slice(half * keys, (half + 1) * keys)
                wide = soft[unit, span, columns].astype(f32)
                product = scores[unit, span, columns] * wide
                inner = jnp.sum(product, axis=-1, keepdims=True)
                grad_scores[unit, span, columns] = (product - wide * inner).astype(bf16)
    for unit, (query, key, value, grad, put) in enumerate(units):
        grad_value = own_columns(dot_tn(soft[unit], grad()), low_half)
        grad_query = dot_nn(grad_scores[unit], two_heads(key() * scale, low_half)).astype(bf16)
        grad_key = own_columns(dot_tn(grad_scores[unit], query() * scale), low_half)
        put(grad_query, grad_key, grad_value)


def feed_forward(second, w_up, w_down, active_ref, slope_ref, chunk=512):
    hidden = w_up.shape[1]
    for start in range(0, hidden, chunk):
        active, slope = gelu_pair(dot_nn(second, w_up[:, start : start + chunk]))
        active_ref[:, start : start + chunk] = active.astype(bf16)
        slope_ref[:, start : start + chunk] = slope.astype(bf16)
    return dot_nn(active_ref[...], w_down[...])


def hidden_backward(branch, w_down, slope_ref, hidden_ref, chunk=512):
    hidden = w_down.shape[0]
    for start in range(0, hidden, chunk):
        grad = dot_nt(branch, w_down[start : start + chunk, :])
        slope = slope_ref[:, start : start + chunk].astype(f32)
        hidden_ref[:, start : start + chunk] = (grad * slope).astype(bf16)


def spatial_forward_kernel(plan, x_ref, *refs):
    step, last = pl.program_id(1), pl.num_programs(1) - 1
    opening = pl.program_id(0) == 0
    if plan is None:
        w_qkv, w_out, w_up, w_down, norm_ref = refs[:5]
        refs = refs[5:]
        packed_ref, weights_ref, mixture_ref, middle_ref, active_ref, slope_ref, after_ref = refs[:7]
        scores, mixture_all = refs[7:]
    else:
        shard_ref, norm_par_ref = refs[:2]
        refs = refs[2:]
        packed_ref, weights_ref, mixture_ref, middle_ref, active_ref, slope_ref, after_ref = refs[:7]
        held_out, held_next, norm_ref = refs[7:10]
        scores, mixture_all, w_qkv, w_out, w_up, w_down, held, staged, send, recv, local = refs[10:]
        matrices = (w_qkv, w_out, w_up, w_down)
        place = Place(lax.axis_index("dp"))
        order = [place.z] + [k - (place.z + 4 - k) // 4 for k in range(1, 4)]
        now = Gather(place, held, send.at[0], recv.at[0])
        later = Gather(place, held_next, send.at[1], recv.at[1])
        keep = pltpu.make_async_copy(held, held_out, local.at[0])

        def gathered(*planes):
            for q in planes:
                now.finish(q)
            assemble(plan, held, matrices, planes)
            assemble_norms(len(plan), held, norm_ref, planes)

        @pl.when(opening & (step == 0))
        def _():
            enter(place)
            load_shard(plan, place.me, 0, shard_ref, norm_par_ref, held.at[place.z, place.y, place.x, place.c])
            now.start_z()
            load_shard(plan, place.me, 1, shard_ref, norm_par_ref, staged)
            copy = pltpu.make_async_copy(
                staged, held_next.at[place.z, place.y, place.x, place.c], local.at[1]
            )
            copy.start()
            copy.wait()
            now.begin_first(order[0])
            later.begin_first(order[0])
            now.begin_second(order[0])
            later.begin_second(order[0])
            now.begin_first(order[1])
            now.begin_third(order[0])
            now.begin_second(order[1])
            later.start_z()
            now.begin_third(order[1])
            now.begin_first(order[2])
            now.begin_first(order[3])
            gathered(0)

        def at(passing, when, *actions):
            @pl.when(passing & (step == when))
            def _():
                for action, k in actions:
                    action(order[k])

        closing = jnp.logical_not(opening)
        at(opening, 1, (now.begin_second, 2))
        at(opening, 2, (now.begin_second, 3))
        at(opening, 3, (now.begin_third, 2))
        at(opening, 4, (later.begin_first, 1), (later.begin_first, 2), (later.begin_first, 3))
        at(opening, 5, (now.begin_third, 3))
        at(opening, 6, (later.begin_second, 1), (later.begin_third, 0))
        at(opening, 7, (later.begin_second, 2))
        at(closing, 0, (later.begin_second, 3))
        at(closing, 1, (later.begin_third, 1))
        at(closing, 3, (later.begin_third, 2))
        at(closing, 6, (later.begin_third, 3))

        @pl.when(jnp.logical_not(opening) & (step == 0))
        def _():
            gathered(1, 2, 3)
            keep.start()

    tile, width = x_ref.shape
    here = pl.ds(pl.multiple_of(step * tile, tile), tile)

    @pl.when(opening)
    def _():
        hat, _ = normalise(x_ref[...].astype(f32))
        first = (hat * norm_ref[0:1] + norm_ref[1:2]).astype(bf16)
        for start in range(0, 3 * width, 512):
            packed_ref[:, start : start + 512] = dot_nn(first, w_qkv[:, start : start + 512]).astype(bf16)
        frame = weights_ref.shape[2]
        low_half = lane_halves(frame)
        for item in range(weights_ref.shape[0]):
            span = slice(item * frame, (item + 1) * frame)
            units = []
            for pair in range(HEADS // 2):

                def cut(part, pair=pair, span=span):
                    start = part * width + 128 * pair
                    return packed_ref[span, start : start + 128]

                def put(value, pair=pair, span=span):
                    mixture_ref[span, 128 * pair : 128 * (pair + 1)] = value

                units.append((partial(cut, 0), partial(cut, 1), partial(cut, 2), put))
            attend(units, scores, weights_ref.at[item], low_half, None)
        mixture_all[here, :] = mixture_ref[...]

    @pl.when(jnp.logical_not(opening))
    def _():
        middle = x_ref[...].astype(f32) + dot_nn(mixture_all[here, :], w_out[...])
        middle_ref[...] = middle
        hat, _ = normalise(middle)
        second = (hat * norm_ref[2:3] + norm_ref[3:4]).astype(bf16)
        after_ref[...] = middle + feed_forward(second, w_up, w_down, active_ref, slope_ref)

    if plan is not None:

        @pl.when(jnp.logical_not(opening) & (step == last))
        def _():
            for q in range(4):
                later.finish(q)
            keep.wait()
            now.drain()
            later.drain()


def whole(shape):
    return pl.BlockSpec(shape, lambda *_: (0,) * len(shape), pipeline_mode=pl.Buffered(1))


def tiles(tile, *rest):
    return pl.BlockSpec((tile, *rest), lambda i: (i,) + (0,) * len(rest))


def spatial_forward(plan, x, sources, frame, hidden):
    tokens, width = x.shape
    tile = SPATIAL_TILE
    frames = tile // frame
    count = tokens // tile

    def opening(*rest):
        return pl.BlockSpec(rest, lambda p, i: (i + p * (count - 1 - i),) + (0,) * (len(rest) - 1))

    def closing(*rest):
        return pl.BlockSpec(rest, lambda p, i: (i * p,) + (0,) * (len(rest) - 1))

    out_specs = [
        opening(tile, 3 * width),
        opening(frames, HEADS // 2, frame, 2 * frame),
        opening(tile, width),
        closing(tile, width),
        closing(tile, hidden),
        closing(tile, hidden),
        closing(tile, width),
    ]
    out_shape = [
        jax.ShapeDtypeStruct((tokens, 3 * width), bf16),
        jax.ShapeDtypeStruct((tokens // frame, HEADS // 2, frame, 2 * frame), bf16),
        jax.ShapeDtypeStruct((tokens, width), bf16),
        jax.ShapeDtypeStruct((tokens, width), f32),
        jax.ShapeDtypeStruct((tokens, hidden), bf16),
        jax.ShapeDtypeStruct((tokens, hidden), bf16),
        jax.ShapeDtypeStruct((tokens, width), f32),
    ]
    scratch = [pltpu.VMEM((HEADS // 2, frame, 2 * frame), f32), pltpu.VMEM((tokens, width), bf16)]
    params = dict(vmem_limit_bytes=60 * MIB)
    if plan is not None:
        held = (4, 2, 2, 2, SHARD, LANES)
        out_specs += [pl.BlockSpec(memory_space=pl.ANY)] * 2 + [whole((8, width))]
        out_shape += [jax.ShapeDtypeStruct(held, bf16)] * 2 + [jax.ShapeDtypeStruct((8, width), f32)]
        scratch += [pltpu.VMEM(shape, bf16) for shape in matrix_shapes(width, hidden)]
        scratch += [
            pltpu.VMEM(held, bf16),
            pltpu.VMEM((SHARD, LANES), bf16),
            pltpu.SemaphoreType.DMA((2, 6, 4)),
            pltpu.SemaphoreType.DMA((2, 6, 4)),
            pltpu.SemaphoreType.DMA((2,)),
        ]
        params |= dict(collective_id=0, has_side_effects=True)
    return pl.pallas_call(
        partial(spatial_forward_kernel, plan),
        grid=(2, count),
        in_specs=[pl.BlockSpec((tile, width), lambda p, i: (i, 0))] + [whole(a.shape) for a in sources],
        out_specs=out_specs,
        out_shape=out_shape,
        scratch_shapes=scratch,
        compiler_params=pltpu.CompilerParams(**params),
    )(x, *sources)


MESH_IDS = pl.DeviceIdType.MESH
LANES = 128
ROW_TILE = 16


def matrix_shapes(width, hidden):
    return ((width, 3 * width), (width, width), (width, hidden), (hidden, width))


def shard_plan(shards, width, hidden):
    plan = []
    base = 0
    regions = []
    for index, (rows, columns) in enumerate(matrix_shapes(width, hidden)):
        regions.append((index, base, rows, columns))
        base += rows * columns
    if base % shards:
        return None
    size = base // shards
    for device in range(shards):
        low, high = device * size, (device + 1) * size
        halves = ([], [])
        for index, start, rows, columns in regions:
            first, last = max(low, start), min(high, start + rows * columns)
            if first >= last:
                continue
            if (first - start) % columns or (last - start) % columns:
                return None
            row, count = (first - start) // columns, (last - first) // columns
            if row % ROW_TILE or count % ROW_TILE:
                return None
            stride = columns // LANES
            for block in range(stride):
                halves[2 * block // stride].append(
                    (index, row, count, block, (first - low) // LANES + block, stride)
                )
        place = 0
        entries = []
        for item in halves[0] + halves[1]:
            entries.append(item + (place,))
            place += item[2]
        plan.append(entries)
    return plan


def by_pattern(plan):
    groups = {}
    for device, entries in enumerate(plan):
        layout = tuple((e[2], e[4], e[5], e[6]) for e in entries)
        ranges = groups.setdefault(layout, [])
        if ranges and ranges[-1][1] == device:
            ranges[-1][1] = device + 1
        else:
            ranges.append([device, device + 1])
    return list(groups.items())


def on_pattern(plan, me, body):
    for layout, ranges in by_pattern(plan):
        inside = None
        for low, high in ranges:
            test = (me >= low) & (me < high)
            inside = test if inside is None else inside | test

        @pl.when(inside)
        def _(layout=layout):
            body(layout)


class Place:
    def __init__(self, me):
        self.me = me
        self.c = lax.rem(me, 2)
        self.x = lax.rem(me // 2, 2)
        self.y = lax.rem(me // 4, 2)
        self.z = me // 8

    def device(self, z, y, x, c):
        return ((z * 2 + y) * 2 + x) * 2 + c

    @property
    def sibling(self):
        return self.device(self.z, self.y, self.x, 1 - self.c)

    @property
    def across_x(self):
        return self.device(self.z, self.y, 1 - self.x, self.c)

    @property
    def across_y(self):
        return self.device(self.z, 1 - self.y, self.x, self.c)

    def plane(self, z):
        return self.device(z, self.y, self.x, self.c)


def remote(src, dst, send, recv, device):
    return pltpu.make_async_remote_copy(
        src_ref=src, dst_ref=dst, send_sem=send, recv_sem=recv, device_id=(device,), device_id_type=MESH_IDS
    )


def enter(place):
    barrier = pltpu.get_barrier_semaphore()
    partners = [place.sibling, place.across_x, place.across_y]
    partners += [place.plane(lax.rem(place.z + k, 4)) for k in range(1, 4)]
    for device in partners:
        pl.semaphore_signal(barrier, inc=1, device_id=(device,), device_id_type=MESH_IDS)
    pl.semaphore_wait(barrier, len(partners))


HALF = 384
SHARD = 784


class Gather:
    SEMS = 9

    def __init__(self, place, held, send, recv):
        self.p, self.held, self.send, self.recv = place, held, send, recv

    def along_z(self, k):
        p = self.p
        here = self.held.at[p.z, p.y, p.x, p.c]
        return remote(here, here, self.send.at[0, k - 1], self.recv.at[0, p.z], p.plane(lax.rem(p.z + k, 4)))

    def start_z(self):
        for k in range(1, 4):
            self.along_z(k).start()

    def wait_z(self, q):
        p = self.p

        @pl.when(q != p.z)
        def _():
            there = self.held.at[q, p.y, p.x, p.c]
            remote(there, there, self.send.at[0, 0], self.recv.at[0, q], p.me).wait_recv()

    def first(self, q):
        p, h = self.p, self.held
        a = h.at[q, p.y, p.x, p.c, pl.ds(0, HALF)]
        b = h.at[q, p.y, p.x, p.c, pl.ds(HALF, SHARD - HALF)]
        return (
            remote(a, a, self.send.at[1, q], self.recv.at[1, q], p.across_x),
            remote(b, b, self.send.at[2, q], self.recv.at[2, q], p.across_y),
        )

    def second(self, q):
        p, h = self.p, self.held
        a = h.at[q, p.y, :, p.c, pl.ds(0, HALF)]
        b = h.at[q, :, p.x, p.c, pl.ds(HALF, SHARD - HALF)]
        return (
            remote(a, a, self.send.at[3, q], self.recv.at[3, q], p.across_y),
            remote(b, b, self.send.at[4, q], self.recv.at[4, q], p.across_x),
        )

    def third(self, q):
        p, h = self.p, self.held
        a = h.at[q, :, :, p.c]
        return (remote(a, a, self.send.at[5, q], self.recv.at[5, q], p.sibling),)

    def begin_first(self, q):
        self.wait_z(q)
        for copy in self.first(q):
            copy.start()

    def begin_second(self, q):
        for copy in self.first(q):
            copy.wait_recv()
        for copy in self.second(q):
            copy.start()

    def begin_third(self, q):
        for copy in self.second(q):
            copy.wait_recv()
        for copy in self.third(q):
            copy.start()

    def finish(self, q):
        for copy in self.third(q):
            copy.wait_recv()

    def drain(self):
        for k in range(1, 4):
            self.along_z(k).wait_send()
        for q in range(4):
            for copy in self.first(q) + self.second(q) + self.third(q):
                copy.wait_send()


def load_shard(plan, me, block, shard_ref, norm_ref, held_here):
    def body(layout):
        for count, flat, stride, place in layout:
            held_here[pl.ds(place, count), :] = shard_ref[pl.ds(2 * flat + block, count, 2 * stride), :].astype(bf16)

    on_pattern(plan, me, body)
    held_here[SHARD - ROW_TILE :, :] = jnp.broadcast_to(norm_ref[...], (ROW_TILE, LANES)).astype(bf16)


def coordinates(device):
    return device // 8, device // 4 % 2, device // 2 % 2, device % 2


def assemble(plan, held, outs, planes):
    for device, entries in enumerate(plan):
        z, y, x, c = coordinates(device)
        if z not in planes:
            continue
        for index, row, count, block, _, _, place in entries:
            outs[index][row : row + count, LANES * block : LANES * (block + 1)] = held[
                z, y, x, c, place : place + count, :
            ]


def assemble_norms(shards, held, norm_out, planes):
    per_row = norm_out.shape[1] // LANES
    for device in range(shards):
        z, y, x, c = coordinates(device)
        if z not in planes:
            continue
        row, column = device // per_row, device % per_row
        norm_out[row : row + 1, LANES * column : LANES * (column + 1)] = held[
            z, y, x, c, SHARD - ROW_TILE : SHARD, :
        ].astype(f32)[0:1]


def accumulate(into, part, chunk):
    def body(i, _):
        span = pl.ds(pl.multiple_of(i * chunk, ROW_TILE), chunk)
        into[span, :] = into[span, :] + part[span, :]
        return 0

    lax.fori_loop(0, into.shape[0] // chunk, body, 0)


class Scatter:
    def __init__(self, place, own, room, send, recv, credit=None, leads=None):
        self.p, self.own = place, own
        rows, half = room[3].shape[1], room[1].shape[2]
        self.low, self.high = pl.ds(0, half), pl.ds(half, rows - half)
        self.chunk, self.chunk_low, self.chunk_high = (112, 128, 80) if rows == SHARD else (ROW_TILE,) * 3
        self.r1, self.r2a, self.r2b, self.r3, self.r4 = room
        self.send, self.recv, self.credit, self.leads = send, recv, credit, leads

    def release(self, kind, q, device):
        if self.leads is True:
            pl.semaphore_signal(self.credit.at[kind, q], inc=1, device_id=(device,), device_id_type=MESH_IDS)

    def claim(self, kind, q):
        if self.leads is False:
            pl.semaphore_wait(self.credit.at[kind, q], 1)

    def first(self, q):
        p = self.p
        return (
            remote(
                self.own.at[q, :, :, 1 - p.c], self.r1.at[q], self.send.at[0, q], self.recv.at[0, q], p.sibling
            ),
        )

    def second(self, q):
        p = self.p
        low, high = self.low, self.high
        return (
            remote(
                self.r1.at[q, :, 1 - p.x, low], self.r2a.at[q], self.send.at[1, q], self.recv.at[1, q], p.across_x
            ),
            remote(
                self.r1.at[q, 1 - p.y, :, high], self.r2b.at[q], self.send.at[2, q], self.recv.at[2, q], p.across_y
            ),
        )

    def third(self, q):
        p = self.p
        low, high = self.low, self.high
        return (
            remote(
                self.r2a.at[q, 1 - p.y], self.r3.at[q, low], self.send.at[3, q], self.recv.at[3, q], p.across_y
            ),
            remote(
                self.r2b.at[q, 1 - p.x], self.r3.at[q, high], self.send.at[4, q], self.recv.at[4, q], p.across_x
            ),
        )

    def along_z(self, q):
        p = self.p
        return remote(self.r3.at[q], self.r4.at[p.z], self.send.at[5, q], self.recv.at[5, p.z], p.plane(q))

    def begin_first(self, q):
        self.claim(0, q)
        for copy in self.first(q):
            copy.start()

    def begin_second(self, q, mine):
        for copy in self.first(q):
            copy.wait_recv()
        for y in range(2):
            for x in range(2):
                accumulate(self.r1.at[q, y, x], mine(y, x), self.chunk)
        self.claim(1, q)
        self.claim(2, q)
        for copy in self.second(q):
            copy.start()

    def begin_third(self, q):
        p = self.p
        for copy in self.second(q):
            copy.wait_recv()
        low, high = self.low, self.high
        for k in range(2):
            accumulate(self.r2a.at[q, k], self.r1.at[q, k, p.x, low], self.chunk_low)
            accumulate(self.r2b.at[q, k], self.r1.at[q, p.y, k, high], self.chunk_high)
        for copy in self.third(q):
            copy.start()
        for copy in self.second(q):
            copy.wait_send()
        self.release(0, q, p.sibling)

    def begin_z(self, q, total):
        p = self.p
        for copy in self.third(q):
            copy.wait_recv()
        low, high = self.low, self.high
        accumulate(self.r3.at[q, low], self.r2a.at[q, p.y], self.chunk_low)
        accumulate(self.r3.at[q, high], self.r2b.at[q, p.x], self.chunk_high)

        @pl.when(q != p.z)
        def _():
            self.along_z(q).start()

        @pl.when(q == p.z)
        def _():
            total[...] = self.r3[q].astype(f32)

        for copy in self.third(q):
            copy.wait_send()
        self.release(1, q, p.across_x)
        self.release(2, q, p.across_y)

    def leave_z(self, q):
        p = self.p

        @pl.when(q != p.z)
        def _():
            self.along_z(q).wait_send()

    def finish(self, total):
        p = self.p
        planes = self.r3.shape[0]

        @pl.when(p.z < planes)
        def _():
            for k in range(1, 4):
                z = lax.rem(p.z + k, 4)
                remote(self.r3.at[0], self.r4.at[z], self.send.at[5, 0], self.recv.at[5, z], p.me).wait_recv()
            for k in range(1, 4):
                total[...] += self.r4[lax.rem(p.z + k, 4)].astype(f32)

        for q in range(planes):
            for copy in self.first(q):
                copy.wait_send()
            self.leave_z(q)


class Relay(Scatter):
    def hand_on(self, room, send, recv, device):
        return remote(self.r3.at[0], room, send.at[0], recv.at[0], device)

    def start_tail(self, total, room, send, recv):
        p = self.p
        for copy in self.third(0):
            copy.wait_recv()
        accumulate(self.r3.at[0, self.low], self.r2a.at[0, p.y], self.chunk_low)
        accumulate(self.r3.at[0, self.high], self.r2b.at[0, p.x], self.chunk_high)

        @pl.when(p.z == 3)
        def _():
            self.hand_on(room, send, recv, p.plane(2)).start()

        @pl.when(p.z == 1)
        def _():
            self.along_z(0).start()

        @pl.when(p.z == 0)
        def _():
            total[...] = self.r3[0].astype(f32)

        for copy in self.third(0):
            copy.wait_send()

    def go_on(self, room, send, recv):
        @pl.when(self.p.z == 2)
        def _():
            self.hand_on(room, send, recv, self.p.me).wait_recv()
            accumulate(self.r3.at[0], room, self.chunk)
            self.along_z(0).start()

    def finish_tail(self, total, room, send, recv):
        p = self.p

        def arrive(z):
            remote(self.r3.at[0], self.r4.at[z], self.send.at[5, 0], self.recv.at[5, z], p.me).wait_recv()

        @pl.when(p.z == 0)
        def _():
            for z in (1, 2):
                arrive(z)
                total[...] += self.r4[z].astype(f32)

        @pl.when(p.z > 0)
        def _():
            for k in range(1, 4):
                z = lax.rem(p.z + k, 4)
                arrive(z)
                total[...] += self.r4[z].astype(f32)

        for q in range(4):
            for copy in self.first(q):
                copy.wait_send()
        for q in range(1, 4):
            self.leave_z(q)

        @pl.when((p.z == 1) | (p.z == 2))
        def _():
            self.along_z(0).wait_send()

        @pl.when(p.z == 3)
        def _():
            self.hand_on(room, send, recv, p.plane(2)).wait_send()


SCATTER_ROOM = [
    pltpu.VMEM((4, 2, 2, SHARD, LANES), bf16),
    pltpu.VMEM((4, 2, HALF, LANES), bf16),
    pltpu.VMEM((4, 2, SHARD - HALF, LANES), bf16),
    pltpu.VMEM((2, 4, SHARD, LANES), bf16),
    pltpu.VMEM((2, 4, SHARD, LANES), bf16),
]

SMALL = 2 * ROW_TILE
SMALL_ROOM = [
    pltpu.VMEM((1, 2, 2, 2, SMALL, LANES), bf16),
    pltpu.VMEM((1, 2, 2, SMALL, LANES), bf16),
    pltpu.VMEM((1, 2, ROW_TILE, LANES), bf16),
    pltpu.VMEM((1, 2, ROW_TILE, LANES), bf16),
    pltpu.VMEM((1, SMALL, LANES), bf16),
    pltpu.VMEM((4, SMALL, LANES), bf16),
    pltpu.VMEM((SMALL, LANES), f32),
    pltpu.SemaphoreType.DMA((6, 4)),
    pltpu.SemaphoreType.DMA((6, 4)),
]


def unload_shard(plan, me, block, total, flat_ref):
    def body(layout):
        for count, flat, stride, place in layout:
            flat_ref[pl.ds(2 * flat + block, count, 2 * stride), :] = total[pl.ds(place, count), :]

    on_pattern(plan, me, body)


def store_travel(plan, own, index, top, start, value):
    for device, entries in enumerate(plan):
        z, y, x, c = coordinates(device)
        for entry, row, count, block, _, _, place in entries:
            column = LANES * block - start
            low, high = max(row, top), min(row + count, top + value.shape[0])
            if entry == index and 0 <= column < value.shape[1] and low < high:
                own[z, y, x, c, place + low - row : place + high - row, :] = value[
                    low - top : high - top, column : column + LANES
                ]


def store_norms(plan, own, block, sums, planes, first=SHARD - ROW_TILE):
    width = sums.shape[2]
    per_row = width // LANES
    line = lax.broadcasted_iota(jnp.int32, (ROW_TILE, LANES), 0)
    for device in range(len(plan)):
        z, y, x, c = coordinates(device)
        if z not in planes:
            continue
        row = device // per_row - 4 * block
        if 0 <= row < 4:
            column = LANES * (device % per_row)
            value = jnp.sum(sums[row, :, column : column + LANES], axis=0, keepdims=True)
            coarse = value.astype(bf16).astype(f32)
            rows = jnp.where(line == 0, coarse, jnp.where(line == 1, value - coarse, 0.0))
        else:
            rows = jnp.zeros((ROW_TILE, LANES), f32)
        own[z, y, x, c, first : first + ROW_TILE, :] = rows.astype(bf16)


def weight_grads(first, grad_packed, mixture, attn, second, grad_hidden, active, branch, store, chunk=512):
    sides = ((first, grad_packed), (mixture, attn), (second, grad_hidden), (active, branch))
    for index, (left, right) in enumerate(sides):
        for start in range(0, right.shape[1], chunk):
            store(index, 0, start, dot_tn(left[...], right[:, start : start + chunk]).astype(bf16))


def grad_outputs(plan, width, hidden):
    shapes = matrix_shapes(width, hidden) if plan is None else [(4, 2, 2, 2, SHARD, LANES)]
    return [whole(s) for s in shapes], [jax.ShapeDtypeStruct(s, bf16) for s in shapes]


def storing(plan, outs):
    if plan is None:
        def store(index, top, start, value):
            outs[index][top : top + value.shape[0], start : start + value.shape[1]] = value
        return store
    return partial(store_travel, plan, outs[0])


def temporal_kernel(
    plan, length_ref, rows_ref, cotangent_ref, *refs
):
    sources = 5 if plan is None else 2
    refs, sources = refs[sources:], refs[:sources]
    result_ref, before_ref, *refs = refs
    if plan is None:
        w_qkv, w_out, w_up, w_down, norm_ref = sources
    else:
        *refs, w_qkv, w_out, w_up, w_down, local = refs
        norm_ref = sources[1].at[4:8]
    outs, g_norm = refs[:-15], refs[-15]
    packed, slope, weights_buf, grad_mix, scores, grad_scores = refs[-14:-8]
    first_all, packed_all, mixture_all, attn_all, second_all, hidden_all, active_all, branch_all = refs[-8:]
    step = pl.program_id(0)
    steps, patches, width = rows_ref.shape
    tile = steps * patches
    here = pl.ds(pl.multiple_of(step * tile, tile), tile)
    length = length_ref[0]
    group = PATCH_GROUP
    count = steps * group

    @pl.when(step == 0)
    def _():
        g_norm[...] = jnp.zeros_like(g_norm)
        if plan is not None:
            load_weights(plan, sources[0], outs[0], (w_qkv, w_out, w_up, w_down), local)

    row = lax.broadcasted_iota(jnp.int32, (count, count), 0)
    column = lax.broadcasted_iota(jnp.int32, (count, count), 1)
    seen = (row % group == column % group) & (column // group <= row // group)
    seen = seen & (column // group < length)
    bias = jnp.where(seen, 0.0, masked_score)
    low_half = lane_halves(count)

    rows = rows_ref[...].reshape(tile, width)
    hat, _ = normalise(rows)
    first = (hat * norm_ref[0:1] + norm_ref[1:2]).astype(bf16)
    first_all[here, :] = first
    packed[...] = dot_nn(first, w_qkv[...]).astype(bf16).reshape(packed.shape)

    mixture_view = mixture_all.at[here, :]

    def cut(source, part, place, pair):
        start = part * width + 128 * pair
        return source[:, place : place + group, start : start + 128].reshape(count, 128)

    def units_of(backward):
        units = []
        for place in range(0, patches, group):
            for pair in range(HEADS // 2):

                def put(*values, place=place, pair=pair):
                    for part, value in enumerate(values):
                        start = part * width + 128 * pair
                        into = packed if backward else grad_mix
                        into[:, place : place + group, start : start + 128] = value.reshape(steps, group, 128)

                gets = [partial(cut, packed, part, place, pair) for part in range(3)]
                if backward:
                    gets.append(partial(cut, grad_mix, 0, place, pair))
                units.append((*gets, put))
        return units

    attend(units_of(False), scores, weights_buf, low_half, bias)
    mixture = grad_mix[...].reshape(tile, width)
    mixture_all[here, :] = mixture
    middle = rows + dot_nn(mixture, w_out[...])
    hat, scale = normalise(middle)
    second = (hat * norm_ref[2:3] + norm_ref[3:4]).astype(bf16)
    second_all[here, :] = second
    after = middle + feed_forward(second, w_up, w_down, active_all.at[here, :], slope)
    result_ref[...] = after.reshape(result_ref.shape)

    slot = lax.broadcasted_iota(jnp.int32, rows_ref.shape, 0)
    live = (slot < length).astype(f32)
    grad_after = (cotangent_ref[...].astype(f32) * live).reshape(tile, width)
    branch = grad_after.astype(bf16)
    branch_all[here, :] = branch
    hidden_backward(branch, w_down, slope, hidden_all.at[here, :])
    grad_second = dot_nt(hidden_all[here, :], w_up[...])
    hat, scale = normalise(middle)
    grad_rows, gain, shift = norm_backward(hat, scale, norm_ref[2:3], grad_second)
    g_norm[2] += gain
    g_norm[3] += shift
    grad_middle = grad_after + grad_rows
    attn = grad_middle.astype(bf16)
    attn_all[here, :] = attn
    grad_mix[...] = dot_nt(attn, w_out[...]).astype(bf16).reshape(grad_mix.shape)
    attend_backward(units_of(True), scores, weights_buf, grad_scores, low_half)
    grad_packed = packed[...].reshape(tile, 3 * width)
    packed_all[here, :] = grad_packed
    grad_first = dot_nt(grad_packed, w_qkv[...])
    hat, scale = normalise(rows)
    grad_rows, gain, shift = norm_backward(hat, scale, norm_ref[0:1], grad_first)
    g_norm[0] += gain
    g_norm[1] += shift
    before_ref[...] = (grad_middle + grad_rows).reshape(before_ref.shape)

    @pl.when(step == pl.num_programs(0) - 1)
    def _():
        if plan is not None:
            store_norms(plan, outs[0], 1, g_norm, range(4))
        weight_grads(
            first_all, packed_all, mixture_all, attn_all, second_all, hidden_all, active_all,
            branch_all, storing(plan, outs),
        )


def load_weights(plan, held, room, matrices, local):
    copy = pltpu.make_async_copy(held, room, local.at[0])
    copy.start()
    copy.wait()
    assemble(plan, room, matrices, range(4))


def weight_sources(plan, weights, norms, hidden):
    width = norms.shape[1]
    if plan is None:
        return [*weights, norms], [whole(a.shape) for a in (*weights, norms)], []
    scratch = [pltpu.VMEM(shape, bf16) for shape in matrix_shapes(width, hidden)]
    scratch.append(pltpu.SemaphoreType.DMA((1,)))
    return [weights, norms], [pl.BlockSpec(memory_space=pl.ANY), whole(norms.shape)], scratch


def temporal_block(plan, length, rows, cotangent, weights, norms, hidden):
    grad_specs, grad_shapes = grad_outputs(plan, norms.shape[1], hidden)
    operands, specs, extra = weight_sources(plan, weights, norms, hidden)
    steps, patches, width = rows.shape
    tokens = steps * patches
    part = TEMPORAL_TILE // steps
    count = steps * PATCH_GROUP
    unit_shape = (part // PATCH_GROUP * (HEADS // 2), count, 2 * count)
    slab = pl.BlockSpec((steps, part, width), lambda i: (0, i, 0))
    return pl.pallas_call(
        partial(temporal_kernel, plan),
        grid=(patches // part,),
        in_specs=[pl.BlockSpec(memory_space=pltpu.SMEM), slab, slab] + specs,
        out_specs=[slab, slab] + grad_specs + [whole((4, 8, width))],
        out_shape=[
            jax.ShapeDtypeStruct(rows.shape, f32),
            jax.ShapeDtypeStruct(rows.shape, f32),
        ]
        + grad_shapes
        + [jax.ShapeDtypeStruct((4, 8, width), f32)],
        scratch_shapes=[
            pltpu.VMEM((steps, part, 3 * width), bf16),
            pltpu.VMEM((TEMPORAL_TILE, hidden), bf16),
            pltpu.VMEM(unit_shape, bf16),
            pltpu.VMEM((steps, part, width), bf16),
            pltpu.VMEM(unit_shape, f32),
            pltpu.VMEM(unit_shape, bf16),
            pltpu.VMEM((tokens, width), bf16),
            pltpu.VMEM((tokens, 3 * width), bf16),
            pltpu.VMEM((tokens, width), bf16),
            pltpu.VMEM((tokens, width), bf16),
            pltpu.VMEM((tokens, width), bf16),
            pltpu.VMEM((tokens, hidden), bf16),
            pltpu.VMEM((tokens, hidden), bf16),
            pltpu.VMEM((tokens, width), bf16),
        ]
        + extra,
        compiler_params=pltpu.CompilerParams(vmem_limit_bytes=62 * MIB),
    )(length, rows, cotangent, *operands)


def spatial_backward_kernel(
    plan, x_ref, grad_ref, packed_ref, weights_ref, middle_ref, slope_ref, mixture_hbm, active_hbm, *refs
):
    step, last = pl.program_id(1), pl.num_programs(1) - 1
    opening, midway, closing = [pl.program_id(0) == k for k in range(3)]
    if plan is None:
        w_qkv, w_out, w_up, w_down, norm_ref, before_ref, *outs, g_norm = refs[:11]
        refs = refs[11:]
    else:
        held, norm_ref, own_next, before_ref, flat, norm_out = refs[:6]
        own_small, *room_small, total_small, send_small, recv_small = refs[-len(SMALL_ROOM) - 3 : -3]
        relay = refs[-3:]
        *refs, total, total_rest, own, mine, load, send, recv, credit = refs[6 : -len(SMALL_ROOM) - 3]
        room, refs = refs[-5:], refs[:-5]
        *refs, g_norm, w_qkv, w_out, w_up, w_down, local = refs
        outs = [own]
        place = Place(lax.axis_index("dp"))
        rooms = [(*room[:3], room[3].at[k], room[4].at[k]) for k in range(2)]
        lead = Scatter(place, own_next, rooms[0], send.at[0], recv.at[0], credit, True)
        rest = Relay(place, own, rooms[1], send.at[1], recv.at[1], credit, False)
        small = Scatter(place, own_small, room_small, send_small, recv_small)
    scores, grad_scores, grad_mix, middle_all, second_all, hidden_all, attn_all, branch_all, side, side_sem = refs
    store = storing(plan, outs)
    tile, width = x_ref.shape
    hidden = slope_ref.shape[1]
    here = pl.ds(pl.multiple_of(step * tile, tile), tile)

    def own_shards(q):
        return pltpu.make_async_copy(own_next.at[q, :, :, place.c], mine.at[q % 2], load.at[q % 2])

    def lead_second(q):
        own_shards(q).wait()
        lead.begin_second(q, lambda y, x: mine.at[q % 2, y, x])
        if q < 2:
            own_shards(q + 2).start()

    def rest_second(q):
        rest.begin_second(q, lambda y, x: own.at[q, y, x, place.c])

    def at(passing, when, *actions):
        @pl.when(passing & (step == when))
        def _():
            for action, *q in actions:
                action(*q)

    def begin():
        enter(place)
        for q in range(4):
            lead.begin_first(q)
        own_shards(0).start()
        own_shards(1).start()
        load_weights(plan, held, own, (w_qkv, w_out, w_up, w_down), local)

    def lead_finish():
        lead.finish(total)
        unload_shard(plan, place.me, 1, total, flat)
        norm_out[...] = total[SHARD - ROW_TILE : SHARD - ROW_TILE + 8]

    @pl.when(opening & (step == 0))
    def _():
        g_norm[...] = jnp.zeros_like(g_norm)

    if plan is not None:
        at(opening, 0, (begin,))
        at(opening, 1, (lead_second, 0))
        at(opening, 2, (lead_second, 1))
        at(opening, 4, (lead.begin_third, 0))
        at(opening, 5, (lead_second, 2))
        at(opening, 6, (lead.begin_third, 1))
        at(opening, 7, (lead_second, 3))
        at(midway, 0, (lead.begin_z, 3, total), (rest_second, 2))
        at(midway, 2, (rest_second, 3))
        at(midway, 4, (rest.begin_third, 1))
        at(midway, 6, (rest.begin_third, 2))
        at(midway, 7, (rest.begin_z, 1, total_rest))
        at(closing, 1, (rest_second, 0))
        at(closing, 4, (rest.begin_z, 3, total_rest))
        at(closing, 7, (rest.begin_third, 0))

    def side_copy(k):
        source = mixture_hbm if k == 0 else active_hbm.at[:, pl.ds((k - 1) * width, width)]
        return pltpu.make_async_copy(source, side.at[k % 2], side_sem.at[k % 2])

    @pl.when(opening & (step == last))
    def _():
        side_copy(0).start()
        side_copy(1).start()

    @pl.when(opening)
    def _():
        grad_after = grad_ref[...]
        branch = grad_after.astype(bf16)
        branch_all[here, :] = branch
        hidden_backward(branch, w_down, slope_ref, hidden_all.at[here, :])
        grad_second = dot_nt(hidden_all[here, :], w_up[...])
        hat, scale = normalise(middle_ref[...])
        second_all[here, :] = (hat * norm_ref[2:3] + norm_ref[3:4]).astype(bf16)
        grad_rows, gain, shift = norm_backward(hat, scale, norm_ref[2:3], grad_second)
        g_norm[2] += gain
        g_norm[3] += shift
        grad_middle = grad_after + grad_rows
        middle_all[here, :] = grad_middle
        attn_all[here, :] = grad_middle.astype(bf16)

    @pl.when(opening & (step == last))
    def _():
        for start in range(0, hidden, width):
            value = dot_tn(second_all[...], hidden_all[:, start : start + width])
            store(2, 0, start, value.astype(bf16))
            if plan is not None and start == width:
                lead.begin_third(2)
                lead.begin_z(0, total)
        if plan is not None:
            lead.begin_z(1, total)
        side_copy(0).wait()
        store(1, 0, 0, dot_tn(side[0], attn_all[...]).astype(bf16))
        if plan is not None:
            store_norms(plan, own, 0, g_norm, (0, 1, 2, 3))
            rest.begin_first(1)
        count = hidden // width
        for k in range(1, count + 1):
            if k < count:
                side_copy(k + 1).start()
            side_copy(k).wait()
            store(3, (k - 1) * width, 0, dot_tn(side[k % 2], branch_all[...]).astype(bf16))
            if plan is not None:
                if k == 1:
                    rest.begin_first(2)
                    lead.begin_third(3)
                if k == 2:
                    lead.begin_z(2, total)
                if k == 3:
                    rest_second(1)
        if plan is not None:
            rest.begin_first(3)

    @pl.when(midway)
    def _():
        hat, _ = normalise(x_ref[...].astype(f32))
        second_all[here, :] = (hat * norm_ref[0:1] + norm_ref[1:2]).astype(bf16)
        grad_mix[...] = dot_nt(attn_all[here, :], w_out[...]).astype(bf16)
        frame = weights_ref.shape[2]
        low_half = lane_halves(frame)
        for item in range(weights_ref.shape[0]):
            span = slice(item * frame, (item + 1) * frame)
            there = pl.ds(pl.multiple_of(step * tile + item * frame, frame), frame)
            units = []
            for pair in range(HEADS // 2):

                def cut(part, pair=pair, span=span):
                    start = part * width + 128 * pair
                    return packed_ref[span, start : start + 128]

                def cut_grad(pair=pair, span=span):
                    return grad_mix[span, 128 * pair : 128 * (pair + 1)]

                def put(*values, pair=pair, there=there):
                    for part, value in enumerate(values):
                        start = part * width + 128 * pair
                        hidden_all[there, start : start + 128] = value

                units.append((partial(cut, 0), partial(cut, 1), partial(cut, 2), cut_grad, put))
            attend_backward(units, scores, weights_ref.at[item], grad_scores, low_half)

    @pl.when(midway & (step == last))
    def _():
        for start in range(0, 3 * width, width):
            value = dot_tn(second_all[...], hidden_all[:, start : start + width])
            store(0, 0, start, value.astype(bf16))
        if plan is not None:
            rest.begin_first(0)
            rest.begin_third(3)
            rest.begin_z(2, total_rest)
            lead_finish()

    @pl.when(closing)
    def _():
        grad_first = dot_nt(hidden_all[here, 0 : 3 * width], w_qkv[...])
        hat, scale = normalise(x_ref[...].astype(f32))
        grad_rows, gain, shift = norm_backward(hat, scale, norm_ref[0:1], grad_first)
        g_norm[0] += gain
        g_norm[1] += shift
        before_ref[...] = middle_all[here, :] + grad_rows

    if plan is not None:

        @pl.when(closing & (step == last))
        def _():
            own_small[...] = jnp.zeros_like(own_small)
            store_norms(plan, own_small, 0, g_norm, (0,), 0)
            small.begin_first(0)
            rest.start_tail(total_rest, *relay)
            small.begin_second(0, lambda y, x: own_small.at[0, y, x, place.c])
            small.begin_third(0)
            rest.go_on(*relay)
            total_small[...] = jnp.zeros_like(total_small)
            small.begin_z(0, total_small)
            small.finish(total_small)
            rest.finish_tail(total_rest, *relay)
            unload_shard(plan, place.me, 0, total_rest, flat)
            norm_out[...] += total_rest[SHARD - ROW_TILE : SHARD - ROW_TILE + 8]

            @pl.when(place.z == 0)
            def _():
                norm_out[...] += total_small[0:8]


def spatial_backward(plan, x, grad, kept, weights, norms, own_next):
    packed, soft, mixture, middle, active, slope = kept
    tokens, width = x.shape
    hidden = active.shape[1]
    operands, specs, extra = weight_sources(plan, weights, norms, hidden)
    frame = soft.shape[2]
    tile = SPATIAL_TILE
    count = tokens // tile

    def opening(*rest):
        return pl.BlockSpec(rest, lambda p, i: (i + (p + 1) // 2 * (count - 1 - i),) + (0,) * (len(rest) - 1))

    def midway(*rest):
        return pl.BlockSpec(rest, lambda p, i: (p * (2 - p) * i + p // 2 * (count - 1),) + (0,) * (len(rest) - 1))

    def closing(*rest):
        return pl.BlockSpec(rest, lambda p, i: (p // 2 * i,) + (0,) * (len(rest) - 1))

    anywhere = pl.BlockSpec(memory_space=pl.ANY)
    norm_sums = (4, 8, width)
    out_specs, out_shape = [closing(tile, width)], [jax.ShapeDtypeStruct((tokens, width), f32)]
    scratch = [
        pltpu.VMEM((HEADS // 2, frame, 2 * frame), f32),
        pltpu.VMEM((HEADS // 2, frame, 2 * frame), bf16),
        pltpu.VMEM((tile, width), bf16),
        pltpu.VMEM((tokens, width), f32),
        pltpu.VMEM((tokens, width), bf16),
        pltpu.VMEM((tokens, hidden), bf16),
        pltpu.VMEM((tokens, width), bf16),
        pltpu.VMEM((tokens, width), bf16),
        pltpu.VMEM((2, tokens, width), bf16),
        pltpu.SemaphoreType.DMA((2,)),
    ]
    params = dict(vmem_limit_bytes=63 * MIB)
    if plan is None:
        grad_specs, grad_shapes = grad_outputs(plan, width, hidden)
        out_specs += grad_specs + [whole(norm_sums)]
        out_shape += grad_shapes + [jax.ShapeDtypeStruct(norm_sums, f32)]
    else:
        rows = SHARD - ROW_TILE
        for shape in ((2 * rows, LANES), (8, LANES)):
            out_specs.append(whole(shape))
            out_shape.append(jax.ShapeDtypeStruct(shape, f32))
        scratch += [pltpu.VMEM(norm_sums, f32)] + extra + SCATTER_ROOM
        scratch += [
            pltpu.VMEM((SHARD, LANES), f32),
            pltpu.VMEM((SHARD, LANES), f32),
            pltpu.VMEM((4, 2, 2, 2, SHARD, LANES), bf16),
            pltpu.VMEM((2, 2, 2, SHARD, LANES), bf16),
            pltpu.SemaphoreType.DMA((2,)),
            pltpu.SemaphoreType.DMA((2, 6, 4)),
            pltpu.SemaphoreType.DMA((2, 6, 4)),
            pltpu.SemaphoreType.REGULAR((3, 4)),
        ]
        scratch += SMALL_ROOM
        scratch += [
            pltpu.VMEM((SHARD, LANES), bf16),
            pltpu.SemaphoreType.DMA((1,)),
            pltpu.SemaphoreType.DMA((1,)),
        ]
        operands, specs = operands + [own_next], specs + [anywhere]
        params |= dict(collective_id=1, has_side_effects=True)
    return pl.pallas_call(
        partial(spatial_backward_kernel, plan),
        grid=(3, count),
        in_specs=[
            pl.BlockSpec((tile, width), lambda p, i: ((p + 1) // 2 * i, 0)),
            opening(tile, width),
            midway(tile, 3 * width),
            midway(tile // frame, HEADS // 2, frame, 2 * frame),
            opening(tile, width),
            opening(tile, hidden),
            anywhere,
            anywhere,
        ]
        + specs,
        out_specs=out_specs,
        out_shape=out_shape,
        scratch_shapes=scratch,
        compiler_params=pltpu.CompilerParams(**params),
    )(x, grad, packed, soft, middle, slope, mixture, active, *operands)


def unpack(flat_weights, model_width, hidden_width):
    cut_qkv = 3 * model_width * model_width
    cut_out = 4 * model_width * model_width
    cut_up = cut_out + model_width * hidden_width
    return (
        flat_weights[:cut_qkv].reshape(model_width, 3 * model_width),
        flat_weights[cut_qkv:cut_out].reshape(model_width, model_width),
        flat_weights[cut_out:cut_up].reshape(model_width, hidden_width),
        flat_weights[cut_up:].reshape(hidden_width, model_width),
    )


def adamw(param_value, moment, second, grad_total, step_value, rate, decay_rate):
    moment_next = beta_first * moment + (1.0 - beta_first) * grad_total
    second_next = beta_second * second + (1.0 - beta_second) * grad_total * grad_total
    moment_hat = moment_next / (1.0 - beta_first**step_value)
    second_hat = second_next / (1.0 - beta_second**step_value)
    param_next = param_value - rate * (
        moment_hat / (jnp.sqrt(second_hat) + adam_floor) + decay_rate * param_value
    )
    return (param_next, moment_next, second_next)


def interleave(pair):
    return pair.reshape(2, -1, LANES).swapaxes(0, 1).reshape(-1, LANES)


def separate(rows):
    return rows.reshape(-1, 2, LANES).swapaxes(0, 1).reshape(2, -1)


def on_device(
    clip_tokens,
    cotangent,
    lengths,
    params,
    param_moment,
    param_second,
    norm_par,
    norm_moment,
    norm_second,
):
    clip_count, step_slots, patch_count, model_width = clip_tokens.shape
    shards = lax.axis_size("dp")
    plan = shard_plan(shards, model_width, FF) if shards == 32 else None
    x = clip_tokens.reshape(-1, model_width)
    if plan is None:
        gathered = lax.all_gather(params.astype(bf16), "dp", axis=1, tiled=True)
        norm_whole = lax.all_gather(norm_par.astype(bf16), "dp", axis=0, tiled=True)
        norm_table = norm_whole.astype(f32).reshape(2, 4, model_width)
        spatial_weights = unpack(gathered[0], model_width, FF)
        temporal_weights = unpack(gathered[1], model_width, FF)
        sources = (*spatial_weights, norm_table[0])
        *kept, after = spatial_forward(plan, x, sources, patch_count, FF)
    else:
        sources = (interleave(params), norm_par.reshape(1, LANES))
        *kept, after, spatial_weights, temporal_weights, norm_table = spatial_forward(
            plan, x, sources, patch_count, FF
        )
    result, grad_after, *temporal_grads, temporal_norm = temporal_block(
        plan,
        lengths,
        after.reshape(step_slots, patch_count, model_width),
        cotangent.reshape(step_slots, patch_count, model_width),
        temporal_weights,
        norm_table[1] if plan is None else norm_table,
        FF,
    )
    grad_before, *spatial_grads, spatial_norm = spatial_backward(
        plan, x, grad_after.reshape(-1, model_width), kept, spatial_weights, norm_table[0] if plan is None else norm_table,
        temporal_grads[0],
    )
    if plan is None:

        def scatter(grads):
            flat = jnp.concatenate([g.reshape(-1) for g in grads])
            return lax.psum_scatter(flat, "dp", scatter_dimension=0, tiled=True).astype(f32)

        weight_sum = jnp.stack([scatter(spatial_grads), scatter(temporal_grads)])
        norm_grad = jnp.stack([spatial_norm, temporal_norm]).sum(axis=2).reshape(-1)
        norm_sum = lax.psum_scatter(norm_grad, "dp", scatter_dimension=0, tiled=True)
    else:
        weight_sum = spatial_grads[0]
        norm_sum = spatial_norm[0] + spatial_norm[1]
    step_value = float(STEP)
    state = (params, param_moment, param_second)
    if plan is None:
        updated = adamw(*state, weight_sum, step_value, learn_rate, weight_decay)
        new_copy = updated[0].astype(bf16)
    else:
        state = lax.optimization_barrier([interleave(part) for part in state])
        updated = adamw(*state, weight_sum, step_value, learn_rate, weight_decay)
        new_copy = separate(updated[0].astype(bf16))
        updated = [separate(part) for part in updated]
    new_params, new_moment, new_second = updated
    new_norm, new_norm_moment, new_norm_second = adamw(
        norm_par, norm_moment, norm_second, norm_sum, step_value, norm_rate, 0.0
    )
    return (
        result.reshape(clip_tokens.shape),
        grad_before.reshape(clip_tokens.shape),
        new_params,
        new_moment,
        new_second,
        new_copy,
        new_norm,
        new_norm_moment,
        new_norm_second,
    )


def solution(mesh):
    placed = (
        P("dp", None, None, None),
        P("dp", None, None, None),
        P("dp"),
        P(None, "dp"),
        P(None, "dp"),
        P(None, "dp"),
        P("dp"),
        P("dp"),
        P("dp"),
    )
    return jax.shard_map(
        on_device,
        mesh=mesh,
        in_specs=placed,
        out_specs=(
            P("dp", None, None, None),
            P("dp", None, None, None),
            P(None, "dp"),
            P(None, "dp"),
            P(None, "dp"),
            P(None, "dp"),
            P("dp"),
            P("dp"),
            P("dp"),
        ),
        check_vma=False,
    )
```

```python
from functools import partial

import jax
import jax.numpy as jnp
from jax import lax
from jax.experimental import pallas as pl
from jax.experimental.pallas import tpu as pltpu
from jax.sharding import PartitionSpec as P

HEADS = 8
HEAD_DIM = 64
FF = 2048
STEP = 7

norm_epsilon = 1e-05
beta_first = 0.9
beta_second = 0.999
learn_rate = 0.05
norm_rate = 0.5
weight_decay = 0.1
adam_floor = 1e-08
masked_score = -1e30

bf16 = jnp.bfloat16
f32 = jnp.float32
MIB = 2**20

SPATIAL_TILE = 256
TEMPORAL_TILE = 256
PATCH_GROUP = 16


def dot_nn(left, right):
    return lax.dot_general(left, right, (((1,), (0,)), ((), ())), preferred_element_type=f32)


def dot_nt(left, right):
    return lax.dot_general(left, right, (((1,), (1,)), ((), ())), preferred_element_type=f32)


def dot_tn(left, right):
    return lax.dot_general(left, right, (((0,), (0,)), ((), ())), preferred_element_type=f32)


def normalise(rows):
    center = rows - jnp.mean(rows, axis=-1, keepdims=True)
    spread = jnp.mean(center * center, axis=-1, keepdims=True)
    scale = lax.rsqrt(spread + norm_epsilon)
    return center * scale, scale


def fold_rows(rows):
    return jnp.sum(rows.reshape(-1, 8, rows.shape[-1]), axis=0)


def norm_backward(hat, scale, gain, grad):
    weighted = grad * gain
    mean_first = jnp.mean(weighted, axis=-1, keepdims=True)
    mean_second = jnp.mean(weighted * hat, axis=-1, keepdims=True)
    grad_rows = scale * (weighted - mean_first - hat * mean_second)
    return grad_rows, fold_rows(grad * hat), fold_rows(grad)


def gelu_pair(value):
    cumulative = 0.5 + 0.5 * lax.erf(value * 0.7071067811865476)
    density = jnp.exp(-0.5 * value * value) * 0.3989422804014327
    return value * cumulative, cumulative + value * density


def lane_halves(count):
    lane = lax.broadcasted_iota(jnp.int32, (count, 2 * HEAD_DIM), 1)
    return lane < HEAD_DIM


def two_heads(pair, low_half):
    zero = jnp.zeros_like(pair)
    return jnp.concatenate([jnp.where(low_half, pair, zero), jnp.where(low_half, zero, pair)], axis=0)


def own_columns(stacked, low_half):
    rows = stacked.shape[0] // 2
    return jnp.where(low_half, stacked[:rows], stacked[rows:]).astype(bf16)


ROW_CHUNK = 64


def attend(units, scores, soft, low_half, bias):
    rows, double = scores.shape[1:]
    keys = double // 2
    for unit, (query, key, value, put) in enumerate(units):
        scaled = query() * jnp.asarray(HEAD_DIM**-0.5, bf16)
        scores[unit] = dot_nt(scaled, two_heads(key(), low_half))
    for unit in range(len(units)):
        for start in range(0, rows, ROW_CHUNK):
            span = slice(start, start + ROW_CHUNK)
            for half in range(2):
                columns = slice(half * keys, (half + 1) * keys)
                part = scores[unit, span, columns]
                if bias is not None:
                    part = part + bias[span]
                powers = jnp.exp(part - jnp.max(part, axis=-1, keepdims=True))
                part = powers * (1.0 / jnp.sum(powers, axis=-1, keepdims=True))
                soft[unit, span, columns] = part.astype(bf16)
    for unit, (query, key, value, put) in enumerate(units):
        put(dot_nn(soft[unit], two_heads(value(), low_half)).astype(bf16))


def attend_backward(units, scores, soft, grad_scores, low_half):
    rows, double = scores.shape[1:]
    keys = double // 2
    scale = jnp.asarray(HEAD_DIM**-0.5, bf16)
    for unit, (query, key, value, grad, put) in enumerate(units):
        scores[unit] = dot_nt(grad(), two_heads(value(), low_half))
    for unit in range(len(units)):
        for start in range(0, rows, ROW_CHUNK):
            span = slice(start, start + ROW_CHUNK)
            for half in range(2):
                columns = slice(half * keys, (half + 1) * keys)
                wide = soft[unit, span, columns].astype(f32)
                product = scores[unit, span, columns] * wide
                inner = jnp.sum(product, axis=-1, keepdims=True)
                grad_scores[unit, span, columns] = (product - wide * inner).astype(bf16)
    for unit, (query, key, value, grad, put) in enumerate(units):
        grad_value = own_columns(dot_tn(soft[unit], grad()), low_half)
        grad_query = dot_nn(grad_scores[unit], two_heads(key() * scale, low_half)).astype(bf16)
        grad_key = own_columns(dot_tn(grad_scores[unit], query() * scale), low_half)
        put(grad_query, grad_key, grad_value)


def feed_forward(second, w_up, w_down, active_ref, slope_ref, chunk=512):
    hidden = w_up.shape[1]
    for start in range(0, hidden, chunk):
        active, slope = gelu_pair(dot_nn(second, w_up[:, start : start + chunk]))
        active_ref[:, start : start + chunk] = active.astype(bf16)
        slope_ref[:, start : start + chunk] = slope.astype(bf16)
    return dot_nn(active_ref[...], w_down[...])


def hidden_backward(branch, w_down, slope_ref, hidden_ref, chunk=512):
    hidden = w_down.shape[0]
    for start in range(0, hidden, chunk):
        grad = dot_nt(branch, w_down[start : start + chunk, :])
        slope = slope_ref[:, start : start + chunk].astype(f32)
        hidden_ref[:, start : start + chunk] = (grad * slope).astype(bf16)


def spatial_forward_kernel(plan, x_ref, *refs):
    step, last = pl.program_id(1), pl.num_programs(1) - 1
    opening = pl.program_id(0) == 0
    if plan is None:
        w_qkv, w_out, w_up, w_down, norm_ref = refs[:5]
        refs = refs[5:]
        packed_ref, weights_ref, mixture_ref, middle_ref, active_ref, slope_ref, after_ref = refs[:7]
        scores, mixture_all = refs[7:]
    else:
        shard_ref, norm_par_ref = refs[:2]
        refs = refs[2:]
        packed_ref, weights_ref, mixture_ref, middle_ref, active_ref, slope_ref, after_ref = refs[:7]
        held_out, held_next, norm_ref = refs[7:10]
        scores, mixture_all, w_qkv, w_out, w_up, w_down, held, staged, send, recv, local = refs[10:]
        matrices = (w_qkv, w_out, w_up, w_down)
        place = Place(lax.axis_index("dp"))
        order = [place.z] + [k - (place.z + 4 - k) // 4 for k in range(1, 4)]
        now = Gather(place, held, send.at[0], recv.at[0])
        later = Gather(place, held_next, send.at[1], recv.at[1])
        keep = pltpu.make_async_copy(held, held_out, local.at[0])

        def gathered(*planes):
            for q in planes:
                now.finish(q)
            assemble(plan, held, matrices, planes)
            assemble_norms(len(plan), held, norm_ref, planes)

        @pl.when(opening & (step == 0))
        def _():
            enter(place)
            load_shard(plan, place.me, 0, shard_ref, norm_par_ref, held.at[place.z, place.y, place.x, place.c])
            now.start_z()
            load_shard(plan, place.me, 1, shard_ref, norm_par_ref, staged)
            copy = pltpu.make_async_copy(
                staged, held_next.at[place.z, place.y, place.x, place.c], local.at[1]
            )
            copy.start()
            copy.wait()
            now.begin_first(order[0])
            later.begin_first(order[0])
            now.begin_second(order[0])
            later.begin_second(order[0])
            now.begin_first(order[1])
            now.begin_third(order[0])
            now.begin_second(order[1])
            later.start_z()
            now.begin_third(order[1])
            now.begin_first(order[2])
            now.begin_first(order[3])
            gathered(0)

        def at(passing, when, *actions):
            @pl.when(passing & (step == when))
            def _():
                for action, k in actions:
                    action(order[k])

        closing = jnp.logical_not(opening)
        at(opening, 1, (now.begin_second, 2))
        at(opening, 2, (now.begin_second, 3))
        at(opening, 3, (now.begin_third, 2))
        at(opening, 4, (later.begin_first, 1), (later.begin_first, 2), (later.begin_first, 3))
        at(opening, 5, (now.begin_third, 3))
        at(opening, 6, (later.begin_second, 1), (later.begin_third, 0))
        at(opening, 7, (later.begin_second, 2))
        at(closing, 0, (later.begin_second, 3))
        at(closing, 1, (later.begin_third, 1))
        at(closing, 3, (later.begin_third, 2))
        at(closing, 6, (later.begin_third, 3))

        @pl.when(jnp.logical_not(opening) & (step == 0))
        def _():
            gathered(1, 2, 3)
            keep.start()

    tile, width = x_ref.shape
    here = pl.ds(pl.multiple_of(step * tile, tile), tile)

    @pl.when(opening)
    def _():
        hat, _ = normalise(x_ref[...].astype(f32))
        first = (hat * norm_ref[0:1] + norm_ref[1:2]).astype(bf16)
        for start in range(0, 3 * width, 512):
            packed_ref[:, start : start + 512] = dot_nn(first, w_qkv[:, start : start + 512]).astype(bf16)
        frame = weights_ref.shape[2]
        low_half = lane_halves(frame)
        for item in range(weights_ref.shape[0]):
            span = slice(item * frame, (item + 1) * frame)
            units = []
            for pair in range(HEADS // 2):

                def cut(part, pair=pair, span=span):
                    start = part * width + 128 * pair
                    return packed_ref[span, start : start + 128]

                def put(value, pair=pair, span=span):
                    mixture_ref[span, 128 * pair : 128 * (pair + 1)] = value

                units.append((partial(cut, 0), partial(cut, 1), partial(cut, 2), put))
            attend(units, scores, weights_ref.at[item], low_half, None)
        mixture_all[here, :] = mixture_ref[...]

    @pl.when(jnp.logical_not(opening))
    def _():
        middle = x_ref[...].astype(f32) + dot_nn(mixture_all[here, :], w_out[...])
        middle_ref[...] = middle
        hat, _ = normalise(middle)
        second = (hat * norm_ref[2:3] + norm_ref[3:4]).astype(bf16)
        after_ref[...] = middle + feed_forward(second, w_up, w_down, active_ref, slope_ref)

    if plan is not None:

        @pl.when(jnp.logical_not(opening) & (step == last))
        def _():
            for q in range(4):
                later.finish(q)
            keep.wait()
            now.drain()
            later.drain()


def whole(shape):
    return pl.BlockSpec(shape, lambda *_: (0,) * len(shape), pipeline_mode=pl.Buffered(1))


def tiles(tile, *rest):
    return pl.BlockSpec((tile, *rest), lambda i: (i,) + (0,) * len(rest))


def spatial_forward(plan, x, sources, frame, hidden):
    tokens, width = x.shape
    tile = SPATIAL_TILE
    frames = tile // frame
    count = tokens // tile

    def opening(*rest):
        return pl.BlockSpec(rest, lambda p, i: (i + p * (count - 1 - i),) + (0,) * (len(rest) - 1))

    def closing(*rest):
        return pl.BlockSpec(rest, lambda p, i: (i * p,) + (0,) * (len(rest) - 1))

    out_specs = [
        opening(tile, 3 * width),
        opening(frames, HEADS // 2, frame, 2 * frame),
        opening(tile, width),
        closing(tile, width),
        closing(tile, hidden),
        closing(tile, hidden),
        closing(tile, width),
    ]
    out_shape = [
        jax.ShapeDtypeStruct((tokens, 3 * width), bf16),
        jax.ShapeDtypeStruct((tokens // frame, HEADS // 2, frame, 2 * frame), bf16),
        jax.ShapeDtypeStruct((tokens, width), bf16),
        jax.ShapeDtypeStruct((tokens, width), f32),
        jax.ShapeDtypeStruct((tokens, hidden), bf16),
        jax.ShapeDtypeStruct((tokens, hidden), bf16),
        jax.ShapeDtypeStruct((tokens, width), f32),
    ]
    scratch = [pltpu.VMEM((HEADS // 2, frame, 2 * frame), f32), pltpu.VMEM((tokens, width), bf16)]
    params = dict(vmem_limit_bytes=60 * MIB)
    if plan is not None:
        held = (4, 2, 2, 2, SHARD, LANES)
        out_specs += [pl.BlockSpec(memory_space=pl.ANY)] * 2 + [whole((8, width))]
        out_shape += [jax.ShapeDtypeStruct(held, bf16)] * 2 + [jax.ShapeDtypeStruct((8, width), f32)]
        scratch += [pltpu.VMEM(shape, bf16) for shape in matrix_shapes(width, hidden)]
        scratch += [
            pltpu.VMEM(held, bf16),
            pltpu.VMEM((SHARD, LANES), bf16),
            pltpu.SemaphoreType.DMA((2, 6, 4)),
            pltpu.SemaphoreType.DMA((2, 6, 4)),
            pltpu.SemaphoreType.DMA((2,)),
        ]
        params |= dict(collective_id=0, has_side_effects=True)
    return pl.pallas_call(
        partial(spatial_forward_kernel, plan),
        grid=(2, count),
        in_specs=[pl.BlockSpec((tile, width), lambda p, i: (i, 0))] + [whole(a.shape) for a in sources],
        out_specs=out_specs,
        out_shape=out_shape,
        scratch_shapes=scratch,
        compiler_params=pltpu.CompilerParams(**params),
    )(x, *sources)


MESH_IDS = pl.DeviceIdType.MESH
LANES = 128
ROW_TILE = 16


def matrix_shapes(width, hidden):
    return ((width, 3 * width), (width, width), (width, hidden), (hidden, width))


def shard_plan(shards, width, hidden):
    plan = []
    base = 0
    regions = []
    for index, (rows, columns) in enumerate(matrix_shapes(width, hidden)):
        regions.append((index, base, rows, columns))
        base += rows * columns
    if base % shards:
        return None
    size = base // shards
    for device in range(shards):
        low, high = device * size, (device + 1) * size
        halves = ([], [])
        for index, start, rows, columns in regions:
            first, last = max(low, start), min(high, start + rows * columns)
            if first >= last:
                continue
            if (first - start) % columns or (last - start) % columns:
                return None
            row, count = (first - start) // columns, (last - first) // columns
            if row % ROW_TILE or count % ROW_TILE:
                return None
            stride = columns // LANES
            for block in range(stride):
                halves[2 * block // stride].append(
                    (index, row, count, block, (first - low) // LANES + block, stride)
                )
        place = 0
        entries = []
        for item in halves[0] + halves[1]:
            entries.append(item + (place,))
            place += item[2]
        plan.append(entries)
    return plan


def by_pattern(plan):
    groups = {}
    for device, entries in enumerate(plan):
        layout = tuple((e[2], e[4], e[5], e[6]) for e in entries)
        ranges = groups.setdefault(layout, [])
        if ranges and ranges[-1][1] == device:
            ranges[-1][1] = device + 1
        else:
            ranges.append([device, device + 1])
    return list(groups.items())


def on_pattern(plan, me, body):
    for layout, ranges in by_pattern(plan):
        inside = None
        for low, high in ranges:
            test = (me >= low) & (me < high)
            inside = test if inside is None else inside | test

        @pl.when(inside)
        def _(layout=layout):
            body(layout)


class Place:
    def __init__(self, me):
        self.me = me
        self.c = lax.rem(me, 2)
        self.x = lax.rem(me // 2, 2)
        self.y = lax.rem(me // 4, 2)
        self.z = me // 8

    def device(self, z, y, x, c):
        return ((z * 2 + y) * 2 + x) * 2 + c

    @property
    def sibling(self):
        return self.device(self.z, self.y, self.x, 1 - self.c)

    @property
    def across_x(self):
        return self.device(self.z, self.y, 1 - self.x, self.c)

    @property
    def across_y(self):
        return self.device(self.z, 1 - self.y, self.x, self.c)

    def plane(self, z):
        return self.device(z, self.y, self.x, self.c)


def remote(src, dst, send, recv, device):
    return pltpu.make_async_remote_copy(
        src_ref=src, dst_ref=dst, send_sem=send, recv_sem=recv, device_id=(device,), device_id_type=MESH_IDS
    )


def enter(place):
    barrier = pltpu.get_barrier_semaphore()
    partners = [place.sibling, place.across_x, place.across_y]
    partners += [place.plane(lax.rem(place.z + k, 4)) for k in range(1, 4)]
    for device in partners:
        pl.semaphore_signal(barrier, inc=1, device_id=(device,), device_id_type=MESH_IDS)
    pl.semaphore_wait(barrier, len(partners))


HALF = 384
SHARD = 784


class Gather:
    SEMS = 9

    def __init__(self, place, held, send, recv):
        self.p, self.held, self.send, self.recv = place, held, send, recv

    def along_z(self, k):
        p = self.p
        here = self.held.at[p.z, p.y, p.x, p.c]
        return remote(here, here, self.send.at[0, k - 1], self.recv.at[0, p.z], p.plane(lax.rem(p.z + k, 4)))

    def start_z(self):
        for k in range(1, 4):
            self.along_z(k).start()

    def wait_z(self, q):
        p = self.p

        @pl.when(q != p.z)
        def _():
            there = self.held.at[q, p.y, p.x, p.c]
            remote(there, there, self.send.at[0, 0], self.recv.at[0, q], p.me).wait_recv()

    def first(self, q):
        p, h = self.p, self.held
        a = h.at[q, p.y, p.x, p.c, pl.ds(0, HALF)]
        b = h.at[q, p.y, p.x, p.c, pl.ds(HALF, SHARD - HALF)]
        return (
            remote(a, a, self.send.at[1, q], self.recv.at[1, q], p.across_x),
            remote(b, b, self.send.at[2, q], self.recv.at[2, q], p.across_y),
        )

    def second(self, q):
        p, h = self.p, self.held
        a = h.at[q, p.y, :, p.c, pl.ds(0, HALF)]
        b = h.at[q, :, p.x, p.c, pl.ds(HALF, SHARD - HALF)]
        return (
            remote(a, a, self.send.at[3, q], self.recv.at[3, q], p.across_y),
            remote(b, b, self.send.at[4, q], self.recv.at[4, q], p.across_x),
        )

    def third(self, q):
        p, h = self.p, self.held
        a = h.at[q, :, :, p.c]
        return (remote(a, a, self.send.at[5, q], self.recv.at[5, q], p.sibling),)

    def begin_first(self, q):
        self.wait_z(q)
        for copy in self.first(q):
            copy.start()

    def begin_second(self, q):
        for copy in self.first(q):
            copy.wait_recv()
        for copy in self.second(q):
            copy.start()

    def begin_third(self, q):
        for copy in self.second(q):
            copy.wait_recv()
        for copy in self.third(q):
            copy.start()

    def finish(self, q):
        for copy in self.third(q):
            copy.wait_recv()

    def drain(self):
        for k in range(1, 4):
            self.along_z(k).wait_send()
        for q in range(4):
            for copy in self.first(q) + self.second(q) + self.third(q):
                copy.wait_send()


def load_shard(plan, me, block, shard_ref, norm_ref, held_here):
    def body(layout):
        for count, flat, stride, place in layout:
            held_here[pl.ds(place, count), :] = shard_ref[pl.ds(2 * flat + block, count, 2 * stride), :].astype(bf16)

    on_pattern(plan, me, body)
    held_here[SHARD - ROW_TILE :, :] = jnp.broadcast_to(norm_ref[...], (ROW_TILE, LANES)).astype(bf16)


def coordinates(device):
    return device // 8, device // 4 % 2, device // 2 % 2, device % 2


def assemble(plan, held, outs, planes):
    for device, entries in enumerate(plan):
        z, y, x, c = coordinates(device)
        if z not in planes:
            continue
        for index, row, count, block, _, _, place in entries:
            outs[index][row : row + count, LANES * block : LANES * (block + 1)] = held[
                z, y, x, c, place : place + count, :
            ]


def assemble_norms(shards, held, norm_out, planes):
    per_row = norm_out.shape[1] // LANES
    for device in range(shards):
        z, y, x, c = coordinates(device)
        if z not in planes:
            continue
        row, column = device // per_row, device % per_row
        norm_out[row : row + 1, LANES * column : LANES * (column + 1)] = held[
            z, y, x, c, SHARD - ROW_TILE : SHARD, :
        ].astype(f32)[0:1]


def accumulate(into, part, chunk):
    def body(i, _):
        span = pl.ds(pl.multiple_of(i * chunk, ROW_TILE), chunk)
        into[span, :] = into[span, :] + part[span, :]
        return 0

    lax.fori_loop(0, into.shape[0] // chunk, body, 0)


class Scatter:
    def __init__(self, place, own, room, send, recv, credit=None, leads=None):
        self.p, self.own = place, own
        rows, half = room[3].shape[1], room[1].shape[2]
        self.low, self.high = pl.ds(0, half), pl.ds(half, rows - half)
        self.chunk, self.chunk_low, self.chunk_high = (112, 128, 80) if rows == SHARD else (ROW_TILE,) * 3
        self.r1, self.r2a, self.r2b, self.r3, self.r4 = room
        self.send, self.recv, self.credit, self.leads = send, recv, credit, leads

    def release(self, kind, q, device):
        if self.leads is True:
            pl.semaphore_signal(self.credit.at[kind, q], inc=1, device_id=(device,), device_id_type=MESH_IDS)

    def claim(self, kind, q):
        if self.leads is False:
            pl.semaphore_wait(self.credit.at[kind, q], 1)

    def first(self, q):
        p = self.p
        return (
            remote(
                self.own.at[q, :, :, 1 - p.c], self.r1.at[q], self.send.at[0, q], self.recv.at[0, q], p.sibling
            ),
        )

    def second(self, q):
        p = self.p
        low, high = self.low, self.high
        return (
            remote(
                self.r1.at[q, :, 1 - p.x, low], self.r2a.at[q], self.send.at[1, q], self.recv.at[1, q], p.across_x
            ),
            remote(
                self.r1.at[q, 1 - p.y, :, high], self.r2b.at[q], self.send.at[2, q], self.recv.at[2, q], p.across_y
            ),
        )

    def third(self, q):
        p = self.p
        low, high = self.low, self.high
        return (
            remote(
                self.r2a.at[q, 1 - p.y], self.r3.at[q, low], self.send.at[3, q], self.recv.at[3, q], p.across_y
            ),
            remote(
                self.r2b.at[q, 1 - p.x], self.r3.at[q, high], self.send.at[4, q], self.recv.at[4, q], p.across_x
            ),
        )

    def along_z(self, q):
        p = self.p
        return remote(self.r3.at[q], self.r4.at[p.z], self.send.at[5, q], self.recv.at[5, p.z], p.plane(q))

    def begin_first(self, q):
        self.claim(0, q)
        for copy in self.first(q):
            copy.start()

    def begin_second(self, q, mine):
        for copy in self.first(q):
            copy.wait_recv()
        for y in range(2):
            for x in range(2):
                accumulate(self.r1.at[q, y, x], mine(y, x), self.chunk)
        self.claim(1, q)
        self.claim(2, q)
        for copy in self.second(q):
            copy.start()

    def begin_third(self, q):
        p = self.p
        for copy in self.second(q):
            copy.wait_recv()
        low, high = self.low, self.high
        for k in range(2):
            accumulate(self.r2a.at[q, k], self.r1.at[q, k, p.x, low], self.chunk_low)
            accumulate(self.r2b.at[q, k], self.r1.at[q, p.y, k, high], self.chunk_high)
        for copy in self.third(q):
            copy.start()
        for copy in self.second(q):
            copy.wait_send()
        self.release(0, q, p.sibling)

    def begin_z(self, q, total):
        p = self.p
        for copy in self.third(q):
            copy.wait_recv()
        low, high = self.low, self.high
        accumulate(self.r3.at[q, low], self.r2a.at[q, p.y], self.chunk_low)
        accumulate(self.r3.at[q, high], self.r2b.at[q, p.x], self.chunk_high)

        @pl.when(q != p.z)
        def _():
            self.along_z(q).start()

        @pl.when(q == p.z)
        def _():
            total[...] = self.r3[q].astype(f32)

        for copy in self.third(q):
            copy.wait_send()
        self.release(1, q, p.across_x)
        self.release(2, q, p.across_y)

    def leave_z(self, q):
        p = self.p

        @pl.when(q != p.z)
        def _():
            self.along_z(q).wait_send()

    def finish(self, total):
        p = self.p
        planes = self.r3.shape[0]

        @pl.when(p.z < planes)
        def _():
            for k in range(1, 4):
                z = lax.rem(p.z + k, 4)
                remote(self.r3.at[0], self.r4.at[z], self.send.at[5, 0], self.recv.at[5, z], p.me).wait_recv()
            for k in range(1, 4):
                total[...] += self.r4[lax.rem(p.z + k, 4)].astype(f32)

        for q in range(planes):
            for copy in self.first(q):
                copy.wait_send()
            self.leave_z(q)


class Relay(Scatter):
    def hand_on(self, room, send, recv, device):
        return remote(self.r3.at[0], room, send.at[0], recv.at[0], device)

    def start_tail(self, total, room, send, recv):
        p = self.p
        for copy in self.third(0):
            copy.wait_recv()
        accumulate(self.r3.at[0, self.low], self.r2a.at[0, p.y], self.chunk_low)
        accumulate(self.r3.at[0, self.high], self.r2b.at[0, p.x], self.chunk_high)

        @pl.when(p.z == 3)
        def _():
            self.hand_on(room, send, recv, p.plane(2)).start()

        @pl.when(p.z == 1)
        def _():
            self.along_z(0).start()

        @pl.when(p.z == 0)
        def _():
            total[...] = self.r3[0].astype(f32)

        for copy in self.third(0):
            copy.wait_send()

    def go_on(self, room, send, recv):
        @pl.when(self.p.z == 2)
        def _():
            self.hand_on(room, send, recv, self.p.me).wait_recv()
            accumulate(self.r3.at[0], room, self.chunk)
            self.along_z(0).start()

    def finish_tail(self, total, room, send, recv):
        p = self.p

        def arrive(z):
            remote(self.r3.at[0], self.r4.at[z], self.send.at[5, 0], self.recv.at[5, z], p.me).wait_recv()

        @pl.when(p.z == 0)
        def _():
            for z in (1, 2):
                arrive(z)
                total[...] += self.r4[z].astype(f32)

        @pl.when(p.z > 0)
        def _():
            for k in range(1, 4):
                z = lax.rem(p.z + k, 4)
                arrive(z)
                total[...] += self.r4[z].astype(f32)

        for q in range(4):
            for copy in self.first(q):
                copy.wait_send()
        for q in range(1, 4):
            self.leave_z(q)

        @pl.when((p.z == 1) | (p.z == 2))
        def _():
            self.along_z(0).wait_send()

        @pl.when(p.z == 3)
        def _():
            self.hand_on(room, send, recv, p.plane(2)).wait_send()


SCATTER_ROOM = [
    pltpu.VMEM((4, 2, 2, SHARD, LANES), bf16),
    pltpu.VMEM((4, 2, HALF, LANES), bf16),
    pltpu.VMEM((4, 2, SHARD - HALF, LANES), bf16),
    pltpu.VMEM((2, 4, SHARD, LANES), bf16),
    pltpu.VMEM((2, 4, SHARD, LANES), bf16),
]

SMALL = 2 * ROW_TILE
SMALL_ROOM = [
    pltpu.VMEM((1, 2, 2, 2, SMALL, LANES), bf16),
    pltpu.VMEM((1, 2, 2, SMALL, LANES), bf16),
    pltpu.VMEM((1, 2, ROW_TILE, LANES), bf16),
    pltpu.VMEM((1, 2, ROW_TILE, LANES), bf16),
    pltpu.VMEM((1, SMALL, LANES), bf16),
    pltpu.VMEM((4, SMALL, LANES), bf16),
    pltpu.VMEM((SMALL, LANES), f32),
    pltpu.SemaphoreType.DMA((6, 4)),
    pltpu.SemaphoreType.DMA((6, 4)),
]


def unload_shard(plan, me, block, total, flat_ref):
    def body(layout):
        for count, flat, stride, place in layout:
            flat_ref[pl.ds(2 * flat + block, count, 2 * stride), :] = total[pl.ds(place, count), :]

    on_pattern(plan, me, body)


def store_travel(plan, own, index, top, start, value):
    for device, entries in enumerate(plan):
        z, y, x, c = coordinates(device)
        for entry, row, count, block, _, _, place in entries:
            column = LANES * block - start
            low, high = max(row, top), min(row + count, top + value.shape[0])
            if entry == index and 0 <= column < value.shape[1] and low < high:
                own[z, y, x, c, place + low - row : place + high - row, :] = value[
                    low - top : high - top, column : column + LANES
                ]


def store_norms(plan, own, block, sums, planes, first=SHARD - ROW_TILE):
    width = sums.shape[2]
    per_row = width // LANES
    line = lax.broadcasted_iota(jnp.int32, (ROW_TILE, LANES), 0)
    for device in range(len(plan)):
        z, y, x, c = coordinates(device)
        if z not in planes:
            continue
        row = device // per_row - 4 * block
        if 0 <= row < 4:
            column = LANES * (device % per_row)
            value = jnp.sum(sums[row, :, column : column + LANES], axis=0, keepdims=True)
            coarse = value.astype(bf16).astype(f32)
            rows = jnp.where(line == 0, coarse, jnp.where(line == 1, value - coarse, 0.0))
        else:
            rows = jnp.zeros((ROW_TILE, LANES), f32)
        own[z, y, x, c, first : first + ROW_TILE, :] = rows.astype(bf16)


def weight_grads(first, grad_packed, mixture, attn, second, grad_hidden, active, branch, store, chunk=512):
    sides = ((first, grad_packed), (mixture, attn), (second, grad_hidden), (active, branch))
    for index, (left, right) in enumerate(sides):
        for start in range(0, right.shape[1], chunk):
            store(index, 0, start, dot_tn(left[...], right[:, start : start + chunk]).astype(bf16))


def grad_outputs(plan, width, hidden):
    shapes = matrix_shapes(width, hidden) if plan is None else [(4, 2, 2, 2, SHARD, LANES)]
    return [whole(s) for s in shapes], [jax.ShapeDtypeStruct(s, bf16) for s in shapes]


def storing(plan, outs):
    if plan is None:
        def store(index, top, start, value):
            outs[index][top : top + value.shape[0], start : start + value.shape[1]] = value
        return store
    return partial(store_travel, plan, outs[0])


def temporal_kernel(
    plan, length_ref, rows_ref, cotangent_ref, *refs
):
    sources = 5 if plan is None else 2
    refs, sources = refs[sources:], refs[:sources]
    result_ref, before_ref, *refs = refs
    if plan is None:
        w_qkv, w_out, w_up, w_down, norm_ref = sources
    else:
        *refs, w_qkv, w_out, w_up, w_down, local = refs
        norm_ref = sources[1].at[4:8]
    outs, g_norm = refs[:-15], refs[-15]
    packed, slope, weights_buf, grad_mix, scores, grad_scores = refs[-14:-8]
    first_all, packed_all, mixture_all, attn_all, second_all, hidden_all, active_all, branch_all = refs[-8:]
    step = pl.program_id(0)
    steps, patches, width = rows_ref.shape
    tile = steps * patches
    here = pl.ds(pl.multiple_of(step * tile, tile), tile)
    length = length_ref[0]
    group = PATCH_GROUP
    count = steps * group

    @pl.when(step == 0)
    def _():
        g_norm[...] = jnp.zeros_like(g_norm)
        if plan is not None:
            load_weights(plan, sources[0], outs[0], (w_qkv, w_out, w_up, w_down), local)

    row = lax.broadcasted_iota(jnp.int32, (count, count), 0)
    column = lax.broadcasted_iota(jnp.int32, (count, count), 1)
    seen = (row % group == column % group) & (column // group <= row // group)
    seen = seen & (column // group < length)
    bias = jnp.where(seen, 0.0, masked_score)
    low_half = lane_halves(count)

    rows = rows_ref[...].reshape(tile, width)
    hat, _ = normalise(rows)
    first = (hat * norm_ref[0:1] + norm_ref[1:2]).astype(bf16)
    first_all[here, :] = first
    packed[...] = dot_nn(first, w_qkv[...]).astype(bf16).reshape(packed.shape)

    mixture_view = mixture_all.at[here, :]

    def cut(source, part, place, pair):
        start = part * width + 128 * pair
        return source[:, place : place + group, start : start + 128].reshape(count, 128)

    def units_of(backward):
        units = []
        for place in range(0, patches, group):
            for pair in range(HEADS // 2):

                def put(*values, place=place, pair=pair):
                    for part, value in enumerate(values):
                        start = part * width + 128 * pair
                        into = packed if backward else grad_mix
                        into[:, place : place + group, start : start + 128] = value.reshape(steps, group, 128)

                gets = [partial(cut, packed, part, place, pair) for part in range(3)]
                if backward:
                    gets.append(partial(cut, grad_mix, 0, place, pair))
                units.append((*gets, put))
        return units

    attend(units_of(False), scores, weights_buf, low_half, bias)
    mixture = grad_mix[...].reshape(tile, width)
    mixture_all[here, :] = mixture
    middle = rows + dot_nn(mixture, w_out[...])
    hat, scale = normalise(middle)
    second = (hat * norm_ref[2:3] + norm_ref[3:4]).astype(bf16)
    second_all[here, :] = second
    after = middle + feed_forward(second, w_up, w_down, active_all.at[here, :], slope)
    result_ref[...] = after.reshape(result_ref.shape)

    slot = lax.broadcasted_iota(jnp.int32, rows_ref.shape, 0)
    live = (slot < length).astype(f32)
    grad_after = (cotangent_ref[...].astype(f32) * live).reshape(tile, width)
    branch = grad_after.astype(bf16)
    branch_all[here, :] = branch
    hidden_backward(branch, w_down, slope, hidden_all.at[here, :])
    grad_second = dot_nt(hidden_all[here, :], w_up[...])
    hat, scale = normalise(middle)
    grad_rows, gain, shift = norm_backward(hat, scale, norm_ref[2:3], grad_second)
    g_norm[2] += gain
    g_norm[3] += shift
    grad_middle = grad_after + grad_rows
    attn = grad_middle.astype(bf16)
    attn_all[here, :] = attn
    grad_mix[...] = dot_nt(attn, w_out[...]).astype(bf16).reshape(grad_mix.shape)
    attend_backward(units_of(True), scores, weights_buf, grad_scores, low_half)
    grad_packed = packed[...].reshape(tile, 3 * width)
    packed_all[here, :] = grad_packed
    grad_first = dot_nt(grad_packed, w_qkv[...])
    hat, scale = normalise(rows)
    grad_rows, gain, shift = norm_backward(hat, scale, norm_ref[0:1], grad_first)
    g_norm[0] += gain
    g_norm[1] += shift
    before_ref[...] = (grad_middle + grad_rows).reshape(before_ref.shape)

    @pl.when(step == pl.num_programs(0) - 1)
    def _():
        if plan is not None:
            store_norms(plan, outs[0], 1, g_norm, range(4))
        weight_grads(
            first_all, packed_all, mixture_all, attn_all, second_all, hidden_all, active_all,
            branch_all, storing(plan, outs),
        )


def load_weights(plan, held, room, matrices, local):
    copies = [pltpu.make_async_copy(held.at[z], room.at[z], local.at[z]) for z in range(4)]
    for copy in copies:
        copy.start()
    for z, copy in enumerate(copies):
        copy.wait()
        assemble(plan, room, matrices, (z,))


def weight_sources(plan, weights, norms, hidden):
    width = norms.shape[1]
    if plan is None:
        return [*weights, norms], [whole(a.shape) for a in (*weights, norms)], []
    scratch = [pltpu.VMEM(shape, bf16) for shape in matrix_shapes(width, hidden)]
    scratch.append(pltpu.SemaphoreType.DMA((4,)))
    return [weights, norms], [pl.BlockSpec(memory_space=pl.ANY), whole(norms.shape)], scratch


def temporal_block(plan, length, rows, cotangent, weights, norms, hidden):
    grad_specs, grad_shapes = grad_outputs(plan, norms.shape[1], hidden)
    operands, specs, extra = weight_sources(plan, weights, norms, hidden)
    steps, patches, width = rows.shape
    tokens = steps * patches
    part = TEMPORAL_TILE // steps
    count = steps * PATCH_GROUP
    unit_shape = (part // PATCH_GROUP * (HEADS // 2), count, 2 * count)
    slab = pl.BlockSpec((steps, part, width), lambda i: (0, i, 0))
    return pl.pallas_call(
        partial(temporal_kernel, plan),
        grid=(patches // part,),
        in_specs=[pl.BlockSpec(memory_space=pltpu.SMEM), slab, slab] + specs,
        out_specs=[slab, slab] + grad_specs + [whole((4, 8, width))],
        out_shape=[
            jax.ShapeDtypeStruct(rows.shape, f32),
            jax.ShapeDtypeStruct(rows.shape, f32),
        ]
        + grad_shapes
        + [jax.ShapeDtypeStruct((4, 8, width), f32)],
        scratch_shapes=[
            pltpu.VMEM((steps, part, 3 * width), bf16),
            pltpu.VMEM((TEMPORAL_TILE, hidden), bf16),
            pltpu.VMEM(unit_shape, bf16),
            pltpu.VMEM((steps, part, width), bf16),
            pltpu.VMEM(unit_shape, f32),
            pltpu.VMEM(unit_shape, bf16),
            pltpu.VMEM((tokens, width), bf16),
            pltpu.VMEM((tokens, 3 * width), bf16),
            pltpu.VMEM((tokens, width), bf16),
            pltpu.VMEM((tokens, width), bf16),
            pltpu.VMEM((tokens, width), bf16),
            pltpu.VMEM((tokens, hidden), bf16),
            pltpu.VMEM((tokens, hidden), bf16),
            pltpu.VMEM((tokens, width), bf16),
        ]
        + extra,
        compiler_params=pltpu.CompilerParams(vmem_limit_bytes=62 * MIB),
    )(length, rows, cotangent, *operands)


def spatial_backward_kernel(
    plan, x_ref, grad_ref, packed_ref, weights_ref, middle_ref, slope_ref, mixture_hbm, active_hbm, *refs
):
    step, last = pl.program_id(1), pl.num_programs(1) - 1
    opening, midway, closing = [pl.program_id(0) == k for k in range(3)]
    if plan is None:
        w_qkv, w_out, w_up, w_down, norm_ref, before_ref, *outs, g_norm = refs[:11]
        refs = refs[11:]
    else:
        held, norm_ref, own_next, before_ref, flat, norm_out = refs[:6]
        own_small, *room_small, total_small, send_small, recv_small = refs[-len(SMALL_ROOM) - 3 : -3]
        relay = refs[-3:]
        *refs, total, total_rest, own, mine, load, send, recv, credit = refs[6 : -len(SMALL_ROOM) - 3]
        room, refs = refs[-5:], refs[:-5]
        *refs, g_norm, w_qkv, w_out, w_up, w_down, local = refs
        outs = [own]
        place = Place(lax.axis_index("dp"))
        rooms = [(*room[:3], room[3].at[k], room[4].at[k]) for k in range(2)]
        lead = Scatter(place, own_next, rooms[0], send.at[0], recv.at[0], credit, True)
        rest = Relay(place, own, rooms[1], send.at[1], recv.at[1], credit, False)
        small = Scatter(place, own_small, room_small, send_small, recv_small)
    scores, grad_scores, grad_mix, middle_all, second_all, hidden_all, attn_all, branch_all, side, side_sem = refs
    store = storing(plan, outs)
    tile, width = x_ref.shape
    hidden = slope_ref.shape[1]
    here = pl.ds(pl.multiple_of(step * tile, tile), tile)

    def own_shards(q):
        return pltpu.make_async_copy(own_next.at[q, :, :, place.c], mine.at[q % 2], load.at[q % 2])

    def lead_second(q):
        own_shards(q).wait()
        lead.begin_second(q, lambda y, x: mine.at[q % 2, y, x])
        if q < 2:
            own_shards(q + 2).start()

    def rest_second(q):
        rest.begin_second(q, lambda y, x: own.at[q, y, x, place.c])

    def at(passing, when, *actions):
        @pl.when(passing & (step == when))
        def _():
            for action, *q in actions:
                action(*q)

    def begin():
        enter(place)
        for q in range(4):
            lead.begin_first(q)
        own_shards(0).start()
        own_shards(1).start()
        load_weights(plan, held, own, (w_qkv, w_out, w_up, w_down), local)

    def lead_finish():
        lead.finish(total)
        unload_shard(plan, place.me, 1, total, flat)
        norm_out[...] = total[SHARD - ROW_TILE : SHARD - ROW_TILE + 8]

    @pl.when(opening & (step == 0))
    def _():
        g_norm[...] = jnp.zeros_like(g_norm)

    if plan is not None:
        at(opening, 0, (begin,))
        at(opening, 1, (lead_second, 0))
        at(opening, 2, (lead_second, 1))
        at(opening, 4, (lead.begin_third, 0))
        at(opening, 5, (lead_second, 2))
        at(opening, 6, (lead.begin_third, 1))
        at(opening, 7, (lead_second, 3))
        at(midway, 0, (lead.begin_z, 3, total), (rest_second, 2))
        at(midway, 2, (rest_second, 3))
        at(midway, 4, (rest.begin_third, 1))
        at(midway, 6, (rest.begin_third, 2))
        at(midway, 7, (rest.begin_z, 1, total_rest))
        at(closing, 1, (rest_second, 0))
        at(closing, 4, (rest.begin_z, 3, total_rest))
        at(closing, 7, (rest.begin_third, 0))

    def side_copy(k):
        source = mixture_hbm if k == 0 else active_hbm.at[:, pl.ds((k - 1) * width, width)]
        return pltpu.make_async_copy(source, side.at[k % 2], side_sem.at[k % 2])

    @pl.when(opening & (step == last))
    def _():
        side_copy(0).start()
        side_copy(1).start()

    @pl.when(opening)
    def _():
        grad_after = grad_ref[...]
        branch = grad_after.astype(bf16)
        branch_all[here, :] = branch
        hidden_backward(branch, w_down, slope_ref, hidden_all.at[here, :])
        grad_second = dot_nt(hidden_all[here, :], w_up[...])
        hat, scale = normalise(middle_ref[...])
        second_all[here, :] = (hat * norm_ref[2:3] + norm_ref[3:4]).astype(bf16)
        grad_rows, gain, shift = norm_backward(hat, scale, norm_ref[2:3], grad_second)
        g_norm[2] += gain
        g_norm[3] += shift
        grad_middle = grad_after + grad_rows
        middle_all[here, :] = grad_middle
        attn_all[here, :] = grad_middle.astype(bf16)

    @pl.when(opening & (step == last))
    def _():
        for start in range(0, hidden, width):
            value = dot_tn(second_all[...], hidden_all[:, start : start + width])
            store(2, 0, start, value.astype(bf16))
            if plan is not None and start == width:
                lead.begin_third(2)
                lead.begin_z(0, total)
        if plan is not None:
            lead.begin_z(1, total)
        side_copy(0).wait()
        store(1, 0, 0, dot_tn(side[0], attn_all[...]).astype(bf16))
        if plan is not None:
            store_norms(plan, own, 0, g_norm, (0, 1, 2, 3))
            rest.begin_first(1)
        count = hidden // width
        for k in range(1, count + 1):
            if k < count:
                side_copy(k + 1).start()
            side_copy(k).wait()
            store(3, (k - 1) * width, 0, dot_tn(side[k % 2], branch_all[...]).astype(bf16))
            if plan is not None:
                if k == 1:
                    rest.begin_first(2)
                    lead.begin_third(3)
                if k == 2:
                    lead.begin_z(2, total)
                if k == 3:
                    rest_second(1)
        if plan is not None:
            rest.begin_first(3)

    @pl.when(midway)
    def _():
        hat, _ = normalise(x_ref[...].astype(f32))
        second_all[here, :] = (hat * norm_ref[0:1] + norm_ref[1:2]).astype(bf16)
        grad_mix[...] = dot_nt(attn_all[here, :], w_out[...]).astype(bf16)
        frame = weights_ref.shape[2]
        low_half = lane_halves(frame)
        for item in range(weights_ref.shape[0]):
            span = slice(item * frame, (item + 1) * frame)
            there = pl.ds(pl.multiple_of(step * tile + item * frame, frame), frame)
            units = []
            for pair in range(HEADS // 2):

                def cut(part, pair=pair, span=span):
                    start = part * width + 128 * pair
                    return packed_ref[span, start : start + 128]

                def cut_grad(pair=pair, span=span):
                    return grad_mix[span, 128 * pair : 128 * (pair + 1)]

                def put(*values, pair=pair, there=there):
                    for part, value in enumerate(values):
                        start = part * width + 128 * pair
                        hidden_all[there, start : start + 128] = value

                units.append((partial(cut, 0), partial(cut, 1), partial(cut, 2), cut_grad, put))
            attend_backward(units, scores, weights_ref.at[item], grad_scores, low_half)

    @pl.when(midway & (step == last))
    def _():
        for start in range(0, 3 * width, width):
            value = dot_tn(second_all[...], hidden_all[:, start : start + width])
            store(0, 0, start, value.astype(bf16))
        if plan is not None:
            rest.begin_first(0)
            rest.begin_third(3)
            rest.begin_z(2, total_rest)
            lead_finish()

    @pl.when(closing)
    def _():
        grad_first = dot_nt(hidden_all[here, 0 : 3 * width], w_qkv[...])
        hat, scale = normalise(x_ref[...].astype(f32))
        grad_rows, gain, shift = norm_backward(hat, scale, norm_ref[0:1], grad_first)
        g_norm[0] += gain
        g_norm[1] += shift
        before_ref[...] = middle_all[here, :] + grad_rows

    if plan is not None:

        @pl.when(closing & (step == last))
        def _():
            own_small[...] = jnp.zeros_like(own_small)
            store_norms(plan, own_small, 0, g_norm, (0,), 0)
            small.begin_first(0)
            rest.start_tail(total_rest, *relay)
            small.begin_second(0, lambda y, x: own_small.at[0, y, x, place.c])
            small.begin_third(0)
            rest.go_on(*relay)
            total_small[...] = jnp.zeros_like(total_small)
            small.begin_z(0, total_small)
            small.finish(total_small)
            rest.finish_tail(total_rest, *relay)
            unload_shard(plan, place.me, 0, total_rest, flat)
            norm_out[...] += total_rest[SHARD - ROW_TILE : SHARD - ROW_TILE + 8]

            @pl.when(place.z == 0)
            def _():
                norm_out[...] += total_small[0:8]


def spatial_backward(plan, x, grad, kept, weights, norms, own_next):
    packed, soft, mixture, middle, active, slope = kept
    tokens, width = x.shape
    hidden = active.shape[1]
    operands, specs, extra = weight_sources(plan, weights, norms, hidden)
    frame = soft.shape[2]
    tile = SPATIAL_TILE
    count = tokens // tile

    def opening(*rest):
        return pl.BlockSpec(rest, lambda p, i: (i + (p + 1) // 2 * (count - 1 - i),) + (0,) * (len(rest) - 1))

    def midway(*rest):
        return pl.BlockSpec(rest, lambda p, i: (p * (2 - p) * i + p // 2 * (count - 1),) + (0,) * (len(rest) - 1))

    def closing(*rest):
        return pl.BlockSpec(rest, lambda p, i: (p // 2 * i,) + (0,) * (len(rest) - 1))

    anywhere = pl.BlockSpec(memory_space=pl.ANY)
    norm_sums = (4, 8, width)
    out_specs, out_shape = [closing(tile, width)], [jax.ShapeDtypeStruct((tokens, width), f32)]
    scratch = [
        pltpu.VMEM((HEADS // 2, frame, 2 * frame), f32),
        pltpu.VMEM((HEADS // 2, frame, 2 * frame), bf16),
        pltpu.VMEM((tile, width), bf16),
        pltpu.VMEM((tokens, width), f32),
        pltpu.VMEM((tokens, width), bf16),
        pltpu.VMEM((tokens, hidden), bf16),
        pltpu.VMEM((tokens, width), bf16),
        pltpu.VMEM((tokens, width), bf16),
        pltpu.VMEM((2, tokens, width), bf16),
        pltpu.SemaphoreType.DMA((2,)),
    ]
    params = dict(vmem_limit_bytes=63 * MIB)
    if plan is None:
        grad_specs, grad_shapes = grad_outputs(plan, width, hidden)
        out_specs += grad_specs + [whole(norm_sums)]
        out_shape += grad_shapes + [jax.ShapeDtypeStruct(norm_sums, f32)]
    else:
        rows = SHARD - ROW_TILE
        for shape in ((2 * rows, LANES), (8, LANES)):
            out_specs.append(whole(shape))
            out_shape.append(jax.ShapeDtypeStruct(shape, f32))
        scratch += [pltpu.VMEM(norm_sums, f32)] + extra + SCATTER_ROOM
        scratch += [
            pltpu.VMEM((SHARD, LANES), f32),
            pltpu.VMEM((SHARD, LANES), f32),
            pltpu.VMEM((4, 2, 2, 2, SHARD, LANES), bf16),
            pltpu.VMEM((2, 2, 2, SHARD, LANES), bf16),
            pltpu.SemaphoreType.DMA((2,)),
            pltpu.SemaphoreType.DMA((2, 6, 4)),
            pltpu.SemaphoreType.DMA((2, 6, 4)),
            pltpu.SemaphoreType.REGULAR((3, 4)),
        ]
        scratch += SMALL_ROOM
        scratch += [
            pltpu.VMEM((SHARD, LANES), bf16),
            pltpu.SemaphoreType.DMA((1,)),
            pltpu.SemaphoreType.DMA((1,)),
        ]
        operands, specs = operands + [own_next], specs + [anywhere]
        params |= dict(collective_id=1, has_side_effects=True)
    return pl.pallas_call(
        partial(spatial_backward_kernel, plan),
        grid=(3, count),
        in_specs=[
            pl.BlockSpec((tile, width), lambda p, i: ((p + 1) // 2 * i, 0)),
            opening(tile, width),
            midway(tile, 3 * width),
            midway(tile // frame, HEADS // 2, frame, 2 * frame),
            opening(tile, width),
            opening(tile, hidden),
            anywhere,
            anywhere,
        ]
        + specs,
        out_specs=out_specs,
        out_shape=out_shape,
        scratch_shapes=scratch,
        compiler_params=pltpu.CompilerParams(**params),
    )(x, grad, packed, soft, middle, slope, mixture, active, *operands)


def unpack(flat_weights, model_width, hidden_width):
    cut_qkv = 3 * model_width * model_width
    cut_out = 4 * model_width * model_width
    cut_up = cut_out + model_width * hidden_width
    return (
        flat_weights[:cut_qkv].reshape(model_width, 3 * model_width),
        flat_weights[cut_qkv:cut_out].reshape(model_width, model_width),
        flat_weights[cut_out:cut_up].reshape(model_width, hidden_width),
        flat_weights[cut_up:].reshape(hidden_width, model_width),
    )


def adamw(param_value, moment, second, grad_total, step_value, rate, decay_rate):
    moment_next = beta_first * moment + (1.0 - beta_first) * grad_total
    second_next = beta_second * second + (1.0 - beta_second) * grad_total * grad_total
    moment_hat = moment_next / (1.0 - beta_first**step_value)
    second_hat = second_next / (1.0 - beta_second**step_value)
    param_next = param_value - rate * (
        moment_hat / (jnp.sqrt(second_hat) + adam_floor) + decay_rate * param_value
    )
    return (param_next, moment_next, second_next)


def interleave(pair):
    return pair.reshape(2, -1, LANES).swapaxes(0, 1).reshape(-1, LANES)


def separate(rows):
    return rows.reshape(-1, 2, LANES).swapaxes(0, 1).reshape(2, -1)


def on_device(
    clip_tokens,
    cotangent,
    lengths,
    params,
    param_moment,
    param_second,
    norm_par,
    norm_moment,
    norm_second,
):
    clip_count, step_slots, patch_count, model_width = clip_tokens.shape
    shards = lax.axis_size("dp")
    plan = shard_plan(shards, model_width, FF) if shards == 32 else None
    x = clip_tokens.reshape(-1, model_width)
    if plan is None:
        gathered = lax.all_gather(params.astype(bf16), "dp", axis=1, tiled=True)
        norm_whole = lax.all_gather(norm_par.astype(bf16), "dp", axis=0, tiled=True)
        norm_table = norm_whole.astype(f32).reshape(2, 4, model_width)
        spatial_weights = unpack(gathered[0], model_width, FF)
        temporal_weights = unpack(gathered[1], model_width, FF)
        sources = (*spatial_weights, norm_table[0])
        *kept, after = spatial_forward(plan, x, sources, patch_count, FF)
    else:
        sources = (interleave(params), norm_par.reshape(1, LANES))
        *kept, after, spatial_weights, temporal_weights, norm_table = spatial_forward(
            plan, x, sources, patch_count, FF
        )
    result, grad_after, *temporal_grads, temporal_norm = temporal_block(
        plan,
        lengths,
        after.reshape(step_slots, patch_count, model_width),
        cotangent.reshape(step_slots, patch_count, model_width),
        temporal_weights,
        norm_table[1] if plan is None else norm_table,
        FF,
    )
    grad_before, *spatial_grads, spatial_norm = spatial_backward(
        plan, x, grad_after.reshape(-1, model_width), kept, spatial_weights, norm_table[0] if plan is None else norm_table,
        temporal_grads[0],
    )
    if plan is None:

        def scatter(grads):
            flat = jnp.concatenate([g.reshape(-1) for g in grads])
            return lax.psum_scatter(flat, "dp", scatter_dimension=0, tiled=True).astype(f32)

        weight_sum = jnp.stack([scatter(spatial_grads), scatter(temporal_grads)])
        norm_grad = jnp.stack([spatial_norm, temporal_norm]).sum(axis=2).reshape(-1)
        norm_sum = lax.psum_scatter(norm_grad, "dp", scatter_dimension=0, tiled=True)
    else:
        weight_sum = spatial_grads[0]
        norm_sum = spatial_norm[0] + spatial_norm[1]
    step_value = float(STEP)
    state = (params, param_moment, param_second)
    if plan is None:
        updated = adamw(*state, weight_sum, step_value, learn_rate, weight_decay)
        new_copy = updated[0].astype(bf16)
    else:
        state = lax.optimization_barrier([interleave(part) for part in state])
        updated = adamw(*state, weight_sum, step_value, learn_rate, weight_decay)
        new_copy = separate(updated[0].astype(bf16))
        updated = [separate(part) for part in updated]
    new_params, new_moment, new_second = updated
    new_norm, new_norm_moment, new_norm_second = adamw(
        norm_par, norm_moment, norm_second, norm_sum, step_value, norm_rate, 0.0
    )
    return (
        result.reshape(clip_tokens.shape),
        grad_before.reshape(clip_tokens.shape),
        new_params,
        new_moment,
        new_second,
        new_copy,
        new_norm,
        new_norm_moment,
        new_norm_second,
    )


def solution(mesh):
    placed = (
        P("dp", None, None, None),
        P("dp", None, None, None),
        P("dp"),
        P(None, "dp"),
        P(None, "dp"),
        P(None, "dp"),
        P("dp"),
        P("dp"),
        P("dp"),
    )
    return jax.shard_map(
        on_device,
        mesh=mesh,
        in_specs=placed,
        out_specs=(
            P("dp", None, None, None),
            P("dp", None, None, None),
            P(None, "dp"),
            P(None, "dp"),
            P(None, "dp"),
            P(None, "dp"),
            P("dp"),
            P("dp"),
            P("dp"),
        ),
        check_vma=False,
    )
```
